32 devices in a mesh: section: 4 (over y, x), seq: 8 (over z, core).
Axes of the slice: x: 2, y: 2, z: 4, core: 2. Of those that a mesh axis runs over, the one named last changes fastest.
Arguments:
- latents: bfloat16 [2, 320, 1536], P(None, 'seq'), may hold values from -6 to 6
- lengths: int32 [2], replicated, may hold values from 1 to 320, as said below
- segment_layers: int32 [4], P('section'), may hold values from 1 to 2, as said below
- norm_gain: bfloat16 [8, 1536], P('section'), may hold values from 0.3984375 to 1.59375
- qkv_weight: bfloat16 [8, 1536, 2304], P('section'), may hold values from -0.15625 to 0.15625
- qk_gain: bfloat16 [8, 128], P('section'), may hold values from 0.25 to 1.75
- out_weight: bfloat16 [8, 768, 1536], P('section'), may hold values from -0.21875 to 0.21875
Outputs:
- denoised: bfloat16 [2, 320, 1536], P(None, 'seq', 'section')
The draws below stay inside these ranges and needn't reach their ends.
Inputs may be any that keep to these rules, and one draw needn't show every extreme that they name: `lengths`: one micro-batch in every draw has all 320 tokens live. `segment_layers`: some section runs all 2 slots and some section runs one.
All inputs are finite; a program needn't handle non-finite values.
Results may differ from the reference program's by a relative error of at most 0.023.
Values may be sent and summed in bfloat16 or wider, within the bound.
No kernel may reach another device: no remote copies, remote signals or barrier semaphores. Data moves between devices by JAX's collectives and lax.ppermute only.
A program may use at most 128 MiB of HBM per device.

```python
import jax
import jax.numpy as jnp
from jax import lax

D = 1536
HDIM = 64
SLOTS = 2
MICRO = 2
HD = 768
SEQ = 320
LAYERS = 8
N_SECTION = 4


def draw_lengths(key, part):
    key_len = jax.random.fold_in(key, 11)
    key_pick = jax.random.fold_in(key, 12)
    drawn = jax.random.randint(key_len, (MICRO,), 1, SEQ + 1)
    picked = jax.random.randint(key_pick, (), 0, MICRO)
    return jnp.where(jnp.arange(MICRO) == picked, SEQ, drawn).astype(jnp.int32)


def draw_segment_layers(key, part):
    key_count = jax.random.fold_in(key, 21)
    key_pick = jax.random.fold_in(key, 22)
    drawn = jax.random.randint(key_count, (N_SECTION,), 1, SLOTS + 1)
    picked = jax.random.randint(key_pick, (), 0, N_SECTION)
    positions = jnp.arange(N_SECTION)
    drawn = jnp.where(positions == picked, SLOTS, drawn)
    drawn = jnp.where(positions == (picked + 1) % N_SECTION, 1, drawn)
    return drawn.astype(jnp.int32)


def block_scale(own_key, shape, shards, low, top_value):
    level = 1.0
    for dim, blocks in shards:
        draws = jax.random.uniform(jax.random.fold_in(jax.random.fold_in(own_key, 6), dim), (blocks,), jnp.float32, low / len(shards), top_value / len(shards))
        level = level * jnp.repeat(jnp.exp(draws), shape[dim] // blocks).reshape((-1,) + (1,) * (len(shape) - 1 - dim))
    return level


def normal_values(stream_key, extent, deviation, bound, pieces=(), kind=jnp.bfloat16):
    array = deviation * jax.random.normal(stream_key, extent, jnp.float32)
    if pieces:
        array = array * block_scale(stream_key, extent, pieces, -0.22, 0.18)
    return jnp.clip(array, -bound, bound).astype(kind)


def setup_inputs(seed: int = 0) -> dict:
    arg_keys = jax.random.split(jax.random.key(seed), 8)
    latents = normal_values(arg_keys[0], (MICRO, SEQ, D), 1.0, 6.0, ((1, 8),))
    lengths = draw_lengths(jax.random.fold_in(arg_keys[7], 71), 0)
    segment_layers = draw_segment_layers(jax.random.fold_in(arg_keys[7], 71), 0)
    norm_gain = jnp.clip(1.0 + 0.12 * jax.random.normal(arg_keys[3], (LAYERS, D), jnp.float32), 0.3984375, 1.59375).astype(jnp.bfloat16)
    qkv_weight = normal_values(arg_keys[4], (LAYERS, D, 3 * HD), D ** -0.5, 0.15625, ((0, 4),))
    qk_gain = jnp.clip(1.0 + 0.15 * jax.random.normal(arg_keys[5], (LAYERS, 2 * HDIM), jnp.float32), 0.25, 1.75).astype(jnp.bfloat16)
    out_weight = normal_values(arg_keys[6], (LAYERS, HD, D), HD ** -0.5, 0.21875, ((0, 4),))
    return dict(latents=latents, lengths=lengths, segment_layers=segment_layers, norm_gain=norm_gain, qkv_weight=qkv_weight, qk_gain=qk_gain, out_weight=out_weight)


eps_norm = 1e-06
neg_large = -1e+30

def rms_scale(values, gain_vec):
    return values * lax.rsqrt(lax.optimization_barrier(jnp.mean(values * values, axis=-1, keepdims=True)) + eps_norm) * gain_vec

def rounded(values):
    return lax.optimization_barrier(values.astype(jnp.bfloat16)).astype(jnp.float32)

def attention_layer(current, length, norm_w, qkv_w, qk_w, out_w):
    seq_rows, width = current.shape
    inner = qkv_w.shape[1] // 3
    head_dim = qk_w.shape[0] // 2
    head_count = inner // head_dim
    resid = current.astype(jnp.float32)
    normed = rms_scale(resid, norm_w.astype(jnp.float32)).astype(jnp.bfloat16)
    projected = jnp.dot(normed, qkv_w, preferred_element_type=jnp.float32)
    queries = rounded(rms_scale(projected[:, :inner].reshape(seq_rows, head_count, head_dim), qk_w[:head_dim].astype(jnp.float32)))
    keys = rounded(rms_scale(projected[:, inner:2 * inner].reshape(seq_rows, head_count, head_dim), qk_w[head_dim:].astype(jnp.float32)))
    values = rounded(projected[:, 2 * inner:].reshape(seq_rows, head_count, head_dim))
    scores = jnp.einsum('qhd,khd->hqk', queries, keys) * head_dim ** (-0.5)
    key_mask = jnp.arange(seq_rows, dtype=jnp.int32) < length
    scores = jnp.where(key_mask[None, None, :], scores, neg_large)
    top_score = lax.optimization_barrier(jnp.max(scores, axis=-1, keepdims=True))
    weights = jnp.exp(scores - top_score)
    totals = lax.optimization_barrier(jnp.sum(weights, axis=-1))
    mixed = jnp.einsum('hqk,khd->hqd', rounded(weights), values)
    attended = rounded(mixed / totals[..., None])
    update = jnp.einsum('hqd,hde->qe', attended, out_w.reshape(head_count, head_dim, width).astype(jnp.float32))
    return (resid + update).astype(jnp.bfloat16)

def reference(latents, lengths, segment_layers, norm_gain, qkv_weight, qk_gain, out_weight):
    layer_ids = jnp.arange(qkv_weight.shape[0], dtype=jnp.int32)
    active = layer_ids % SLOTS < segment_layers[layer_ids // SLOTS]

    def run_micro(inputs):
        sample, length = inputs

        def step_layer(current, layer_in):
            flag, norm_w, qkv_w, qk_w, out_w = layer_in
            updated = attention_layer(current, length, norm_w, qkv_w, qk_w, out_w)
            return (jnp.where(flag, updated, current), None)
        final_x, unused = lax.scan(step_layer, sample, (active, norm_gain, qkv_weight, qk_gain, out_weight))
        return final_x
    return lax.map(run_micro, (latents, lengths))
```

```python
import functools

import jax
import jax.numpy as jnp
from jax import lax
from jax.experimental import pallas as pl
from jax.experimental.pallas import tpu as pltpu
from jax.sharding import PartitionSpec as P

eps_norm = 1e-06
neg_large = -1e30
F32, BF16 = jnp.float32, jnp.bfloat16
TILE = 256


def shifted(value, axis, steps):
    count = lax.axis_size(axis)
    leading, last = (max(0, -steps), min(count, count - steps))
    return lax.ppermute(value, axis, [(source, source + steps) for source in range(leading, last)])


def rms_scale(values, gain_vec):
    return (
        values * lax.rsqrt(jnp.mean(values * values, axis=-1, keepdims=True) + eps_norm) * gain_vec
    )


def body_layer(current, length, norm_w, qkv_w, qk_w, out_w):
    tok_rows, width = current.shape
    inner = qkv_w.shape[1] // 3
    head_dim = qk_w.shape[0] // 2
    head_count = inner // head_dim
    resid = current.astype(jnp.float32)
    normed = rms_scale(resid, norm_w.astype(jnp.float32)).astype(jnp.bfloat16)
    projected = jnp.dot(normed, qkv_w, preferred_element_type=jnp.float32)
    queries = rms_scale(
        projected[:, :inner].reshape(tok_rows, head_count, head_dim),
        qk_w[:head_dim].astype(jnp.float32),
    ).astype(jnp.bfloat16)
    keys = (
        rms_scale(
            projected[:, inner : 2 * inner].reshape(tok_rows, head_count, head_dim),
            qk_w[head_dim:].astype(jnp.float32),
        )
        .astype(jnp.bfloat16)
        .reshape(tok_rows, inner)
    )
    values = projected[:, 2 * inner :].astype(jnp.bfloat16)
    score_scale = head_dim ** (-0.5)
    run_max = jnp.full((head_count, tok_rows), neg_large, jnp.float32)
    key_block = lax.all_gather(keys, "seq", axis=0, tiled=True)
    value_block = lax.all_gather(values, "seq", axis=0, tiled=True)
    block_rows = key_block.shape[0]
    key_heads = key_block.reshape(block_rows, head_count, head_dim)
    value_heads = value_block.reshape(block_rows, head_count, head_dim)
    scores = (
        jnp.einsum("qhd,khd->hqk", queries, key_heads, preferred_element_type=jnp.float32)
        * score_scale
    )
    positions = jnp.arange(block_rows, dtype=jnp.int32)
    scores = jnp.where((positions < length)[None, None, :], scores, neg_large)
    new_max = jnp.maximum(run_max, jnp.max(scores, axis=-1))
    weights = jnp.exp(scores - new_max[..., None])
    run_total = jnp.sum(weights, axis=-1)
    run_acc = jnp.einsum(
        "hqk,khd->hqd",
        weights.astype(jnp.bfloat16),
        value_heads,
        preferred_element_type=jnp.float32,
    )
    run_max, run_total, run_acc = (new_max, run_total, run_acc)
    attended = (run_acc / run_total[..., None]).astype(jnp.bfloat16)
    update = jnp.einsum(
        "hqd,hde->qe",
        attended,
        out_w.reshape(head_count, head_dim, width),
        preferred_element_type=jnp.float32,
    )
    return (resid + update).astype(jnp.bfloat16)


def relay_local(latents, lengths, segment_layers, norm_gain, qkv_weight, qk_gain, out_weight):
    segment_count = lax.axis_size("section")
    segment_pos = lax.axis_index("section")
    micro_count, tok_rows, width = latents.shape
    slot_count = qkv_weight.shape[0]
    own_layers = segment_layers[0]
    tick_count = micro_count + segment_count - 1

    def slot_layer(slot_index, current, length):
        return body_layer(
            current,
            length,
            lax.dynamic_index_in_dim(norm_gain, slot_index, 0, False),
            lax.dynamic_index_in_dim(qkv_weight, slot_index, 0, False),
            lax.dynamic_index_in_dim(qk_gain, slot_index, 0, False),
            lax.dynamic_index_in_dim(out_weight, slot_index, 0, False),
        )

    def advance(tick_index, loop_state):
        received, finished = loop_state
        micro_index = tick_index - segment_pos
        is_valid = (micro_index >= 0) & (micro_index < micro_count)
        clipped = jnp.clip(micro_index, 0, micro_count - 1)
        entering = lax.dynamic_index_in_dim(latents, clipped, 0, False)
        current = jnp.where(segment_pos == 0, entering, received)
        length = lax.dynamic_index_in_dim(lengths, clipped, 0, False)
        for slot_index in range(slot_count):
            updated = slot_layer(slot_index, current, length)
            current = jnp.where(slot_index < own_layers, updated, current)
        previous = lax.dynamic_index_in_dim(finished, clipped, 0, True)
        keep_it = is_valid & (segment_pos == segment_count - 1)
        finished = lax.dynamic_update_index_in_dim(
            finished, jnp.where(keep_it, current[None], previous), clipped, 0
        )
        received = shifted(current, "section", 1)
        return (received, finished)

    start_state = (
        jnp.zeros((tok_rows, width), jnp.bfloat16),
        jnp.zeros((micro_count, tok_rows, width), jnp.bfloat16),
    )
    final_state = lax.fori_loop(0, tick_count, advance, start_state)
    finished = final_state[1]
    terms = jnp.where(segment_pos == segment_count - 1, finished.astype(jnp.float32), 0.0)
    return lax.psum_scatter(terms.astype(jnp.bfloat16), "section", scatter_dimension=2, tiled=True)


def norm_rows(dst, src, row, count, gain):
    values = src[pl.ds(row, count), :].astype(F32)
    mean = jnp.mean(values * values, axis=-1, keepdims=True)
    dst[pl.ds(row, count), :] = (values * lax.rsqrt(mean + eps_norm) * gain).astype(BF16)


def head_norm(acc, gain, head_ones):
    mean = jnp.dot((acc * acc).astype(BF16), head_ones[...], preferred_element_type=F32)
    return (acc * lax.rsqrt(mean + eps_norm) * gain).astype(BF16)


def spread_heads(dst, tile, block, head_dim):
    rows = block.shape[0]
    lane = lax.broadcasted_iota(jnp.int32, (1, TILE), 1) // head_dim
    for h in range(TILE // head_dim):
        dst[tile, h * rows : (h + 1) * rows, :] = jnp.where(lane == h, block, jnp.zeros_like(block))


def head_totals(weights, rows, head_dim):
    half = lax.broadcasted_iota(jnp.int32, (1, 128), 1) < 64
    totals = []
    for h in range(TILE // head_dim):
        low, high = h * rows, (h + 1) * rows
        total = None
        for at in range(low // 128 * 128, high, 128):
            piece = weights[:, at : at + 128]
            if at < low:
                piece = jnp.where(half, 0.0, piece)
            elif at + 128 > high:
                piece = jnp.where(half, piece, 0.0)
            total = piece if total is None else total + piece
        totals.append(1.0 / jnp.sum(total, axis=-1, keepdims=True))
    return totals


def sublayer(q_rows, q_start, head_dim, slot, refs, residual, store):
    xn, q_s, k_s, v_s, att, gains, bias, head_ones, qkv_w, out_w = refs
    rows = xn.shape[0]
    inner, width = out_w.shape[1:]
    tiles = inner // TILE
    q_gain, k_gain = gains[slot, 0:1, :], gains[slot, 1:2, :]
    log2e = 1.4426950408889634
    top = 1.01 * head_dim**0.5 * log2e * jnp.max(jnp.abs(q_gain)) * jnp.max(jnp.abs(k_gain))
    key_bias = bias[...] - top
    score_scale = head_dim ** (-0.5) * log2e
    for t in range(tiles):
        at = inner + t * TILE
        acc = jnp.dot(xn[...], qkv_w[slot, :, at : at + TILE], preferred_element_type=F32)
        spread_heads(k_s, t, head_norm(acc, k_gain, head_ones), head_dim)
    for t in range(tiles):
        at = 2 * inner + t * TILE
        acc = jnp.dot(xn[...], qkv_w[slot, :, at : at + TILE], preferred_element_type=F32)
        spread_heads(v_s, t, acc.astype(BF16), head_dim)
    for t in range(tiles):
        at = t * TILE
        acc = jnp.dot(xn[pl.ds(q_start, q_rows), :], qkv_w[slot, :, at : at + TILE], preferred_element_type=F32)
        q_s[0:q_rows, at : at + TILE] = head_norm(acc, q_gain, head_ones)
    step = min(q_rows, 160)
    half = lax.broadcasted_iota(jnp.int32, (1, 128), 1) < 64
    for t in range(tiles):
        for r in range(0, q_rows, step):
            queries = q_s[r : r + step, t * TILE : (t + 1) * TILE]
            scores = lax.dot_general(queries, k_s[t], (((1,), (1,)), ((), ())), preferred_element_type=F32)
            weights = jnp.exp2(scores * score_scale + key_bias)
            inverse = head_totals(weights, rows, head_dim)
            mixed = jnp.dot(weights.astype(BF16), v_s[t], preferred_element_type=F32)
            for g in range(2):
                scale = jnp.where(half, inverse[2 * g], inverse[2 * g + 1])
                at = t * TILE + g * 128
                att[r : r + step, at : at + 128] = (mixed[:, g * 128 : (g + 1) * 128] * scale).astype(BF16)
    for at in range(0, width, TILE):
        acc = jnp.dot(att[0:q_rows, :], out_w[slot, :, at : at + TILE], preferred_element_type=F32)
        store(at, (residual(at) + acc).astype(BF16))


def stage_kernel(head_dim, info, own, other, norm_g, gains, bias, head_ones, qkv_w, out_w, out, x_s, xn, q_s, k_s, v_s, att):
    half_rows = own.shape[0]
    rows, out_rows = 2 * half_rows, out.shape[0]
    refs = (xn, q_s, k_s, v_s, att, gains, bias, head_ones, qkv_w, out_w)

    def norm_all(slot):
        gain = norm_g[slot]

        def one(step, carry):
            norm_rows(xn, x_s, pl.multiple_of(step * 16, 16), 16, gain)
            return carry

        lax.fori_loop(0, rows // 16, one, 0, unroll=10)

    @pl.when(info[0] != 0)
    def run():
        count = info[1]
        start = pl.multiple_of(info[2], 16)
        x_s[0:half_rows, :] = own[...]
        x_s[half_rows:rows, :] = other[...]
        norm_all(0)

        @pl.when(count > 1)
        def first():
            def store(at, block):
                x_s[:, at : at + TILE] = block

            sublayer(rows, 0, head_dim, 0, refs, lambda at: x_s[:, at : at + TILE].astype(F32), store)
            norm_all(1)

        def store(at, block):
            out[:, at : at + TILE] = block

        def residual(at):
            return x_s[pl.ds(start, out_rows), at : at + TILE].astype(F32)

        sublayer(out_rows, start, head_dim, count - 1, refs, residual, store)


def run_stage(info, own, other, norm_g, gains, bias, head_ones, qkv_w, out_w, head_dim, out_rows):
    half_rows, width = own.shape
    rows = 2 * half_rows
    inner = out_w.shape[1]
    tiles, per_tile = inner // TILE, TILE // head_dim
    whole = pl.BlockSpec(memory_space=pltpu.VMEM)
    return pl.pallas_call(
        functools.partial(stage_kernel, head_dim),
        out_shape=jax.ShapeDtypeStruct((out_rows, width), BF16),
        in_specs=[pl.BlockSpec(memory_space=pltpu.SMEM)] + [whole] * 8,
        out_specs=whole,
        scratch_shapes=[
            pltpu.VMEM((rows, width), BF16),
            pltpu.VMEM((rows, width), BF16),
            pltpu.VMEM((rows, inner), BF16),
            pltpu.VMEM((tiles, per_tile * rows, TILE), BF16),
            pltpu.VMEM((tiles, per_tile * rows, TILE), BF16),
            pltpu.VMEM((rows, inner), BF16),
        ],
        compiler_params=pltpu.CompilerParams(vmem_limit_bytes=16 * 2**20),
        name="stage",
    )(info, own, other, norm_g, gains, bias, head_ones, qkv_w, out_w)


def sent(value, seq_count, pairs):
    flat = [(a * seq_count + b, c * seq_count + d) for (a, b), (c, d) in pairs]
    return lax.ppermute(value, ("section", "seq"), flat)


def pair_local(latents, lengths, segment_layers, norm_gain, qkv_weight, qk_gain, out_weight):
    sections = lax.axis_size("section")
    seq_count = lax.axis_size("seq")
    chips = seq_count // 2
    micro_count, tok_rows, width = latents.shape
    slots = qkv_weight.shape[0]
    head_dim = qk_gain.shape[1] // 2
    per_tile = TILE // head_dim
    section = lax.axis_index("section")
    seq = lax.axis_index("seq")
    chip, core = seq // 2, seq % 2
    micro = chip // 2
    seqs = range(seq_count)

    gains = jnp.tile(qk_gain.reshape(slots, 2, head_dim).astype(F32), (1, 1, per_tile))
    norm_g = norm_gain.astype(F32)[:, None, :]
    heads = jnp.arange(TILE) // head_dim
    head_ones = jnp.where(heads[:, None] == heads[None, :], 1.0 / head_dim, 0.0).astype(BF16)
    piece = jnp.arange(chips)[None, :, None] ^ chip
    cores = jnp.arange(2)[:, None, None] ^ core
    position = (tok_rows * (2 * piece + cores) + jnp.arange(tok_rows)[None, None, :]).reshape(1, -1)
    length = lax.dynamic_index_in_dim(lengths, micro, 0, False)
    bias = jnp.tile(jnp.where(position < length, 0.0, neg_large).astype(F32), (1, per_tile))
    own_layers = segment_layers[0]

    pieces = [lax.dynamic_index_in_dim(latents, micro, 0, False)]
    away = lax.dynamic_index_in_dim(latents, 1 - micro, 0, False)
    for k in range(1, chips):
        pairs = [((0, s), (0, s ^ (2 * k))) for s in seqs]
        pieces.append(sent(pieces[0] if k < 2 else away, seq_count, pairs))
    own = jnp.concatenate(pieces, axis=0)

    for stage in range(sections):
        other = sent(own, seq_count, [((stage, s), (stage, s ^ 1)) for s in seqs])
        last = stage == sections - 1
        out_rows = 2 * tok_rows if last else chips * tok_rows
        start = jnp.where((chip == 1) | (chip == 2), out_rows, 0) if last else 0
        info = jnp.stack([(section == stage).astype(jnp.int32), own_layers, jnp.int32(start), jnp.int32(0)])
        own = run_stage(info, own, other, norm_g, gains, bias, head_ones, qkv_weight, out_weight, head_dim, out_rows)
        if not last:
            own = sent(own, seq_count, [((stage, s), (stage + 1, s)) for s in seqs])

    final = sections - 1
    swap = micro == 1
    front, back = own[:tok_rows], own[tok_rows:]
    ways = ((jnp.where(swap, back, front), (0, 3, 1, 2)), (jnp.where(swap, front, back), (1, 2, 0, 3)))
    got = []
    for block, targets in ways:
        cols = width // sections
        mine = None
        for t in range(sections):
            pairs = [((final, s), (t, 2 * targets[s // 2] + s % 2)) for s in seqs]
            here = sent(block[:, t * cols : (t + 1) * cols], seq_count, pairs)
            mine = here if mine is None else jnp.where(section == t, here, mine)
        got.append(mine)
    first = (chip == 0) | (chip == 3)
    return jnp.stack([jnp.where(first, got[0], got[1]), jnp.where(first, got[1], got[0])])


def local(latents, lengths, segment_layers, norm_gain, qkv_weight, qk_gain, out_weight):
    args = (latents, lengths, segment_layers, norm_gain, qkv_weight, qk_gain, out_weight)
    pairwise = lax.axis_size("seq") == 8 and latents.shape[0] == 2
    return pair_local(*args) if pairwise else relay_local(*args)


def solution(mesh):
    return jax.shard_map(
        local,
        mesh=mesh,
        in_specs=(
            P(None, "seq", None),
            P(),
            P("section"),
            P("section", None),
            P("section", None, None),
            P("section", None),
            P("section", None, None),
        ),
        out_specs=P(None, "seq", "section"),
        check_vma=False,
    )
```

```python
import functools

import jax
import jax.numpy as jnp
from jax import lax
from jax.experimental import pallas as pl
from jax.experimental.pallas import tpu as pltpu
from jax.sharding import PartitionSpec as P

eps_norm = 1e-06
neg_large = -1e30
F32, BF16 = jnp.float32, jnp.bfloat16
TILE = 256


def shifted(value, axis, steps):
    count = lax.axis_size(axis)
    leading, last = (max(0, -steps), min(count, count - steps))
    return lax.ppermute(value, axis, [(source, source + steps) for source in range(leading, last)])


def rms_scale(values, gain_vec):
    return (
        values * lax.rsqrt(jnp.mean(values * values, axis=-1, keepdims=True) + eps_norm) * gain_vec
    )


def body_layer(current, length, norm_w, qkv_w, qk_w, out_w):
    tok_rows, width = current.shape
    inner = qkv_w.shape[1] // 3
    head_dim = qk_w.shape[0] // 2
    head_count = inner // head_dim
    resid = current.astype(jnp.float32)
    normed = rms_scale(resid, norm_w.astype(jnp.float32)).astype(jnp.bfloat16)
    projected = jnp.dot(normed, qkv_w, preferred_element_type=jnp.float32)
    queries = rms_scale(
        projected[:, :inner].reshape(tok_rows, head_count, head_dim),
        qk_w[:head_dim].astype(jnp.float32),
    ).astype(jnp.bfloat16)
    keys = (
        rms_scale(
            projected[:, inner : 2 * inner].reshape(tok_rows, head_count, head_dim),
            qk_w[head_dim:].astype(jnp.float32),
        )
        .astype(jnp.bfloat16)
        .reshape(tok_rows, inner)
    )
    values = projected[:, 2 * inner :].astype(jnp.bfloat16)
    score_scale = head_dim ** (-0.5)
    run_max = jnp.full((head_count, tok_rows), neg_large, jnp.float32)
    key_block = lax.all_gather(keys, "seq", axis=0, tiled=True)
    value_block = lax.all_gather(values, "seq", axis=0, tiled=True)
    block_rows = key_block.shape[0]
    key_heads = key_block.reshape(block_rows, head_count, head_dim)
    value_heads = value_block.reshape(block_rows, head_count, head_dim)
    scores = (
        jnp.einsum("qhd,khd->hqk", queries, key_heads, preferred_element_type=jnp.float32)
        * score_scale
    )
    positions = jnp.arange(block_rows, dtype=jnp.int32)
    scores = jnp.where((positions < length)[None, None, :], scores, neg_large)
    new_max = jnp.maximum(run_max, jnp.max(scores, axis=-1))
    weights = jnp.exp(scores - new_max[..., None])
    run_total = jnp.sum(weights, axis=-1)
    run_acc = jnp.einsum(
        "hqk,khd->hqd",
        weights.astype(jnp.bfloat16),
        value_heads,
        preferred_element_type=jnp.float32,
    )
    run_max, run_total, run_acc = (new_max, run_total, run_acc)
    attended = (run_acc / run_total[..., None]).astype(jnp.bfloat16)
    update = jnp.einsum(
        "hqd,hde->qe",
        attended,
        out_w.reshape(head_count, head_dim, width),
        preferred_element_type=jnp.float32,
    )
    return (resid + update).astype(jnp.bfloat16)


def relay_local(latents, lengths, segment_layers, norm_gain, qkv_weight, qk_gain, out_weight):
    segment_count = lax.axis_size("section")
    segment_pos = lax.axis_index("section")
    micro_count, tok_rows, width = latents.shape
    slot_count = qkv_weight.shape[0]
    own_layers = segment_layers[0]
    tick_count = micro_count + segment_count - 1

    def slot_layer(slot_index, current, length):
        return body_layer(
            current,
            length,
            lax.dynamic_index_in_dim(norm_gain, slot_index, 0, False),
            lax.dynamic_index_in_dim(qkv_weight, slot_index, 0, False),
            lax.dynamic_index_in_dim(qk_gain, slot_index, 0, False),
            lax.dynamic_index_in_dim(out_weight, slot_index, 0, False),
        )

    def advance(tick_index, loop_state):
        received, finished = loop_state
        micro_index = tick_index - segment_pos
        is_valid = (micro_index >= 0) & (micro_index < micro_count)
        clipped = jnp.clip(micro_index, 0, micro_count - 1)
        entering = lax.dynamic_index_in_dim(latents, clipped, 0, False)
        current = jnp.where(segment_pos == 0, entering, received)
        length = lax.dynamic_index_in_dim(lengths, clipped, 0, False)
        for slot_index in range(slot_count):
            updated = slot_layer(slot_index, current, length)
            current = jnp.where(slot_index < own_layers, updated, current)
        previous = lax.dynamic_index_in_dim(finished, clipped, 0, True)
        keep_it = is_valid & (segment_pos == segment_count - 1)
        finished = lax.dynamic_update_index_in_dim(
            finished, jnp.where(keep_it, current[None], previous), clipped, 0
        )
        received = shifted(current, "section", 1)
        return (received, finished)

    start_state = (
        jnp.zeros((tok_rows, width), jnp.bfloat16),
        jnp.zeros((micro_count, tok_rows, width), jnp.bfloat16),
    )
    final_state = lax.fori_loop(0, tick_count, advance, start_state)
    finished = final_state[1]
    terms = jnp.where(segment_pos == segment_count - 1, finished.astype(jnp.float32), 0.0)
    return lax.psum_scatter(terms.astype(jnp.bfloat16), "section", scatter_dimension=2, tiled=True)


def norm_rows(dst, src, row, count, gain):
    values = src[pl.ds(row, count), :].astype(F32)
    mean = jnp.mean(values * values, axis=-1, keepdims=True)
    dst[pl.ds(row, count), :] = (values * lax.rsqrt(mean + eps_norm) * gain).astype(BF16)


def head_norm(acc, gain, head_ones):
    mean = jnp.dot((acc * acc).astype(BF16), head_ones[...], preferred_element_type=F32)
    return (acc * lax.rsqrt(mean + eps_norm) * gain).astype(BF16)


def spread_heads(dst, tile, block, head_dim):
    rows = block.shape[0]
    lane = lax.broadcasted_iota(jnp.int32, (1, TILE), 1) // head_dim
    for h in range(TILE // head_dim):
        dst[tile, h * rows : (h + 1) * rows, :] = jnp.where(lane == h, block, jnp.zeros_like(block))


def head_totals(weights, rows, head_dim):
    half = lax.broadcasted_iota(jnp.int32, (1, 128), 1) < 64
    totals = []
    for h in range(TILE // head_dim):
        low, high = h * rows, (h + 1) * rows
        total = None
        for at in range(low // 128 * 128, high, 128):
            piece = weights[:, at : at + 128]
            if at < low:
                piece = jnp.where(half, 0.0, piece)
            elif at + 128 > high:
                piece = jnp.where(half, piece, 0.0)
            total = piece if total is None else total + piece
        totals.append(1.0 / jnp.sum(total, axis=-1, keepdims=True))
    return totals


def weight_copies(slot, qkv_hbm, out_hbm, qkv_w, out_w, sems):
    inner = out_w.shape[1]
    tiles = inner // TILE
    order = [*range(tiles, 3 * tiles), *range(tiles)]
    copies = []
    for n, tile in enumerate(order):
        cols = pl.ds(tile * TILE, TILE)
        copies.append(pltpu.make_async_copy(qkv_hbm.at[slot, :, cols], qkv_w.at[slot, :, cols], sems.at[slot, n]))
    copies.append(pltpu.make_async_copy(out_hbm.at[slot], out_w.at[slot], sems.at[slot, 3 * tiles]))
    return copies


def sublayer(q_rows, q_start, head_dim, slot, copies, refs, residual, store):
    xn, q_s, k_s, v_s, att, gains, bias, head_ones, qkv_w, out_w = refs
    rows = xn.shape[0]
    inner, width = out_w.shape[1:]
    tiles = inner // TILE
    q_gain, k_gain = gains[slot, 0:1, :], gains[slot, 1:2, :]
    log2e = 1.4426950408889634
    top = 1.01 * head_dim**0.5 * log2e * jnp.max(jnp.abs(q_gain)) * jnp.max(jnp.abs(k_gain))
    key_bias = bias[...] - top
    score_scale = head_dim ** (-0.5) * log2e
    for t in range(tiles):
        at = inner + t * TILE
        copies[t].wait()
        acc = jnp.dot(xn[...], qkv_w[slot, :, at : at + TILE], preferred_element_type=F32)
        spread_heads(k_s, t, head_norm(acc, k_gain, head_ones), head_dim)
    for t in range(tiles):
        at = 2 * inner + t * TILE
        copies[tiles + t].wait()
        acc = jnp.dot(xn[...], qkv_w[slot, :, at : at + TILE], preferred_element_type=F32)
        spread_heads(v_s, t, acc.astype(BF16), head_dim)
    for t in range(tiles):
        at = t * TILE
        copies[2 * tiles + t].wait()
        acc = jnp.dot(xn[pl.ds(q_start, q_rows), :], qkv_w[slot, :, at : at + TILE], preferred_element_type=F32)
        q_s[0:q_rows, at : at + TILE] = head_norm(acc, q_gain, head_ones)
    step = min(q_rows, 160)
    half = lax.broadcasted_iota(jnp.int32, (1, 128), 1) < 64
    for t in range(tiles):
        for r in range(0, q_rows, step):
            queries = q_s[r : r + step, t * TILE : (t + 1) * TILE]
            scores = lax.dot_general(queries, k_s[t], (((1,), (1,)), ((), ())), preferred_element_type=F32)
            weights = jnp.exp2(scores * score_scale + key_bias)
            inverse = head_totals(weights, rows, head_dim)
            mixed = jnp.dot(weights.astype(BF16), v_s[t], preferred_element_type=F32)
            for g in range(2):
                scale = jnp.where(half, inverse[2 * g], inverse[2 * g + 1])
                at = t * TILE + g * 128
                att[r : r + step, at : at + 128] = (mixed[:, g * 128 : (g + 1) * 128] * scale).astype(BF16)
    copies[3 * tiles].wait()
    for at in range(0, width, TILE):
        acc = jnp.dot(att[0:q_rows, :], out_w[slot, :, at : at + TILE], preferred_element_type=F32)
        store(at, (residual(at) + acc).astype(BF16))


def stage_kernel(head_dim, parts, info, *refs):
    blocks, refs = refs[:parts], refs[parts:]
    norm_g, gains, bias, head_ones, qkv_hbm, out_hbm, out, x_s, xn, q_s, k_s, v_s, att, qkv_w, out_w, sems = refs
    rows, out_rows = x_s.shape[0], out.shape[0]
    refs = (xn, q_s, k_s, v_s, att, gains, bias, head_ones, qkv_w, out_w)

    def norm_all(slot):
        gain = norm_g[slot]

        def one(step, carry):
            norm_rows(xn, x_s, pl.multiple_of(step * 16, 16), 16, gain)
            return carry

        lax.fori_loop(0, rows // 16, one, 0, unroll=10)

    def weights_of(slot):
        return weight_copies(slot, qkv_hbm, out_hbm, qkv_w, out_w, sems)

    @pl.when(info[0] != 0)
    def run():
        count, start, core = info[1], pl.multiple_of(info[2], 16), info[3]
        for copy in weights_of(0):
            copy.start()

        @pl.when(count > 1)
        def ahead():
            for copy in weights_of(1):
                copy.start()

        if parts == 2:
            half_rows = rows // 2
            x_s[0:half_rows, :] = blocks[0][...]
            x_s[half_rows:rows, :] = blocks[1][...]
        else:
            for n in range(parts // 2):
                own, other = blocks[n][...].astype(F32), blocks[n + parts // 2][...].astype(F32)
                first, second = jnp.where(core == 0, own, other), jnp.where(core == 0, other, own)
                both = jnp.concatenate([first, second], axis=0).astype(BF16)
                x_s[n * both.shape[0] : (n + 1) * both.shape[0], :] = both
        norm_all(0)

        @pl.when(count > 1)
        def first():
            def store(at, block):
                x_s[:, at : at + TILE] = block

            sublayer(rows, 0, head_dim, 0, weights_of(0), refs, lambda at: x_s[:, at : at + TILE].astype(F32), store)
            norm_all(1)

        def store(at, block):
            out[:, at : at + TILE] = block

        def residual(at):
            return x_s[pl.ds(start, out_rows), at : at + TILE].astype(F32)

        last = count - 1
        sublayer(out_rows, start, head_dim, last, weights_of(last), refs, residual, store)


def run_stage(info, blocks, norm_g, gains, bias, head_ones, qkv_w, out_w, head_dim, out_rows):
    rows = sum(block.shape[0] for block in blocks)
    slots, inner, width = out_w.shape
    tiles, per_tile = inner // TILE, TILE // head_dim
    whole = pl.BlockSpec(memory_space=pltpu.VMEM)
    far = pl.BlockSpec(memory_space=pltpu.HBM)
    return pl.pallas_call(
        functools.partial(stage_kernel, head_dim, len(blocks)),
        out_shape=jax.ShapeDtypeStruct((out_rows, width), BF16),
        in_specs=[pl.BlockSpec(memory_space=pltpu.SMEM)] + [whole] * (len(blocks) + 4) + [far] * 2,
        out_specs=whole,
        scratch_shapes=[
            pltpu.VMEM((rows, width), BF16),
            pltpu.VMEM((rows, width), BF16),
            pltpu.VMEM((rows, inner), BF16),
            pltpu.VMEM((tiles, per_tile * rows, TILE), BF16),
            pltpu.VMEM((tiles, per_tile * rows, TILE), BF16),
            pltpu.VMEM((rows, inner), BF16),
            pltpu.VMEM(qkv_w.shape, BF16),
            pltpu.VMEM(out_w.shape, BF16),
            pltpu.SemaphoreType.DMA((slots, 3 * tiles + 1)),
        ],
        compiler_params=pltpu.CompilerParams(vmem_limit_bytes=40 * 2**20),
        name="stage",
    )(info, *blocks, norm_g, gains, bias, head_ones, qkv_w, out_w)


def sent(value, seq_count, pairs):
    flat = [(a * seq_count + b, c * seq_count + d) for (a, b), (c, d) in pairs]
    return lax.ppermute(value, ("section", "seq"), flat)


def pair_local(latents, lengths, segment_layers, norm_gain, qkv_weight, qk_gain, out_weight):
    sections = lax.axis_size("section")
    seq_count = lax.axis_size("seq")
    chips = seq_count // 2
    micro_count, tok_rows, width = latents.shape
    slots = qkv_weight.shape[0]
    head_dim = qk_gain.shape[1] // 2
    per_tile = TILE // head_dim
    section = lax.axis_index("section")
    seq = lax.axis_index("seq")
    chip, core = seq // 2, seq % 2
    micro = chip // 2
    seqs = range(seq_count)

    gains = jnp.tile(qk_gain.reshape(slots, 2, head_dim).astype(F32), (1, 1, per_tile))
    norm_g = norm_gain.astype(F32)[:, None, :]
    heads = jnp.arange(TILE) // head_dim
    head_ones = jnp.where(heads[:, None] == heads[None, :], 1.0 / head_dim, 0.0).astype(BF16)
    def key_bias(blocks):
        position = 2 * tok_rows * (blocks[:, None] ^ chip) + jnp.arange(2 * tok_rows)[None, :]
        bias = jnp.where(position.reshape(1, -1) < length, 0.0, neg_large).astype(F32)
        return jnp.tile(bias, (1, per_tile))

    length = lax.dynamic_index_in_dim(lengths, micro, 0, False)
    first_bias = key_bias(jnp.arange(chips))
    own_bias = key_bias(jnp.arange(chips) ^ (chips // 2 * core))
    own_layers = segment_layers[0]

    pieces = [lax.dynamic_index_in_dim(latents, micro, 0, False)]
    away = lax.dynamic_index_in_dim(latents, 1 - micro, 0, False)
    for k in range(1, chips):
        pairs = [(((0, 0, 1, 2)[k], s), (0, s ^ (2 * k))) for s in seqs]
        pieces.append(sent(pieces[0] if k < 2 else away, seq_count, pairs))
    blocks = pieces + [sent(part, seq_count, [((0, s), (0, s ^ 1)) for s in seqs]) for part in pieces]

    half_rows = chips * tok_rows
    for stage in range(sections):
        last = stage == sections - 1
        out_rows = 2 * tok_rows if last else half_rows
        start = half_rows * core if stage == 0 else jnp.int32(0)
        info = jnp.stack([(section == stage).astype(jnp.int32), own_layers, start, core])
        bias = own_bias if stage else first_bias
        own = run_stage(info, blocks, norm_g, gains, bias, head_ones, qkv_weight, out_weight, head_dim, out_rows)
        if not last:
            own = sent(own, seq_count, [((stage, s), (stage + 1, s)) for s in seqs])
            blocks = [own, sent(own, seq_count, [((stage + 1, s), (stage + 1, s ^ 1)) for s in seqs])]

    final = sections - 1
    cols = width // sections
    mine = None
    for t in range(sections):
        pairs = [((final, s), (t, 2 * ((s // 2) ^ (chips // 2 * (s % 2))) + s // 2 // (chips // 2))) for s in seqs]
        here = sent(own[:, t * cols : (t + 1) * cols], seq_count, pairs)
        mine = here if mine is None else jnp.where(section == t, here, mine)
    front, back = mine[:tok_rows], mine[tok_rows:]
    pairs = [((t, s), (t, s ^ 1)) for t in range(sections) for s in seqs]
    got = sent(jnp.where(core == 0, back, front), seq_count, pairs)
    return jnp.where(core == 0, jnp.stack([front, got]), jnp.stack([got, back]))


def local(latents, lengths, segment_layers, norm_gain, qkv_weight, qk_gain, out_weight):
    args = (latents, lengths, segment_layers, norm_gain, qkv_weight, qk_gain, out_weight)
    pairwise = lax.axis_size("seq") == 8 and latents.shape[0] == 2
    return pair_local(*args) if pairwise else relay_local(*args)


def solution(mesh):
    return jax.shard_map(
        local,
        mesh=mesh,
        in_specs=(
            P(None, "seq", None),
            P(),
            P("section"),
            P("section", None),
            P("section", None, None),
            P("section", None),
            P("section", None, None),
        ),
        out_specs=P(None, "seq", "section"),
        check_vma=False,
    )
```

```python
import functools

import jax
import jax.numpy as jnp
from jax import lax
from jax.experimental import pallas as pl
from jax.experimental.pallas import tpu as pltpu
from jax.sharding import PartitionSpec as P

eps_norm = 1e-06
neg_large = -1e30
F32, BF16 = jnp.float32, jnp.bfloat16
TILE = 256


def shifted(value, axis, steps):
    count = lax.axis_size(axis)
    leading, last = (max(0, -steps), min(count, count - steps))
    return lax.ppermute(value, axis, [(source, source + steps) for source in range(leading, last)])


def rms_scale(values, gain_vec):
    return (
        values * lax.rsqrt(jnp.mean(values * values, axis=-1, keepdims=True) + eps_norm) * gain_vec
    )


def body_layer(current, length, norm_w, qkv_w, qk_w, out_w):
    tok_rows, width = current.shape
    inner = qkv_w.shape[1] // 3
    head_dim = qk_w.shape[0] // 2
    head_count = inner // head_dim
    resid = current.astype(jnp.float32)
    normed = rms_scale(resid, norm_w.astype(jnp.float32)).astype(jnp.bfloat16)
    projected = jnp.dot(normed, qkv_w, preferred_element_type=jnp.float32)
    queries = rms_scale(
        projected[:, :inner].reshape(tok_rows, head_count, head_dim),
        qk_w[:head_dim].astype(jnp.float32),
    ).astype(jnp.bfloat16)
    keys = (
        rms_scale(
            projected[:, inner : 2 * inner].reshape(tok_rows, head_count, head_dim),
            qk_w[head_dim:].astype(jnp.float32),
        )
        .astype(jnp.bfloat16)
        .reshape(tok_rows, inner)
    )
    values = projected[:, 2 * inner :].astype(jnp.bfloat16)
    score_scale = head_dim ** (-0.5)
    run_max = jnp.full((head_count, tok_rows), neg_large, jnp.float32)
    key_block = lax.all_gather(keys, "seq", axis=0, tiled=True)
    value_block = lax.all_gather(values, "seq", axis=0, tiled=True)
    block_rows = key_block.shape[0]
    key_heads = key_block.reshape(block_rows, head_count, head_dim)
    value_heads = value_block.reshape(block_rows, head_count, head_dim)
    scores = (
        jnp.einsum("qhd,khd->hqk", queries, key_heads, preferred_element_type=jnp.float32)
        * score_scale
    )
    positions = jnp.arange(block_rows, dtype=jnp.int32)
    scores = jnp.where((positions < length)[None, None, :], scores, neg_large)
    new_max = jnp.maximum(run_max, jnp.max(scores, axis=-1))
    weights = jnp.exp(scores - new_max[..., None])
    run_total = jnp.sum(weights, axis=-1)
    run_acc = jnp.einsum(
        "hqk,khd->hqd",
        weights.astype(jnp.bfloat16),
        value_heads,
        preferred_element_type=jnp.float32,
    )
    run_max, run_total, run_acc = (new_max, run_total, run_acc)
    attended = (run_acc / run_total[..., None]).astype(jnp.bfloat16)
    update = jnp.einsum(
        "hqd,hde->qe",
        attended,
        out_w.reshape(head_count, head_dim, width),
        preferred_element_type=jnp.float32,
    )
    return (resid + update).astype(jnp.bfloat16)


def relay_local(latents, lengths, segment_layers, norm_gain, qkv_weight, qk_gain, out_weight):
    segment_count = lax.axis_size("section")
    segment_pos = lax.axis_index("section")
    micro_count, tok_rows, width = latents.shape
    slot_count = qkv_weight.shape[0]
    own_layers = segment_layers[0]
    tick_count = micro_count + segment_count - 1

    def slot_layer(slot_index, current, length):
        return body_layer(
            current,
            length,
            lax.dynamic_index_in_dim(norm_gain, slot_index, 0, False),
            lax.dynamic_index_in_dim(qkv_weight, slot_index, 0, False),
            lax.dynamic_index_in_dim(qk_gain, slot_index, 0, False),
            lax.dynamic_index_in_dim(out_weight, slot_index, 0, False),
        )

    def advance(tick_index, loop_state):
        received, finished = loop_state
        micro_index = tick_index - segment_pos
        is_valid = (micro_index >= 0) & (micro_index < micro_count)
        clipped = jnp.clip(micro_index, 0, micro_count - 1)
        entering = lax.dynamic_index_in_dim(latents, clipped, 0, False)
        current = jnp.where(segment_pos == 0, entering, received)
        length = lax.dynamic_index_in_dim(lengths, clipped, 0, False)
        for slot_index in range(slot_count):
            updated = slot_layer(slot_index, current, length)
            current = jnp.where(slot_index < own_layers, updated, current)
        previous = lax.dynamic_index_in_dim(finished, clipped, 0, True)
        keep_it = is_valid & (segment_pos == segment_count - 1)
        finished = lax.dynamic_update_index_in_dim(
            finished, jnp.where(keep_it, current[None], previous), clipped, 0
        )
        received = shifted(current, "section", 1)
        return (received, finished)

    start_state = (
        jnp.zeros((tok_rows, width), jnp.bfloat16),
        jnp.zeros((micro_count, tok_rows, width), jnp.bfloat16),
    )
    final_state = lax.fori_loop(0, tick_count, advance, start_state)
    finished = final_state[1]
    terms = jnp.where(segment_pos == segment_count - 1, finished.astype(jnp.float32), 0.0)
    return lax.psum_scatter(terms.astype(jnp.bfloat16), "section", scatter_dimension=2, tiled=True)


def norm_rows(dst, src, row, count, gain):
    values = src[pl.ds(row, count), :].astype(F32)
    mean = jnp.mean(values * values, axis=-1, keepdims=True)
    dst[pl.ds(row, count), :] = (values * lax.rsqrt(mean + eps_norm) * gain).astype(BF16)


def head_norm(acc, gain, head_ones):
    mean = jnp.dot((acc * acc).astype(BF16), head_ones[...], preferred_element_type=F32)
    return (acc * lax.rsqrt(mean + eps_norm) * gain).astype(BF16)


def spread_heads(dst, tile, block, head_dim):
    rows = block.shape[0]
    lane = lax.broadcasted_iota(jnp.int32, (1, TILE), 1) // head_dim
    for h in range(TILE // head_dim):
        dst[tile, h * rows : (h + 1) * rows, :] = jnp.where(lane == h, block, jnp.zeros_like(block))


def head_totals(weights, rows, head_dim):
    half = lax.broadcasted_iota(jnp.int32, (1, 128), 1) < 64
    totals = []
    for h in range(TILE // head_dim):
        low, high = h * rows, (h + 1) * rows
        total = None
        for at in range(low // 128 * 128, high, 128):
            piece = weights[:, at : at + 128]
            if at < low:
                piece = jnp.where(half, 0.0, piece)
            elif at + 128 > high:
                piece = jnp.where(half, piece, 0.0)
            total = piece if total is None else total + piece
        totals.append(1.0 / jnp.sum(total, axis=-1, keepdims=True))
    return totals


def keep_kernel(qkv_hbm, out_hbm, qkv_w, out_w, sems):
    copies = [pltpu.make_async_copy(qkv_hbm, qkv_w, sems.at[0]), pltpu.make_async_copy(out_hbm, out_w, sems.at[1])]
    for copy in copies:
        copy.start()
    for copy in copies:
        copy.wait()


def keep_weights(qkv_w, out_w):
    far = pl.BlockSpec(memory_space=pltpu.HBM)
    whole = pl.BlockSpec(memory_space=pltpu.VMEM)
    size = 2 * (qkv_w.size + out_w.size)
    return pl.pallas_call(
        keep_kernel,
        out_shape=[pltpu.VMEM(qkv_w.shape, BF16), pltpu.VMEM(out_w.shape, BF16)],
        in_specs=[far, far],
        out_specs=[whole, whole],
        scratch_shapes=[pltpu.SemaphoreType.DMA((2,))],
        compiler_params=pltpu.CompilerParams(vmem_limit_bytes=40 * 2**20),
        cost_estimate=pl.CostEstimate(flops=0, bytes_accessed=2 * size, transcendentals=0),
        name="keep_weights",
    )(qkv_w, out_w)


def sublayer(q_rows, q_start, head_dim, slot, refs, residual, store):
    xn, q_s, k_s, v_s, att, gains, bias, head_ones, qkv_w, out_w = refs
    rows = xn.shape[0]
    inner, width = out_w.shape[1:]
    tiles = inner // TILE
    q_gain, k_gain = gains[slot, 0:1, :], gains[slot, 1:2, :]
    log2e = 1.4426950408889634
    top = 1.01 * head_dim**0.5 * log2e * jnp.max(jnp.abs(q_gain)) * jnp.max(jnp.abs(k_gain))
    key_bias = bias[...] - top
    score_scale = head_dim ** (-0.5) * log2e
    def project(n):
        at = ((n + tiles) % (3 * tiles)) * TILE
        values = xn[...] if n < 2 * tiles else xn[pl.ds(q_start, q_rows), :]
        return jnp.dot(values, qkv_w[slot, :, at : at + TILE], preferred_element_type=F32)

    def keep(n, acc):
        if n < tiles:
            spread_heads(k_s, n, head_norm(acc, k_gain, head_ones), head_dim)
        elif n < 2 * tiles:
            spread_heads(v_s, n - tiles, acc.astype(BF16), head_dim)
        else:
            at = (n - 2 * tiles) * TILE
            q_s[0:q_rows, at : at + TILE] = head_norm(acc, q_gain, head_ones)

    for n in range(3 * tiles):
        keep(n, project(n))
    step = min(q_rows, 160)
    half = lax.broadcasted_iota(jnp.int32, (1, 128), 1) < 64
    for t in range(tiles):
        for r in range(0, q_rows, step):
            queries = q_s[r : r + step, t * TILE : (t + 1) * TILE]
            scores = lax.dot_general(queries, k_s[t], (((1,), (1,)), ((), ())), preferred_element_type=F32)
            weights = jnp.exp2(scores * score_scale + key_bias)
            inverse = head_totals(weights, rows, head_dim)
            mixed = jnp.dot(weights.astype(BF16), v_s[t], preferred_element_type=F32)
            for g in range(2):
                scale = jnp.where(half, inverse[2 * g], inverse[2 * g + 1])
                at = t * TILE + g * 128
                att[r : r + step, at : at + 128] = (mixed[:, g * 128 : (g + 1) * 128] * scale).astype(BF16)
    for at in range(0, width, TILE):
        acc = jnp.dot(att[0:q_rows, :], out_w[slot, :, at : at + TILE], preferred_element_type=F32)
        store(at, (residual(at) + acc).astype(BF16))


def stage_kernel(head_dim, parts, info, *refs):
    blocks, refs = refs[:parts], refs[parts:]
    norm_g, gains, bias, head_ones, qkv_w, out_w, out, x_s, xn, q_s, k_s, v_s, att = refs
    rows, out_rows = x_s.shape[0], out.shape[0]
    refs = (xn, q_s, k_s, v_s, att, gains, bias, head_ones, qkv_w, out_w)

    def norm_all(slot):
        gain = norm_g[slot]

        def one(step, carry):
            norm_rows(xn, x_s, pl.multiple_of(step * 16, 16), 16, gain)
            return carry

        lax.fori_loop(0, rows // 16, one, 0, unroll=10)

    @pl.when(info[0] != 0)
    def run():
        count, start, core = info[1], pl.multiple_of(info[2], 16), info[3]
        if parts == 2:
            half_rows = rows // 2
            x_s[0:half_rows, :] = blocks[0][...]
            x_s[half_rows:rows, :] = blocks[1][...]
        else:
            for n in range(parts // 2):
                own, other = blocks[n][...].astype(F32), blocks[n + parts // 2][...].astype(F32)
                first, second = jnp.where(core == 0, own, other), jnp.where(core == 0, other, own)
                both = jnp.concatenate([first, second], axis=0).astype(BF16)
                x_s[n * both.shape[0] : (n + 1) * both.shape[0], :] = both
        norm_all(0)

        @pl.when(count > 1)
        def first():
            def store(at, block):
                x_s[:, at : at + TILE] = block

            sublayer(rows, 0, head_dim, 0, refs, lambda at: x_s[:, at : at + TILE].astype(F32), store)
            norm_all(1)

        last = count - 1

        def store(at, block):
            out[:, at : at + TILE] = block

        def residual(at):
            return x_s[pl.ds(start, out_rows), at : at + TILE].astype(F32)

        sublayer(out_rows, start, head_dim, last, refs, residual, store)


def run_stage(info, blocks, norm_g, gains, bias, head_ones, qkv_w, out_w, head_dim, out_rows):
    rows = sum(block.shape[0] for block in blocks)
    slots, inner, width = out_w.shape
    tiles, per_tile = inner // TILE, TILE // head_dim
    whole = pl.BlockSpec(memory_space=pltpu.VMEM)
    qkv_w, out_w = (pltpu.with_memory_space_constraint(w, pltpu.VMEM) for w in (qkv_w, out_w))
    return pl.pallas_call(
        functools.partial(stage_kernel, head_dim, len(blocks)),
        out_shape=jax.ShapeDtypeStruct((out_rows, width), BF16),
        in_specs=[pl.BlockSpec(memory_space=pltpu.SMEM)] + [whole] * (len(blocks) + 6),
        out_specs=whole,
        scratch_shapes=[
            pltpu.VMEM((rows, width), BF16),
            pltpu.VMEM((rows, width), BF16),
            pltpu.VMEM((rows, inner), BF16),
            pltpu.VMEM((tiles, per_tile * rows, TILE), BF16),
            pltpu.VMEM((tiles, per_tile * rows, TILE), BF16),
            pltpu.VMEM((rows, inner), BF16),
        ],
        compiler_params=pltpu.CompilerParams(vmem_limit_bytes=16 * 2**20),
        name="stage",
    )(info, *blocks, norm_g, gains, bias, head_ones, qkv_w, out_w)


def sent(value, seq_count, pairs):
    flat = [(a * seq_count + b, c * seq_count + d) for (a, b), (c, d) in pairs]
    return lax.ppermute(value, ("section", "seq"), flat)


def pair_local(latents, lengths, segment_layers, norm_gain, qkv_weight, qk_gain, out_weight):
    sections = lax.axis_size("section")
    seq_count = lax.axis_size("seq")
    chips = seq_count // 2
    micro_count, tok_rows, width = latents.shape
    slots = qkv_weight.shape[0]
    head_dim = qk_gain.shape[1] // 2
    per_tile = TILE // head_dim
    section = lax.axis_index("section")
    seq = lax.axis_index("seq")
    chip, core = seq // 2, seq % 2
    micro = chip // 2
    seqs = range(seq_count)

    gains = jnp.tile(qk_gain.reshape(slots, 2, head_dim).astype(F32), (1, 1, per_tile))
    norm_g = norm_gain.astype(F32)[:, None, :]
    heads = jnp.arange(TILE) // head_dim
    head_ones = jnp.where(heads[:, None] == heads[None, :], 1.0 / head_dim, 0.0).astype(BF16)
    def key_bias(blocks):
        position = 2 * tok_rows * (blocks[:, None] ^ chip) + jnp.arange(2 * tok_rows)[None, :]
        bias = jnp.where(position.reshape(1, -1) < length, 0.0, neg_large).astype(F32)
        return jnp.tile(bias, (1, per_tile))

    length = lax.dynamic_index_in_dim(lengths, micro, 0, False)
    first_bias = key_bias(jnp.arange(chips))
    own_bias = key_bias(jnp.arange(chips) ^ (chips // 2 * core))
    own_layers = segment_layers[0]

    pieces = [lax.dynamic_index_in_dim(latents, micro, 0, False)]
    away = lax.dynamic_index_in_dim(latents, 1 - micro, 0, False)
    for k in range(1, chips):
        pairs = [(((0, 0, 1, 2)[k], s), (0, s ^ (2 * k))) for s in seqs]
        pieces.append(sent(pieces[0] if k < 2 else away, seq_count, pairs))
    blocks = pieces + [sent(part, seq_count, [((0, s), (0, s ^ 1)) for s in seqs]) for part in pieces]

    qkv_weight, out_weight = keep_weights(qkv_weight, out_weight)
    half_rows = chips * tok_rows
    for stage in range(sections):
        last = stage == sections - 1
        out_rows = 2 * tok_rows if last else half_rows
        start = half_rows * core if stage == 0 else jnp.int32(0)
        info = jnp.stack([(section == stage).astype(jnp.int32), own_layers, start, core])
        bias = own_bias if stage else first_bias
        own = run_stage(info, blocks, norm_g, gains, bias, head_ones, qkv_weight, out_weight, head_dim, out_rows)
        if not last:
            own = sent(own, seq_count, [((stage, s), (stage + 1, s)) for s in seqs])
            blocks = [own, sent(own, seq_count, [((stage + 1, s), (stage + 1, s ^ 1)) for s in seqs])]

    final = sections - 1
    cols = width // sections
    mine = None
    for t in range(sections):
        pairs = [((final, s), (t, 2 * ((s // 2) ^ (chips // 2 * (s % 2))) + s // 2 // (chips // 2))) for s in seqs]
        here = sent(own[:, t * cols : (t + 1) * cols], seq_count, pairs)
        mine = here if mine is None else jnp.where(section == t, here, mine)
    front, back = mine[:tok_rows], mine[tok_rows:]
    pairs = [((t, s), (t, s ^ 1)) for t in range(sections) for s in seqs]
    got = sent(jnp.where(core == 0, back, front), seq_count, pairs)
    return jnp.where(core == 0, jnp.stack([front, got]), jnp.stack([got, back]))


def local(latents, lengths, segment_layers, norm_gain, qkv_weight, qk_gain, out_weight):
    args = (latents, lengths, segment_layers, norm_gain, qkv_weight, qk_gain, out_weight)
    pairwise = lax.axis_size("seq") == 8 and latents.shape[0] == 2
    return pair_local(*args) if pairwise else relay_local(*args)


def solution(mesh):
    return jax.shard_map(
        local,
        mesh=mesh,
        in_specs=(
            P(None, "seq", None),
            P(),
            P("section"),
            P("section", None),
            P("section", None, None),
            P("section", None),
            P("section", None, None),
        ),
        out_specs=P(None, "seq", "section"),
        check_vma=False,
    )
```

```python
import functools

import jax
import jax.numpy as jnp
from jax import lax
from jax.experimental import pallas as pl
from jax.experimental.pallas import tpu as pltpu
from jax.sharding import PartitionSpec as P

eps_norm = 1e-06
neg_large = -1e30
F32, BF16 = jnp.float32, jnp.bfloat16
TILE = 256


def shifted(value, axis, steps):
    count = lax.axis_size(axis)
    leading, last = (max(0, -steps), min(count, count - steps))
    return lax.ppermute(value, axis, [(source, source + steps) for source in range(leading, last)])


def rms_scale(values, gain_vec):
    return (
        values * lax.rsqrt(jnp.mean(values * values, axis=-1, keepdims=True) + eps_norm) * gain_vec
    )


def body_layer(current, length, norm_w, qkv_w, qk_w, out_w):
    tok_rows, width = current.shape
    inner = qkv_w.shape[1] // 3
    head_dim = qk_w.shape[0] // 2
    head_count = inner // head_dim
    resid = current.astype(jnp.float32)
    normed = rms_scale(resid, norm_w.astype(jnp.float32)).astype(jnp.bfloat16)
    projected = jnp.dot(normed, qkv_w, preferred_element_type=jnp.float32)
    queries = rms_scale(
        projected[:, :inner].reshape(tok_rows, head_count, head_dim),
        qk_w[:head_dim].astype(jnp.float32),
    ).astype(jnp.bfloat16)
    keys = (
        rms_scale(
            projected[:, inner : 2 * inner].reshape(tok_rows, head_count, head_dim),
            qk_w[head_dim:].astype(jnp.float32),
        )
        .astype(jnp.bfloat16)
        .reshape(tok_rows, inner)
    )
    values = projected[:, 2 * inner :].astype(jnp.bfloat16)
    score_scale = head_dim ** (-0.5)
    run_max = jnp.full((head_count, tok_rows), neg_large, jnp.float32)
    key_block = lax.all_gather(keys, "seq", axis=0, tiled=True)
    value_block = lax.all_gather(values, "seq", axis=0, tiled=True)
    block_rows = key_block.shape[0]
    key_heads = key_block.reshape(block_rows, head_count, head_dim)
    value_heads = value_block.reshape(block_rows, head_count, head_dim)
    scores = (
        jnp.einsum("qhd,khd->hqk", queries, key_heads, preferred_element_type=jnp.float32)
        * score_scale
    )
    positions = jnp.arange(block_rows, dtype=jnp.int32)
    scores = jnp.where((positions < length)[None, None, :], scores, neg_large)
    new_max = jnp.maximum(run_max, jnp.max(scores, axis=-1))
    weights = jnp.exp(scores - new_max[..., None])
    run_total = jnp.sum(weights, axis=-1)
    run_acc = jnp.einsum(
        "hqk,khd->hqd",
        weights.astype(jnp.bfloat16),
        value_heads,
        preferred_element_type=jnp.float32,
    )
    run_max, run_total, run_acc = (new_max, run_total, run_acc)
    attended = (run_acc / run_total[..., None]).astype(jnp.bfloat16)
    update = jnp.einsum(
        "hqd,hde->qe",
        attended,
        out_w.reshape(head_count, head_dim, width),
        preferred_element_type=jnp.float32,
    )
    return (resid + update).astype(jnp.bfloat16)


def relay_local(latents, lengths, segment_layers, norm_gain, qkv_weight, qk_gain, out_weight):
    segment_count = lax.axis_size("section")
    segment_pos = lax.axis_index("section")
    micro_count, tok_rows, width = latents.shape
    slot_count = qkv_weight.shape[0]
    own_layers = segment_layers[0]
    tick_count = micro_count + segment_count - 1

    def slot_layer(slot_index, current, length):
        return body_layer(
            current,
            length,
            lax.dynamic_index_in_dim(norm_gain, slot_index, 0, False),
            lax.dynamic_index_in_dim(qkv_weight, slot_index, 0, False),
            lax.dynamic_index_in_dim(qk_gain, slot_index, 0, False),
            lax.dynamic_index_in_dim(out_weight, slot_index, 0, False),
        )

    def advance(tick_index, loop_state):
        received, finished = loop_state
        micro_index = tick_index - segment_pos
        is_valid = (micro_index >= 0) & (micro_index < micro_count)
        clipped = jnp.clip(micro_index, 0, micro_count - 1)
        entering = lax.dynamic_index_in_dim(latents, clipped, 0, False)
        current = jnp.where(segment_pos == 0, entering, received)
        length = lax.dynamic_index_in_dim(lengths, clipped, 0, False)
        for slot_index in range(slot_count):
            updated = slot_layer(slot_index, current, length)
            current = jnp.where(slot_index < own_layers, updated, current)
        previous = lax.dynamic_index_in_dim(finished, clipped, 0, True)
        keep_it = is_valid & (segment_pos == segment_count - 1)
        finished = lax.dynamic_update_index_in_dim(
            finished, jnp.where(keep_it, current[None], previous), clipped, 0
        )
        received = shifted(current, "section", 1)
        return (received, finished)

    start_state = (
        jnp.zeros((tok_rows, width), jnp.bfloat16),
        jnp.zeros((micro_count, tok_rows, width), jnp.bfloat16),
    )
    final_state = lax.fori_loop(0, tick_count, advance, start_state)
    finished = final_state[1]
    terms = jnp.where(segment_pos == segment_count - 1, finished.astype(jnp.float32), 0.0)
    return lax.psum_scatter(terms.astype(jnp.bfloat16), "section", scatter_dimension=2, tiled=True)


LOG2E = 1.4426950408889634


def row_of(ref, slot, first=0, slots=2):
    row = ref[first : first + 1, :]
    for n in range(1, slots):
        row = jnp.where(slot == n, ref[first + n : first + n + 1, :], row)
    return row


def norm_rows(dst, src, row, count, gain):
    values = src[pl.ds(row, count), :].astype(F32)
    mean = jnp.mean(values * values, axis=-1, keepdims=True)
    dst[pl.ds(row, count), :] = (values * lax.rsqrt(mean + eps_norm) * gain).astype(BF16)


def head_norm(acc, gain, head_ones):
    mean = jnp.dot((acc * acc).astype(BF16), head_ones[...], preferred_element_type=F32)
    return (acc * lax.rsqrt(mean + eps_norm) * gain).astype(BF16)


def spread_heads(dst, tile, block, head_dim):
    rows = block.shape[0]
    lane = lax.broadcasted_iota(jnp.int32, (1, TILE), 1) // head_dim
    for h in range(TILE // head_dim):
        dst[tile, h * rows : (h + 1) * rows, :] = jnp.where(lane == h, block, jnp.zeros_like(block))


def head_totals(weights, rows, head_dim):
    half = lax.broadcasted_iota(jnp.int32, (1, 128), 1) < 64
    totals = []
    for h in range(TILE // head_dim):
        low, high = h * rows, (h + 1) * rows
        total = None
        for at in range(low // 128 * 128, high, 128):
            piece = weights[:, at : at + 128]
            if at < low:
                piece = jnp.where(half, 0.0, piece)
            elif at + 128 > high:
                piece = jnp.where(half, piece, 0.0)
            total = piece if total is None else total + piece
        totals.append(1.0 / jnp.sum(total, axis=-1, keepdims=True))
    return totals


def keep_kernel(head_dim, lengths, qkv_hbm, out_hbm, norm_gain, qk_gain, qkv_w, out_w, norm_g, gains, bias, head_ones, token, sems):
    copies = [pltpu.make_async_copy(qkv_hbm, qkv_w, sems.at[0]), pltpu.make_async_copy(out_hbm, out_w, sems.at[1])]
    for copy in copies:
        copy.start()
    slots = norm_gain.shape[0]
    per_tile = TILE // head_dim
    norm_g[...] = norm_gain[...].astype(F32)
    rows_gain = qk_gain[...].astype(F32)
    both = [jnp.concatenate([rows_gain[:, n * head_dim : (n + 1) * head_dim]] * per_tile, axis=1) for n in range(2)]
    gains[...] = jnp.concatenate(both, axis=0)
    lane_head = lax.broadcasted_iota(jnp.int32, (TILE, TILE), 1) // head_dim
    row_head = lax.broadcasted_iota(jnp.int32, (TILE, TILE), 0) // head_dim
    head_ones[...] = jnp.where(lane_head == row_head, 1.0 / head_dim, 0.0).astype(BF16)
    chips = lax.axis_size("seq") // 2
    seq = lax.axis_index("seq")
    chip, core = seq // 2, seq % 2
    rows = bias.shape[1] // per_tile
    block = rows // chips
    key = lax.broadcasted_iota(jnp.int32, (1, bias.shape[1]), 1) % rows
    length = lengths[chip // (chips // lengths.shape[0])]
    biases = []
    for number in (key // block, (key // block) ^ (chips // 2 * core)):
        live = block * (number ^ chip) + key % block < length
        for slot in range(slots):
            most = jnp.max(jnp.abs(both[0][slot : slot + 1])) * jnp.max(jnp.abs(both[1][slot : slot + 1]))
            biases.append(jnp.where(live, -1.01 * head_dim**0.5 * LOG2E * most, neg_large))
    bias[...] = jnp.concatenate(biases, axis=0)
    token[...] = jnp.zeros_like(token)
    for copy in copies:
        copy.wait()


def keep_weights(lengths, qkv_w, out_w, norm_gain, qk_gain, rows):
    far = pl.BlockSpec(memory_space=pltpu.HBM)
    whole = pl.BlockSpec(memory_space=pltpu.VMEM)
    small = pl.BlockSpec(memory_space=pltpu.SMEM)
    size = 2 * (qkv_w.size + out_w.size)
    head_dim, slots = qk_gain.shape[1] // 2, qk_gain.shape[0]
    return pl.pallas_call(
        functools.partial(keep_kernel, head_dim),
        out_shape=[
            pltpu.VMEM(qkv_w.shape, BF16),
            pltpu.VMEM(out_w.shape, BF16),
            pltpu.VMEM(norm_gain.shape, F32),
            pltpu.VMEM((2 * slots, TILE), F32),
            pltpu.VMEM((2 * slots, TILE // head_dim * rows), F32),
            pltpu.VMEM((TILE, TILE), BF16),
            jax.ShapeDtypeStruct((8, 128), F32),
        ],
        in_specs=[small, far, far, whole, whole],
        out_specs=[whole] * 7,
        scratch_shapes=[pltpu.SemaphoreType.DMA((2,))],
        compiler_params=pltpu.CompilerParams(vmem_limit_bytes=40 * 2**20),
        cost_estimate=pl.CostEstimate(flops=0, bytes_accessed=2 * size, transcendentals=0),
        name="keep_weights",
    )(lengths, qkv_w, out_w, norm_gain, qk_gain)


def join_kernel(token, *refs):
    pieces, out = refs[:-1], refs[-1]
    out[...] = jnp.concatenate([piece[...].astype(F32) for piece in pieces], axis=0).astype(BF16)


def join_pieces(token, pieces):
    whole = pl.BlockSpec(memory_space=pltpu.VMEM)
    return pl.pallas_call(
        join_kernel,
        out_shape=jax.ShapeDtypeStruct((sum(piece.shape[0] for piece in pieces), pieces[0].shape[1]), BF16),
        in_specs=[whole] * (1 + len(pieces)),
        out_specs=whole,
        compiler_params=pltpu.CompilerParams(vmem_limit_bytes=8 * 2**20),
        name="join_pieces",
    )(token, *pieces)


def sublayer(chunk, chunks, head_dim, first_stage, slot, refs):
    x_s, xn, q_s, k_s, v_s, att, norm_g, gains, bias, head_ones, qkv_w, out_w = refs
    rows = xn.shape[0]
    inner, width = out_w.shape[1:]
    tiles, per_tile = inner // TILE, TILE // head_dim
    slots = out_w.shape[0]
    q_gain = row_of(gains, slot, 0, slots)
    k_gain = row_of(gains, slot, slots, slots)
    key_bias = row_of(bias, slot, 0 if first_stage else slots, slots)
    score_scale = head_dim ** (-0.5) * LOG2E
    gain = row_of(norm_g, slot, 0, slots)

    def norm_step(step, carry):
        norm_rows(xn, x_s, pl.multiple_of(step * 16, 16), 16, gain)
        return carry

    lax.fori_loop(0, rows // 16, norm_step, 0, unroll=20)

    def project(values, tile):
        return jnp.dot(values, qkv_w[slot, :, tile * TILE : (tile + 1) * TILE], preferred_element_type=F32)

    def keep(kind, t, acc):
        if kind == 0:
            q_s[:, t * TILE : (t + 1) * TILE] = head_norm(acc, q_gain, head_ones)
        elif kind == 1:
            spread_heads(k_s, t, head_norm(acc, k_gain, head_ones), head_dim)
        else:
            spread_heads(v_s, t, acc.astype(BF16), head_dim)

    waiting = None
    for kind, t in [(kind, t) for kind in (1, 0, 2) for t in range(tiles)]:
        acc = project(xn[...], kind * tiles + t)
        if waiting is not None:
            keep(*waiting)
        waiting = (kind, t, acc)
    keep(*waiting)
    half = lax.broadcasted_iota(jnp.int32, (1, 128), 1) < 64

    def chunk_step(n, carry):
        q_rows = pl.ds(pl.multiple_of(n * chunk, 16), chunk)
        for t in range(tiles):
            scores = lax.dot_general(q_s[q_rows, t * TILE : (t + 1) * TILE], k_s[t], (((1,), (1,)), ((), ())), preferred_element_type=F32)
            weights = jnp.exp2(scores * score_scale + key_bias)
            inverse = head_totals(weights, rows, head_dim)
            mixed = jnp.dot(weights.astype(BF16), v_s[t], preferred_element_type=F32)
            for g in range(2):
                scale = jnp.where(half, inverse[2 * g], inverse[2 * g + 1])
                at = t * TILE + g * 128
                att[:, at : at + 128] = (mixed[:, g * 128 : (g + 1) * 128] * scale).astype(BF16)
        for at in range(0, width, TILE):
            acc = jnp.dot(att[...], out_w[slot, :, at : at + TILE], preferred_element_type=F32)
            x_s[q_rows, at : at + TILE] = (x_s[q_rows, at : at + TILE].astype(F32) + acc).astype(BF16)
        return carry

    lax.fori_loop(chunks[0], chunks[1], chunk_step, 0)


def stage_kernel(head_dim, stage, layers, own, other, qkv_w, out_w, norm_g, gains, bias, head_ones, out, x_s, xn, q_s, k_s, v_s, att):
    rows, chunk = x_s.shape[0], out.shape[0]
    half_rows = rows // 2
    chips = lax.axis_size("seq") // 2
    refs = (x_s, xn, q_s, k_s, v_s, att, norm_g, gains, bias, head_ones, qkv_w, out_w)

    @pl.when(lax.axis_index("section") == stage)
    def run():
        count = layers[0]
        core = lax.axis_index("seq") % 2
        block = rows // chips
        if stage == 0:
            start = core
            piece = block // 2
            mine, theirs = own[...].astype(F32), other[...].astype(F32)
            first, second = jnp.where(core == 0, mine, theirs), jnp.where(core == 0, theirs, mine)
            for k in range(chips):
                part = slice(k * piece, (k + 1) * piece)
                both = jnp.concatenate([first[part], second[part]], axis=0).astype(BF16)
                x_s[k * block : (k + 1) * block, :] = both
        else:
            start = 0
            x_s[0:half_rows, :] = own[...]
            x_s[half_rows:rows, :] = other[...]

        def one_slot(slot, carry):
            last = slot == count - 1
            chunks = jnp.where(last, start, 0), jnp.where(last, start + 1, rows // chunk)
            sublayer(chunk, chunks, head_dim, stage == 0, slot, refs)
            return carry

        lax.fori_loop(0, count, one_slot, 0)
        out[...] = x_s[pl.ds(pl.multiple_of(start * chunk, 16), chunk), :]


def run_stage(stage, layers, own, other, kept, head_dim, out_rows):
    kept = [pltpu.with_memory_space_constraint(array, pltpu.VMEM) for array in kept]
    out_w = kept[1]
    half_rows, width = own.shape
    rows = 2 * half_rows
    inner = out_w.shape[1]
    tiles, per_tile = inner // TILE, TILE // head_dim
    whole = pl.BlockSpec(memory_space=pltpu.VMEM)
    small = pl.BlockSpec(memory_space=pltpu.SMEM)
    return pl.pallas_call(
        functools.partial(stage_kernel, head_dim, stage),
        out_shape=jax.ShapeDtypeStruct((out_rows, width), BF16),
        in_specs=[small] + [whole] * 8,
        out_specs=whole,
        scratch_shapes=[
            pltpu.VMEM((rows, width), BF16),
            pltpu.VMEM((rows, width), BF16),
            pltpu.VMEM((rows, inner), BF16),
            pltpu.VMEM((tiles, per_tile * rows, TILE), BF16),
            pltpu.VMEM((tiles, per_tile * rows, TILE), BF16),
            pltpu.VMEM((out_rows, inner), BF16),
        ],
        compiler_params=pltpu.CompilerParams(vmem_limit_bytes=16 * 2**20),
        name="stage",
    )(layers, own, other, *kept)


def sent(value, seq_count, pairs):
    flat = [(a * seq_count + b, c * seq_count + d) for (a, b), (c, d) in pairs]
    return lax.ppermute(value, ("section", "seq"), flat)


def pair_local(latents, lengths, segment_layers, norm_gain, qkv_weight, qk_gain, out_weight):
    sections = lax.axis_size("section")
    seq_count = lax.axis_size("seq")
    chips = seq_count // 2
    micro_count, tok_rows, width = latents.shape
    section = lax.axis_index("section")
    seq = lax.axis_index("seq")
    core = seq % 2
    micro = seq // 2 // (chips // micro_count)
    seqs = range(seq_count)

    pieces = [lax.dynamic_index_in_dim(latents, micro, 0, False)]
    away = lax.dynamic_index_in_dim(latents, 1 - micro, 0, False)
    for k in range(1, chips):
        pairs = [(((0, 0, 1, 2)[k], s), (0, s ^ (2 * k))) for s in seqs]
        pieces.append(sent(pieces[0] if k < 2 else away, seq_count, pairs))
    *kept, token = keep_weights(lengths, qkv_weight, out_weight, norm_gain, qk_gain, seq_count * tok_rows)
    own = join_pieces(token, pieces)

    half_rows = chips * tok_rows
    for stage in range(sections):
        last = stage == sections - 1
        out_rows = half_rows if last else half_rows
        other = sent(own, seq_count, [((stage, s), (stage, s ^ 1)) for s in seqs])
        own = run_stage(stage, segment_layers, own, other, kept, qk_gain.shape[1] // 2, out_rows)
        if not last:
            own = sent(own, seq_count, [((stage, s), (stage + 1, s)) for s in seqs])

    final = sections - 1
    cols = width // sections
    mine = None
    for t in range(sections):
        pairs = [((final, s), (t, 2 * ((s // 2) ^ (chips // 2 * (s % 2))) + s // 2 // (chips // 2))) for s in seqs]
        here = sent(own[: 2 * tok_rows, t * cols : (t + 1) * cols], seq_count, pairs)
        mine = here if mine is None else jnp.where(section == t, here, mine)
    front, back = mine[:tok_rows], mine[tok_rows:]
    pairs = [((t, s), (t, s ^ 1)) for t in range(sections) for s in seqs]
    got = sent(jnp.where(core == 0, back, front), seq_count, pairs)
    return jnp.where(core == 0, jnp.stack([front, got]), jnp.stack([got, back]))


def local(latents, lengths, segment_layers, norm_gain, qkv_weight, qk_gain, out_weight):
    args = (latents, lengths, segment_layers, norm_gain, qkv_weight, qk_gain, out_weight)
    pairwise = lax.axis_size("seq") == 8 and latents.shape[0] == 2
    return pair_local(*args) if pairwise else relay_local(*args)


def solution(mesh):
    return jax.shard_map(
        local,
        mesh=mesh,
        in_specs=(
            P(None, "seq", None),
            P(),
            P("section"),
            P("section", None),
            P("section", None, None),
            P("section", None),
            P("section", None, None),
        ),
        out_specs=P(None, "seq", "section"),
        check_vma=False,
    )
```

```python
import functools

import jax
import jax.numpy as jnp
from jax import lax
from jax.experimental import pallas as pl
from jax.experimental.pallas import tpu as pltpu
from jax.sharding import PartitionSpec as P

eps_norm = 1e-06
neg_large = -1e30
F32, BF16 = jnp.float32, jnp.bfloat16
TILE = 256


def shifted(value, axis, steps):
    count = lax.axis_size(axis)
    leading, last = (max(0, -steps), min(count, count - steps))
    return lax.ppermute(value, axis, [(source, source + steps) for source in range(leading, last)])


def rms_scale(values, gain_vec):
    return (
        values * lax.rsqrt(jnp.mean(values * values, axis=-1, keepdims=True) + eps_norm) * gain_vec
    )


def body_layer(current, length, norm_w, qkv_w, qk_w, out_w):
    tok_rows, width = current.shape
    inner = qkv_w.shape[1] // 3
    head_dim = qk_w.shape[0] // 2
    head_count = inner // head_dim
    resid = current.astype(jnp.float32)
    normed = rms_scale(resid, norm_w.astype(jnp.float32)).astype(jnp.bfloat16)
    projected = jnp.dot(normed, qkv_w, preferred_element_type=jnp.float32)
    queries = rms_scale(
        projected[:, :inner].reshape(tok_rows, head_count, head_dim),
        qk_w[:head_dim].astype(jnp.float32),
    ).astype(jnp.bfloat16)
    keys = (
        rms_scale(
            projected[:, inner : 2 * inner].reshape(tok_rows, head_count, head_dim),
            qk_w[head_dim:].astype(jnp.float32),
        )
        .astype(jnp.bfloat16)
        .reshape(tok_rows, inner)
    )
    values = projected[:, 2 * inner :].astype(jnp.bfloat16)
    score_scale = head_dim ** (-0.5)
    run_max = jnp.full((head_count, tok_rows), neg_large, jnp.float32)
    key_block = lax.all_gather(keys, "seq", axis=0, tiled=True)
    value_block = lax.all_gather(values, "seq", axis=0, tiled=True)
    block_rows = key_block.shape[0]
    key_heads = key_block.reshape(block_rows, head_count, head_dim)
    value_heads = value_block.reshape(block_rows, head_count, head_dim)
    scores = (
        jnp.einsum("qhd,khd->hqk", queries, key_heads, preferred_element_type=jnp.float32)
        * score_scale
    )
    positions = jnp.arange(block_rows, dtype=jnp.int32)
    scores = jnp.where((positions < length)[None, None, :], scores, neg_large)
    new_max = jnp.maximum(run_max, jnp.max(scores, axis=-1))
    weights = jnp.exp(scores - new_max[..., None])
    run_total = jnp.sum(weights, axis=-1)
    run_acc = jnp.einsum(
        "hqk,khd->hqd",
        weights.astype(jnp.bfloat16),
        value_heads,
        preferred_element_type=jnp.float32,
    )
    run_max, run_total, run_acc = (new_max, run_total, run_acc)
    attended = (run_acc / run_total[..., None]).astype(jnp.bfloat16)
    update = jnp.einsum(
        "hqd,hde->qe",
        attended,
        out_w.reshape(head_count, head_dim, width),
        preferred_element_type=jnp.float32,
    )
    return (resid + update).astype(jnp.bfloat16)


def relay_local(latents, lengths, segment_layers, norm_gain, qkv_weight, qk_gain, out_weight):
    segment_count = lax.axis_size("section")
    segment_pos = lax.axis_index("section")
    micro_count, tok_rows, width = latents.shape
    slot_count = qkv_weight.shape[0]
    own_layers = segment_layers[0]
    tick_count = micro_count + segment_count - 1

    def slot_layer(slot_index, current, length):
        return body_layer(
            current,
            length,
            lax.dynamic_index_in_dim(norm_gain, slot_index, 0, False),
            lax.dynamic_index_in_dim(qkv_weight, slot_index, 0, False),
            lax.dynamic_index_in_dim(qk_gain, slot_index, 0, False),
            lax.dynamic_index_in_dim(out_weight, slot_index, 0, False),
        )

    def advance(tick_index, loop_state):
        received, finished = loop_state
        micro_index = tick_index - segment_pos
        is_valid = (micro_index >= 0) & (micro_index < micro_count)
        clipped = jnp.clip(micro_index, 0, micro_count - 1)
        entering = lax.dynamic_index_in_dim(latents, clipped, 0, False)
        current = jnp.where(segment_pos == 0, entering, received)
        length = lax.dynamic_index_in_dim(lengths, clipped, 0, False)
        for slot_index in range(slot_count):
            updated = slot_layer(slot_index, current, length)
            current = jnp.where(slot_index < own_layers, updated, current)
        previous = lax.dynamic_index_in_dim(finished, clipped, 0, True)
        keep_it = is_valid & (segment_pos == segment_count - 1)
        finished = lax.dynamic_update_index_in_dim(
            finished, jnp.where(keep_it, current[None], previous), clipped, 0
        )
        received = shifted(current, "section", 1)
        return (received, finished)

    start_state = (
        jnp.zeros((tok_rows, width), jnp.bfloat16),
        jnp.zeros((micro_count, tok_rows, width), jnp.bfloat16),
    )
    final_state = lax.fori_loop(0, tick_count, advance, start_state)
    finished = final_state[1]
    terms = jnp.where(segment_pos == segment_count - 1, finished.astype(jnp.float32), 0.0)
    return lax.psum_scatter(terms.astype(jnp.bfloat16), "section", scatter_dimension=2, tiled=True)


LOG2E = 1.4426950408889634
PIECES = (0, 2, 1, 3)


def row_of(ref, slot, first=0, slots=2):
    row = ref[first : first + 1, :]
    for n in range(1, slots):
        row = jnp.where(slot == n, ref[first + n : first + n + 1, :], row)
    return row


def norm_rows(dst, src, row, count, gain):
    values = src[pl.ds(row, count), :].astype(F32)
    mean = jnp.mean(values * values, axis=-1, keepdims=True)
    dst[pl.ds(row, count), :] = (values * lax.rsqrt(mean + eps_norm) * gain).astype(BF16)


def head_norm(acc, gain, head_ones):
    mean = jnp.dot((acc * acc).astype(BF16), head_ones[...], preferred_element_type=F32)
    return (acc * lax.rsqrt(mean + eps_norm) * gain).astype(BF16)


def spread_heads(dst, tile, block, head_dim):
    rows = block.shape[0]
    lane = lax.broadcasted_iota(jnp.int32, (1, TILE), 1) // head_dim
    for h in range(TILE // head_dim):
        dst[tile, h * rows : (h + 1) * rows, :] = jnp.where(lane == h, block, jnp.zeros_like(block))


def head_totals(weights, rows, head_dim):
    half = lax.broadcasted_iota(jnp.int32, (1, 128), 1) < 64
    totals = []
    for h in range(TILE // head_dim):
        low, high = h * rows, (h + 1) * rows
        total = None
        for at in range(low // 128 * 128, high, 128):
            piece = weights[:, at : at + 128]
            if at < low:
                piece = jnp.where(half, 0.0, piece)
            elif at + 128 > high:
                piece = jnp.where(half, piece, 0.0)
            total = piece if total is None else total + piece
        totals.append(1.0 / jnp.sum(total, axis=-1, keepdims=True))
    return totals


def keep_kernel(head_dim, lengths, qkv_hbm, norm_gain, qk_gain, qkv_w, norm_g, gains, bias, head_ones, token, sem):
    copy = pltpu.make_async_copy(qkv_hbm, qkv_w, sem)
    copy.start()
    slots = norm_gain.shape[0]
    per_tile = TILE // head_dim
    norm_g[...] = norm_gain[...].astype(F32)
    rows_gain = qk_gain[...].astype(F32)
    both = [jnp.concatenate([rows_gain[:, n * head_dim : (n + 1) * head_dim]] * per_tile, axis=1) for n in range(2)]
    gains[...] = jnp.concatenate(both, axis=0)
    lane_head = lax.broadcasted_iota(jnp.int32, (TILE, TILE), 1) // head_dim
    row_head = lax.broadcasted_iota(jnp.int32, (TILE, TILE), 0) // head_dim
    head_ones[...] = jnp.where(lane_head == row_head, 1.0 / head_dim, 0.0).astype(BF16)
    chips = lax.axis_size("seq") // 2
    seq = lax.axis_index("seq")
    chip, core = seq // 2, seq % 2
    rows = bias.shape[1] // per_tile
    block = rows // chips
    key = lax.broadcasted_iota(jnp.int32, (1, bias.shape[1]), 1) % rows
    length = lengths[chip % lengths.shape[0]]
    biases = []
    for number in (key // block, (key // block) ^ (chips // 2 * core)):
        piece = functools.reduce(lambda found, n: jnp.where(number == n, PIECES[n], found), range(1, len(PIECES)), 0)
        live = block * (piece ^ chip) + key % block < length
        for slot in range(slots):
            most = jnp.max(jnp.abs(both[0][slot : slot + 1])) * jnp.max(jnp.abs(both[1][slot : slot + 1]))
            biases.append(jnp.where(live, -1.01 * head_dim**0.5 * LOG2E * most, neg_large))
    bias[...] = jnp.concatenate(biases, axis=0)
    token[...] = jnp.zeros_like(token)
    copy.wait()


def keep_out_kernel(after, out_hbm, out_w, sem):
    copy = pltpu.make_async_copy(out_hbm, out_w, sem)
    copy.start()
    copy.wait()


def keep_out(after, out_w):
    far = pl.BlockSpec(memory_space=pltpu.HBM)
    whole = pl.BlockSpec(memory_space=pltpu.VMEM)
    return pl.pallas_call(
        keep_out_kernel,
        out_shape=pltpu.VMEM(out_w.shape, BF16),
        in_specs=[whole, far],
        out_specs=whole,
        scratch_shapes=[pltpu.SemaphoreType.DMA],
        compiler_params=pltpu.CompilerParams(vmem_limit_bytes=28 * 2**20),
        cost_estimate=pl.CostEstimate(flops=0, bytes_accessed=4 * out_w.size, transcendentals=0),
        name="keep_out",
    )(after, out_w)


def keep_weights(lengths, qkv_w, norm_gain, qk_gain, rows):
    far = pl.BlockSpec(memory_space=pltpu.HBM)
    whole = pl.BlockSpec(memory_space=pltpu.VMEM)
    small = pl.BlockSpec(memory_space=pltpu.SMEM)
    head_dim, slots = qk_gain.shape[1] // 2, qk_gain.shape[0]
    return pl.pallas_call(
        functools.partial(keep_kernel, head_dim),
        out_shape=[
            pltpu.VMEM(qkv_w.shape, BF16),
            pltpu.VMEM(norm_gain.shape, F32),
            pltpu.VMEM((2 * slots, TILE), F32),
            pltpu.VMEM((2 * slots, TILE // head_dim * rows), F32),
            pltpu.VMEM((TILE, TILE), BF16),
            pltpu.VMEM((8, 128), F32),
        ],
        in_specs=[small, far, whole, whole],
        out_specs=[whole] * 6,
        scratch_shapes=[pltpu.SemaphoreType.DMA],
        compiler_params=pltpu.CompilerParams(vmem_limit_bytes=40 * 2**20),
        cost_estimate=pl.CostEstimate(flops=0, bytes_accessed=4 * qkv_w.size, transcendentals=0),
        name="keep_weights",
    )(lengths, qkv_w, norm_gain, qk_gain)


def join_kernel(token, *refs):
    pieces, out = refs[:-1], refs[-1]
    out[...] = jnp.concatenate([piece[...].astype(F32) for piece in pieces], axis=0).astype(BF16)


def join_pieces(token, pieces):
    token = pltpu.with_memory_space_constraint(token, pltpu.VMEM)
    whole = pl.BlockSpec(memory_space=pltpu.VMEM)
    return pl.pallas_call(
        join_kernel,
        out_shape=jax.ShapeDtypeStruct((sum(piece.shape[0] for piece in pieces), pieces[0].shape[1]), BF16),
        in_specs=[whole] * (1 + len(pieces)),
        out_specs=whole,
        compiler_params=pltpu.CompilerParams(vmem_limit_bytes=8 * 2**20),
        name="join_pieces",
    )(token, *pieces)


def sublayer(chunk, chunks, head_dim, first_stage, slot, refs):
    x_s, xn, q_s, k_s, v_s, att, norm_g, gains, bias, head_ones, qkv_w, out_w = refs
    rows = xn.shape[0]
    inner, width = out_w.shape[1:]
    tiles, per_tile = inner // TILE, TILE // head_dim
    slots = out_w.shape[0]
    q_gain = row_of(gains, slot, 0, slots)
    k_gain = row_of(gains, slot, slots, slots)
    key_bias = row_of(bias, slot, 0 if first_stage else slots, slots)
    score_scale = head_dim ** (-0.5) * LOG2E
    gain = row_of(norm_g, slot, 0, slots)

    def norm_step(step, carry):
        norm_rows(xn, x_s, pl.multiple_of(step * 16, 16), 16, gain)
        return carry

    lax.fori_loop(0, rows // 16, norm_step, 0, unroll=20)

    def project(values, tile):
        return jnp.dot(values, qkv_w[slot, :, tile * TILE : (tile + 1) * TILE], preferred_element_type=F32)

    def keep(kind, t, acc):
        if kind == 0:
            q_s[:, t * TILE : (t + 1) * TILE] = head_norm(acc, q_gain, head_ones)
        elif kind == 1:
            spread_heads(k_s, t, head_norm(acc, k_gain, head_ones), head_dim)
        else:
            spread_heads(v_s, t, acc.astype(BF16), head_dim)

    waiting = None
    for kind, t in [(kind, t) for kind in (1, 0, 2) for t in range(tiles)]:
        acc = project(xn[...], kind * tiles + t)
        if waiting is not None:
            keep(*waiting)
        waiting = (kind, t, acc)
    keep(*waiting)
    half = lax.broadcasted_iota(jnp.int32, (1, 128), 1) < 64

    def chunk_step(n, carry):
        q_rows = pl.ds(pl.multiple_of(n * chunk, 16), chunk)
        for t in range(tiles):
            scores = lax.dot_general(q_s[q_rows, t * TILE : (t + 1) * TILE], k_s[t], (((1,), (1,)), ((), ())), preferred_element_type=F32)
            weights = jnp.exp2(scores * score_scale + key_bias)
            inverse = head_totals(weights, rows, head_dim)
            mixed = jnp.dot(weights.astype(BF16), v_s[t], preferred_element_type=F32)
            for g in range(2):
                scale = jnp.where(half, inverse[2 * g], inverse[2 * g + 1])
                at = t * TILE + g * 128
                att[:, at : at + 128] = (mixed[:, g * 128 : (g + 1) * 128] * scale).astype(BF16)
        for at in range(0, width, TILE):
            acc = jnp.dot(att[...], out_w[slot, :, at : at + TILE], preferred_element_type=F32)
            x_s[q_rows, at : at + TILE] = (x_s[q_rows, at : at + TILE].astype(F32) + acc).astype(BF16)
        return carry

    lax.fori_loop(chunks[0], chunks[1], chunk_step, 0)


def stage_kernel(head_dim, stage, layers, own, other, qkv_w, out_w, norm_g, gains, bias, head_ones, out, x_s, xn, q_s, k_s, v_s, att):
    rows, chunk = x_s.shape[0], out.shape[0]
    half_rows = rows // 2
    chips = lax.axis_size("seq") // 2
    refs = (x_s, xn, q_s, k_s, v_s, att, norm_g, gains, bias, head_ones, qkv_w, out_w)

    @pl.when(lax.axis_index("section") == stage)
    def run():
        count = layers[0]
        core = lax.axis_index("seq") % 2
        block = rows // chips
        if stage == 0:
            start = core
            piece = block // 2
            mine, theirs = own[...].astype(F32), other[...].astype(F32)
            first, second = jnp.where(core == 0, mine, theirs), jnp.where(core == 0, theirs, mine)
            for k in range(chips):
                part = slice(k * piece, (k + 1) * piece)
                both = jnp.concatenate([first[part], second[part]], axis=0).astype(BF16)
                x_s[k * block : (k + 1) * block, :] = both
        else:
            start = 0
            x_s[0:half_rows, :] = own[...]
            x_s[half_rows:rows, :] = other[...]

        def one_slot(slot, carry):
            last = slot == count - 1
            chunks = jnp.where(last, start, 0), jnp.where(last, start + 1, rows // chunk)
            sublayer(chunk, chunks, head_dim, stage == 0, slot, refs)
            return carry

        lax.fori_loop(0, count, one_slot, 0)
        out[...] = x_s[pl.ds(pl.multiple_of(start * chunk, 16), chunk), :]


def run_stage(stage, layers, own, other, kept, head_dim, out_rows):
    kept = [pltpu.with_memory_space_constraint(array, pltpu.VMEM) for array in kept]
    out_w = kept[1]
    half_rows, width = own.shape
    rows = 2 * half_rows
    inner = out_w.shape[1]
    tiles, per_tile = inner // TILE, TILE // head_dim
    whole = pl.BlockSpec(memory_space=pltpu.VMEM)
    small = pl.BlockSpec(memory_space=pltpu.SMEM)
    return pl.pallas_call(
        functools.partial(stage_kernel, head_dim, stage),
        out_shape=jax.ShapeDtypeStruct((out_rows, width), BF16),
        in_specs=[small] + [whole] * 8,
        out_specs=whole,
        scratch_shapes=[
            pltpu.VMEM((rows, width), BF16),
            pltpu.VMEM((rows, width), BF16),
            pltpu.VMEM((rows, inner), BF16),
            pltpu.VMEM((tiles, per_tile * rows, TILE), BF16),
            pltpu.VMEM((tiles, per_tile * rows, TILE), BF16),
            pltpu.VMEM((out_rows, inner), BF16),
        ],
        compiler_params=pltpu.CompilerParams(vmem_limit_bytes=16 * 2**20),
        name="stage",
    )(layers, own, other, *kept)


def sent(value, seq_count, pairs):
    flat = [(a * seq_count + b, c * seq_count + d) for (a, b), (c, d) in pairs]
    return lax.ppermute(value, ("section", "seq"), flat)


def pair_local(latents, lengths, segment_layers, norm_gain, qkv_weight, qk_gain, out_weight):
    sections = lax.axis_size("section")
    seq_count = lax.axis_size("seq")
    chips = seq_count // 2
    micro_count, tok_rows, width = latents.shape
    section = lax.axis_index("section")
    seq = lax.axis_index("seq")
    core = seq % 2
    micro = seq // 2 % micro_count
    seqs = range(seq_count)

    pieces = [lax.dynamic_index_in_dim(latents, micro, 0, False)]
    away = lax.dynamic_index_in_dim(latents, 1 - micro, 0, False)
    for k in range(1, chips):
        pairs = [((k, s), (0, s ^ (2 * k))) for s in seqs]
        pieces.append(sent(away if k % micro_count else pieces[0], seq_count, pairs))
    qkv_kept, *kept, token = keep_weights(lengths, qkv_weight, norm_gain, qk_gain, seq_count * tok_rows)
    own = join_pieces(token, [pieces[k] for k in PIECES])
    kept = [qkv_kept, keep_out(own, out_weight), *kept]

    half_rows = chips * tok_rows
    for stage in range(sections):
        last = stage == sections - 1
        out_rows = half_rows if last else half_rows
        other = sent(own, seq_count, [((t, s), (t, s ^ 1)) for t in range(sections) for s in seqs])
        own = run_stage(stage, segment_layers, own, other, kept, qk_gain.shape[1] // 2, out_rows)
        if not last:
            own = sent(own, seq_count, [((stage, s), (stage + 1, s)) for s in seqs])

    final = sections - 1
    cols = width // sections
    mine = None
    for t in range(sections):
        pairs = [((final, s), (t, 2 * ((s // 2) ^ (s % 2)) + s // 2 % micro_count)) for s in seqs]
        here = sent(own[: 2 * tok_rows, t * cols : (t + 1) * cols], seq_count, pairs)
        mine = here if mine is None else jnp.where(section == t, here, mine)
    front, back = mine[:tok_rows], mine[tok_rows:]
    pairs = [((t, s), (t, s ^ 1)) for t in range(sections) for s in seqs]
    got = sent(jnp.where(core == 0, back, front), seq_count, pairs)
    return jnp.where(core == 0, jnp.stack([front, got]), jnp.stack([got, back]))


def local(latents, lengths, segment_layers, norm_gain, qkv_weight, qk_gain, out_weight):
    args = (latents, lengths, segment_layers, norm_gain, qkv_weight, qk_gain, out_weight)
    pairwise = lax.axis_size("seq") == 8 and latents.shape[0] == 2
    return pair_local(*args) if pairwise else relay_local(*args)


def solution(mesh):
    return jax.shard_map(
        local,
        mesh=mesh,
        in_specs=(
            P(None, "seq", None),
            P(),
            P("section"),
            P("section", None),
            P("section", None, None),
            P("section", None),
            P("section", None, None),
        ),
        out_specs=P(None, "seq", "section"),
        check_vma=False,
    )
```

```python
import functools

import jax
import jax.numpy as jnp
from jax import lax
from jax.experimental import pallas as pl
from jax.experimental.pallas import tpu as pltpu
from jax.sharding import PartitionSpec as P

eps_norm = 1e-06
neg_large = -1e30
F32, BF16 = jnp.float32, jnp.bfloat16
TILE = 256


def shifted(value, axis, steps):
    count = lax.axis_size(axis)
    leading, last = (max(0, -steps), min(count, count - steps))
    return lax.ppermute(value, axis, [(source, source + steps) for source in range(leading, last)])


def rms_scale(values, gain_vec):
    return (
        values * lax.rsqrt(jnp.mean(values * values, axis=-1, keepdims=True) + eps_norm) * gain_vec
    )


def body_layer(current, length, norm_w, qkv_w, qk_w, out_w):
    tok_rows, width = current.shape
    inner = qkv_w.shape[1] // 3
    head_dim = qk_w.shape[0] // 2
    head_count = inner // head_dim
    resid = current.astype(jnp.float32)
    normed = rms_scale(resid, norm_w.astype(jnp.float32)).astype(jnp.bfloat16)
    projected = jnp.dot(normed, qkv_w, preferred_element_type=jnp.float32)
    queries = rms_scale(
        projected[:, :inner].reshape(tok_rows, head_count, head_dim),
        qk_w[:head_dim].astype(jnp.float32),
    ).astype(jnp.bfloat16)
    keys = (
        rms_scale(
            projected[:, inner : 2 * inner].reshape(tok_rows, head_count, head_dim),
            qk_w[head_dim:].astype(jnp.float32),
        )
        .astype(jnp.bfloat16)
        .reshape(tok_rows, inner)
    )
    values = projected[:, 2 * inner :].astype(jnp.bfloat16)
    score_scale = head_dim ** (-0.5)
    run_max = jnp.full((head_count, tok_rows), neg_large, jnp.float32)
    key_block = lax.all_gather(keys, "seq", axis=0, tiled=True)
    value_block = lax.all_gather(values, "seq", axis=0, tiled=True)
    block_rows = key_block.shape[0]
    key_heads = key_block.reshape(block_rows, head_count, head_dim)
    value_heads = value_block.reshape(block_rows, head_count, head_dim)
    scores = (
        jnp.einsum("qhd,khd->hqk", queries, key_heads, preferred_element_type=jnp.float32)
        * score_scale
    )
    positions = jnp.arange(block_rows, dtype=jnp.int32)
    scores = jnp.where((positions < length)[None, None, :], scores, neg_large)
    new_max = jnp.maximum(run_max, jnp.max(scores, axis=-1))
    weights = jnp.exp(scores - new_max[..., None])
    run_total = jnp.sum(weights, axis=-1)
    run_acc = jnp.einsum(
        "hqk,khd->hqd",
        weights.astype(jnp.bfloat16),
        value_heads,
        preferred_element_type=jnp.float32,
    )
    run_max, run_total, run_acc = (new_max, run_total, run_acc)
    attended = (run_acc / run_total[..., None]).astype(jnp.bfloat16)
    update = jnp.einsum(
        "hqd,hde->qe",
        attended,
        out_w.reshape(head_count, head_dim, width),
        preferred_element_type=jnp.float32,
    )
    return (resid + update).astype(jnp.bfloat16)


def relay_local(latents, lengths, segment_layers, norm_gain, qkv_weight, qk_gain, out_weight):
    segment_count = lax.axis_size("section")
    segment_pos = lax.axis_index("section")
    micro_count, tok_rows, width = latents.shape
    slot_count = qkv_weight.shape[0]
    own_layers = segment_layers[0]
    tick_count = micro_count + segment_count - 1

    def slot_layer(slot_index, current, length):
        return body_layer(
            current,
            length,
            lax.dynamic_index_in_dim(norm_gain, slot_index, 0, False),
            lax.dynamic_index_in_dim(qkv_weight, slot_index, 0, False),
            lax.dynamic_index_in_dim(qk_gain, slot_index, 0, False),
            lax.dynamic_index_in_dim(out_weight, slot_index, 0, False),
        )

    def advance(tick_index, loop_state):
        received, finished = loop_state
        micro_index = tick_index - segment_pos
        is_valid = (micro_index >= 0) & (micro_index < micro_count)
        clipped = jnp.clip(micro_index, 0, micro_count - 1)
        entering = lax.dynamic_index_in_dim(latents, clipped, 0, False)
        current = jnp.where(segment_pos == 0, entering, received)
        length = lax.dynamic_index_in_dim(lengths, clipped, 0, False)
        for slot_index in range(slot_count):
            updated = slot_layer(slot_index, current, length)
            current = jnp.where(slot_index < own_layers, updated, current)
        previous = lax.dynamic_index_in_dim(finished, clipped, 0, True)
        keep_it = is_valid & (segment_pos == segment_count - 1)
        finished = lax.dynamic_update_index_in_dim(
            finished, jnp.where(keep_it, current[None], previous), clipped, 0
        )
        received = shifted(current, "section", 1)
        return (received, finished)

    start_state = (
        jnp.zeros((tok_rows, width), jnp.bfloat16),
        jnp.zeros((micro_count, tok_rows, width), jnp.bfloat16),
    )
    final_state = lax.fori_loop(0, tick_count, advance, start_state)
    finished = final_state[1]
    terms = jnp.where(segment_pos == segment_count - 1, finished.astype(jnp.float32), 0.0)
    return lax.psum_scatter(terms.astype(jnp.bfloat16), "section", scatter_dimension=2, tiled=True)


LOG2E = 1.4426950408889634
PIECES = (0, 2, 1, 3)


def row_of(ref, slot, first=0, slots=2):
    row = ref[first : first + 1, :]
    for n in range(1, slots):
        row = jnp.where(slot == n, ref[first + n : first + n + 1, :], row)
    return row


def norm_rows(dst, src, start, gain):
    for row in range(0, dst.shape[0], 16):
        values = src[pl.ds(start + row, 16), :].astype(F32)
        mean = jnp.mean(values * values, axis=-1, keepdims=True)
        dst[row : row + 16, :] = (values * lax.rsqrt(mean + eps_norm) * gain).astype(BF16)


def head_norm(acc, gain, head_ones):
    mean = jnp.dot((acc * acc).astype(BF16), head_ones[...], preferred_element_type=F32)
    return (acc * lax.rsqrt(mean + eps_norm) * gain).astype(BF16)


def spread_heads(dst, tile, block, start, head_dim):
    per_tile = TILE // head_dim
    rows = dst.shape[1] // per_tile
    lane = lax.broadcasted_iota(jnp.int32, (1, TILE), 1) // head_dim
    for h in range(per_tile):
        dst[tile, pl.ds(h * rows + start, block.shape[0]), :] = jnp.where(lane == h, block, jnp.zeros_like(block))


def head_totals(weights, rows, head_dim):
    half = lax.broadcasted_iota(jnp.int32, (1, 128), 1) < 64
    totals = []
    for h in range(TILE // head_dim):
        low, high = h * rows, (h + 1) * rows
        total = None
        for at in range(low // 128 * 128, high, 128):
            piece = weights[:, at : at + 128]
            if at < low:
                piece = jnp.where(half, 0.0, piece)
            elif at + 128 > high:
                piece = jnp.where(half, piece, 0.0)
            total = piece if total is None else total + piece
        totals.append(1.0 / jnp.sum(total, axis=-1, keepdims=True))
    return totals


def keep_kernel(head_dim, lengths, qkv_hbm, norm_gain, qk_gain, qkv_w, norm_g, gains, bias, head_ones, token, sem):
    copy = pltpu.make_async_copy(qkv_hbm, qkv_w, sem)
    copy.start()
    slots = norm_gain.shape[0]
    per_tile = TILE // head_dim
    norm_g[...] = norm_gain[...].astype(F32)
    rows_gain = qk_gain[...].astype(F32)
    both = [jnp.concatenate([rows_gain[:, n * head_dim : (n + 1) * head_dim]] * per_tile, axis=1) for n in range(2)]
    gains[...] = jnp.concatenate(both, axis=0)
    lane_head = lax.broadcasted_iota(jnp.int32, (TILE, TILE), 1) // head_dim
    row_head = lax.broadcasted_iota(jnp.int32, (TILE, TILE), 0) // head_dim
    head_ones[...] = jnp.where(lane_head == row_head, 1.0 / head_dim, 0.0).astype(BF16)
    chips = lax.axis_size("seq") // 2
    seq = lax.axis_index("seq")
    chip, core = seq // 2, seq % 2
    rows = bias.shape[1] // per_tile
    piece = rows // chips // 2
    row = lax.broadcasted_iota(jnp.int32, (1, bias.shape[1]), 1) % rows
    number, half = row // piece % chips, row // (piece * chips)
    later = number % 2 + (chips // 2) * (half ^ core)
    length = lengths[chip % lengths.shape[0]]
    biases = []
    for block, from_core in ((number, half ^ core), (later, (number // 2) ^ half ^ core)):
        away = functools.reduce(lambda found, n: jnp.where(block == n, PIECES[n], found), range(1, len(PIECES)), 0)
        live = piece * (2 * (away ^ chip) + from_core) + row % piece < length
        for slot in range(slots):
            most = jnp.max(jnp.abs(both[0][slot : slot + 1])) * jnp.max(jnp.abs(both[1][slot : slot + 1]))
            biases.append(jnp.where(live, -1.01 * head_dim**0.5 * LOG2E * most, neg_large))
    bias[...] = jnp.concatenate(biases, axis=0)
    token[...] = jnp.zeros_like(token)
    copy.wait()


def keep_out_kernel(after, out_hbm, out_w, sem):
    copy = pltpu.make_async_copy(out_hbm, out_w, sem)
    copy.start()
    copy.wait()


def keep_out(after, out_w):
    far = pl.BlockSpec(memory_space=pltpu.HBM)
    whole = pl.BlockSpec(memory_space=pltpu.VMEM)
    return pl.pallas_call(
        keep_out_kernel,
        out_shape=pltpu.VMEM(out_w.shape, BF16),
        in_specs=[whole, far],
        out_specs=whole,
        scratch_shapes=[pltpu.SemaphoreType.DMA],
        compiler_params=pltpu.CompilerParams(vmem_limit_bytes=28 * 2**20),
        cost_estimate=pl.CostEstimate(flops=0, bytes_accessed=4 * out_w.size, transcendentals=0),
        name="keep_out",
    )(after, out_w)


def keep_weights(lengths, qkv_w, norm_gain, qk_gain, rows):
    far = pl.BlockSpec(memory_space=pltpu.HBM)
    whole = pl.BlockSpec(memory_space=pltpu.VMEM)
    small = pl.BlockSpec(memory_space=pltpu.SMEM)
    head_dim, slots = qk_gain.shape[1] // 2, qk_gain.shape[0]
    return pl.pallas_call(
        functools.partial(keep_kernel, head_dim),
        out_shape=[
            pltpu.VMEM(qkv_w.shape, BF16),
            pltpu.VMEM(norm_gain.shape, F32),
            pltpu.VMEM((2 * slots, TILE), F32),
            pltpu.VMEM((2 * slots, TILE // head_dim * rows), F32),
            pltpu.VMEM((TILE, TILE), BF16),
            pltpu.VMEM((8, 128), F32),
        ],
        in_specs=[small, far, whole, whole],
        out_specs=[whole] * 6,
        scratch_shapes=[pltpu.SemaphoreType.DMA],
        compiler_params=pltpu.CompilerParams(vmem_limit_bytes=40 * 2**20),
        cost_estimate=pl.CostEstimate(flops=0, bytes_accessed=4 * qkv_w.size, transcendentals=0),
        name="keep_weights",
    )(lengths, qkv_w, norm_gain, qk_gain)


def join_kernel(token, *refs):
    pieces, out = refs[:-1], refs[-1]
    out[...] = jnp.concatenate([piece[...].astype(F32) for piece in pieces], axis=0).astype(BF16)


def join_pieces(token, pieces):
    token = pltpu.with_memory_space_constraint(token, pltpu.VMEM)
    whole = pl.BlockSpec(memory_space=pltpu.VMEM)
    return pl.pallas_call(
        join_kernel,
        out_shape=jax.ShapeDtypeStruct((sum(piece.shape[0] for piece in pieces), pieces[0].shape[1]), BF16),
        in_specs=[whole] * (1 + len(pieces)),
        out_specs=whole,
        compiler_params=pltpu.CompilerParams(vmem_limit_bytes=8 * 2**20),
        name="join_pieces",
    )(token, *pieces)


def project_half(src, src_start, start, slot, head_dim, xn, k_s, v_s, q_s, qkv_w, norm_g, gains, head_ones):
    slots, inner = qkv_w.shape[0], qkv_w.shape[2] // 3
    tiles = inner // TILE
    q_gain, k_gain = row_of(gains, slot, 0, slots), row_of(gains, slot, slots, slots)
    norm_rows(xn, src, src_start, row_of(norm_g, slot, 0, slots))

    def keep(kind, t, acc):
        if kind == 0:
            q_s[pl.ds(start, acc.shape[0]), t * TILE : (t + 1) * TILE] = head_norm(acc, q_gain, head_ones)
        elif kind == 1:
            spread_heads(k_s, t, head_norm(acc, k_gain, head_ones), start, head_dim)
        else:
            spread_heads(v_s, t, acc.astype(BF16), start, head_dim)

    waiting = None
    for kind, t in [(kind, t) for kind in (1, 0, 2) for t in range(tiles)]:
        at = kind * inner + t * TILE
        acc = jnp.dot(xn[...], qkv_w[slot, :, at : at + TILE], preferred_element_type=F32)
        if waiting is not None:
            keep(*waiting)
        waiting = (kind, t, acc)
    keep(*waiting)


def attend_rows(starts, part, key_bias, slot, head_dim, x_s, att, k_s, v_s, q_s, out_w):
    rows = x_s.shape[0]
    inner, width = out_w.shape[1:]
    parts = [pl.ds(pl.multiple_of(start, 16), part) for start in starts]
    half = lax.broadcasted_iota(jnp.int32, (1, 128), 1) < 64
    for t in range(inner // TILE):
        queries = jnp.concatenate([q_s[rows_of, t * TILE : (t + 1) * TILE] for rows_of in parts], axis=0)
        scores = lax.dot_general(queries, k_s[t], (((1,), (1,)), ((), ())), preferred_element_type=F32)
        weights = jnp.exp2(scores * (head_dim ** (-0.5) * LOG2E) + key_bias)
        inverse = head_totals(weights, rows, head_dim)
        mixed = jnp.dot(weights.astype(BF16), v_s[t], preferred_element_type=F32)
        for g in range(2):
            scale = jnp.where(half, inverse[2 * g], inverse[2 * g + 1])
            at = t * TILE + g * 128
            att[:, at : at + 128] = (mixed[:, g * 128 : (g + 1) * 128] * scale).astype(BF16)
    for at in range(0, width, TILE):
        acc = jnp.dot(att[...], out_w[slot, :, at : at + TILE], preferred_element_type=F32)
        for n, rows_of in enumerate(parts):
            before = x_s[rows_of, at : at + TILE].astype(F32)
            x_s[rows_of, at : at + TILE] = (before + acc[n * part : (n + 1) * part]).astype(BF16)


def own_kernel(head_dim, stage, own, qkv_w, norm_g, gains, head_ones, k_s, v_s, q_s, xn):
    @pl.when(lax.axis_index("section") == stage)
    def run():
        project_half(own, 0, 0, 0, head_dim, xn, k_s, v_s, q_s, qkv_w, norm_g, gains, head_ones)


def stage_kernel(head_dim, stage, last_stage, layers, own, other, qkv_w, out_w, norm_g, gains, bias, head_ones, k_in, v_in, q_in, out, k_s, v_s, q_s, x_s, xn, att):
    half_rows = own.shape[0]
    rows, part = 2 * half_rows, half_rows // 2
    slots = out_w.shape[0]

    @pl.when(lax.axis_index("section") == stage)
    def run():
        count = layers[0]
        core = lax.axis_index("seq") % 2
        x_s[0:half_rows, :] = own[...]
        x_s[half_rows:rows, :] = other[...]

        def one_slot(slot, carry):
            def one_half(n, carry):
                start = pl.multiple_of(n * half_rows, 16)
                project_half(x_s, start, start, slot, head_dim, xn, k_s, v_s, q_s, qkv_w, norm_g, gains, head_ones)
                return carry

            lax.fori_loop(jnp.where(slot == 0, 1, 0), 2, one_half, 0)
            key_bias = row_of(bias, slot, slots * min(stage, 1), slots)
            last = slot == count - 1

            def one_chunk(n, carry):
                if stage == 0:
                    starts = [jnp.where(last, half_rows * k + part * core, half_rows * n + part * k) for k in range(2)]
                else:
                    starts = [half_rows * n + part * k for k in range(2)]
                attend_rows(starts, part, key_bias, slot, head_dim, x_s, att, k_s, v_s, q_s, out_w)
                return carry

            lax.fori_loop(0, jnp.where(last, 1, 2), one_chunk, 0)
            return carry

        lax.fori_loop(0, count, one_slot, 0)
        if stage == 0:
            for k in range(2):
                start = pl.multiple_of(half_rows * k + part * core, 16)
                out[k * part : (k + 1) * part, :] = x_s[pl.ds(start, part), :]
        elif last_stage:
            piece = part // 2
            rows_out = [x_s[k * part : (k + 1) * part, :].astype(F32)[:piece] for k in range(2)]
            out[...] = jnp.concatenate(rows_out, axis=0).astype(BF16)
        else:
            out[...] = x_s[0:half_rows, :]


def run_stage(stage, last_stage, layers, own, other, kept, head_dim):
    qkv_w, out_w, norm_g, gains, bias, head_ones = (pltpu.with_memory_space_constraint(array, pltpu.VMEM) for array in kept)
    half_rows, width = own.shape
    rows, inner = 2 * half_rows, out_w.shape[1]
    whole = pl.BlockSpec(memory_space=pltpu.VMEM)
    small = pl.BlockSpec(memory_space=pltpu.SMEM)
    heads = (inner // TILE, TILE // head_dim * rows, TILE)
    made_shapes = [pltpu.VMEM(heads, BF16), pltpu.VMEM(heads, BF16), pltpu.VMEM((rows, inner), BF16)]
    made = pl.pallas_call(
        functools.partial(own_kernel, head_dim, stage),
        out_shape=made_shapes,
        in_specs=[whole] * 5,
        out_specs=[whole] * 3,
        scratch_shapes=[pltpu.VMEM((half_rows, width), BF16)],
        compiler_params=pltpu.CompilerParams(vmem_limit_bytes=8 * 2**20),
        cost_estimate=pl.CostEstimate(flops=6 * half_rows * width * inner, bytes_accessed=0, transcendentals=0),
        name="own_half",
    )(own, qkv_w, norm_g, gains, head_ones)
    made = [pltpu.with_memory_space_constraint(array, pltpu.VMEM) for array in made]
    out_rows = half_rows // 2 if last_stage else half_rows
    return pl.pallas_call(
        functools.partial(stage_kernel, head_dim, stage, last_stage),
        out_shape=[jax.ShapeDtypeStruct((out_rows, width), BF16)] + made_shapes,
        in_specs=[small] + [whole] * 11,
        out_specs=[whole] * 4,
        scratch_shapes=[
            pltpu.VMEM((rows, width), BF16),
            pltpu.VMEM((half_rows, width), BF16),
            pltpu.VMEM((half_rows, inner), BF16),
        ],
        input_output_aliases={9: 1, 10: 2, 11: 3},
        compiler_params=pltpu.CompilerParams(vmem_limit_bytes=12 * 2**20),
        name="stage",
    )(layers, own, other, qkv_w, out_w, norm_g, gains, bias, head_ones, *made)[0]


def sent(value, seq_count, pairs):
    flat = [(a * seq_count + b, c * seq_count + d) for (a, b), (c, d) in pairs]
    return lax.ppermute(value, ("section", "seq"), flat)


def pair_local(latents, lengths, segment_layers, norm_gain, qkv_weight, qk_gain, out_weight):
    sections = lax.axis_size("section")
    seq_count = lax.axis_size("seq")
    chips = seq_count // 2
    micro_count, tok_rows, width = latents.shape
    section = lax.axis_index("section")
    seq = lax.axis_index("seq")
    core = seq % 2
    micro = seq // 2 % micro_count
    seqs = range(seq_count)

    pieces = [lax.dynamic_index_in_dim(latents, micro, 0, False)]
    away = lax.dynamic_index_in_dim(latents, 1 - micro, 0, False)
    for k in range(1, chips):
        pairs = [((k, s), (0, s ^ (2 * k))) for s in seqs]
        pieces.append(sent(away if k % micro_count else pieces[0], seq_count, pairs))
    qkv_kept, *kept, token = keep_weights(lengths, qkv_weight, norm_gain, qk_gain, seq_count * tok_rows)
    own = join_pieces(token, [pieces[k] for k in PIECES])
    kept = [qkv_kept, keep_out(own, out_weight), *kept]

    for stage in range(sections):
        last = stage == sections - 1
        other = sent(own, seq_count, [((t, s), (t, s ^ 1)) for t in range(sections) for s in seqs])
        own = run_stage(stage, last, segment_layers, own, other, kept, qk_gain.shape[1] // 2)
        if not last:
            own = sent(own, seq_count, [((stage, s), (stage + 1, s)) for s in seqs])

    final = sections - 1
    cols = width // sections
    mine = None
    for t in range(sections):
        pairs = [((final, s), (t, 2 * ((s // 2) ^ (s % 2)) + s // 2 % micro_count)) for s in seqs]
        here = sent(own[:, t * cols : (t + 1) * cols], seq_count, pairs)
        mine = here if mine is None else jnp.where(section == t, here, mine)
    turned = seq // 2 % micro_count != core
    front = jnp.where(turned, mine[tok_rows:], mine[:tok_rows])
    back = jnp.where(turned, mine[:tok_rows], mine[tok_rows:])
    pairs = [((t, s), (t, s ^ 1)) for t in range(sections) for s in seqs]
    got = sent(jnp.where(core == 0, back, front), seq_count, pairs)
    return jnp.where(core == 0, jnp.stack([front, got]), jnp.stack([got, back]))


def local(latents, lengths, segment_layers, norm_gain, qkv_weight, qk_gain, out_weight):
    args = (latents, lengths, segment_layers, norm_gain, qkv_weight, qk_gain, out_weight)
    pairwise = lax.axis_size("seq") == 8 and latents.shape[0] == 2
    return pair_local(*args) if pairwise else relay_local(*args)


def solution(mesh):
    return jax.shard_map(
        local,
        mesh=mesh,
        in_specs=(
            P(None, "seq", None),
            P(),
            P("section"),
            P("section", None),
            P("section", None, None),
            P("section", None),
            P("section", None, None),
        ),
        out_specs=P(None, "seq", "section"),
        check_vma=False,
    )
```

```python
import functools

import jax
import jax.numpy as jnp
from jax import lax
from jax.experimental import pallas as pl
from jax.experimental.pallas import tpu as pltpu
from jax.sharding import PartitionSpec as P

eps_norm = 1e-06
neg_large = -1e30
F32, BF16 = jnp.float32, jnp.bfloat16
TILE = 256


def shifted(value, axis, steps):
    count = lax.axis_size(axis)
    leading, last = (max(0, -steps), min(count, count - steps))
    return lax.ppermute(value, axis, [(source, source + steps) for source in range(leading, last)])


def rms_scale(values, gain_vec):
    return (
        values * lax.rsqrt(jnp.mean(values * values, axis=-1, keepdims=True) + eps_norm) * gain_vec
    )


def body_layer(current, length, norm_w, qkv_w, qk_w, out_w):
    tok_rows, width = current.shape
    inner = qkv_w.shape[1] // 3
    head_dim = qk_w.shape[0] // 2
    head_count = inner // head_dim
    resid = current.astype(jnp.float32)
    normed = rms_scale(resid, norm_w.astype(jnp.float32)).astype(jnp.bfloat16)
    projected = jnp.dot(normed, qkv_w, preferred_element_type=jnp.float32)
    queries = rms_scale(
        projected[:, :inner].reshape(tok_rows, head_count, head_dim),
        qk_w[:head_dim].astype(jnp.float32),
    ).astype(jnp.bfloat16)
    keys = (
        rms_scale(
            projected[:, inner : 2 * inner].reshape(tok_rows, head_count, head_dim),
            qk_w[head_dim:].astype(jnp.float32),
        )
        .astype(jnp.bfloat16)
        .reshape(tok_rows, inner)
    )
    values = projected[:, 2 * inner :].astype(jnp.bfloat16)
    score_scale = head_dim ** (-0.5)
    run_max = jnp.full((head_count, tok_rows), neg_large, jnp.float32)
    key_block = lax.all_gather(keys, "seq", axis=0, tiled=True)
    value_block = lax.all_gather(values, "seq", axis=0, tiled=True)
    block_rows = key_block.shape[0]
    key_heads = key_block.reshape(block_rows, head_count, head_dim)
    value_heads = value_block.reshape(block_rows, head_count, head_dim)
    scores = (
        jnp.einsum("qhd,khd->hqk", queries, key_heads, preferred_element_type=jnp.float32)
        * score_scale
    )
    positions = jnp.arange(block_rows, dtype=jnp.int32)
    scores = jnp.where((positions < length)[None, None, :], scores, neg_large)
    new_max = jnp.maximum(run_max, jnp.max(scores, axis=-1))
    weights = jnp.exp(scores - new_max[..., None])
    run_total = jnp.sum(weights, axis=-1)
    run_acc = jnp.einsum(
        "hqk,khd->hqd",
        weights.astype(jnp.bfloat16),
        value_heads,
        preferred_element_type=jnp.float32,
    )
    run_max, run_total, run_acc = (new_max, run_total, run_acc)
    attended = (run_acc / run_total[..., None]).astype(jnp.bfloat16)
    update = jnp.einsum(
        "hqd,hde->qe",
        attended,
        out_w.reshape(head_count, head_dim, width),
        preferred_element_type=jnp.float32,
    )
    return (resid + update).astype(jnp.bfloat16)


def relay_local(latents, lengths, segment_layers, norm_gain, qkv_weight, qk_gain, out_weight):
    segment_count = lax.axis_size("section")
    segment_pos = lax.axis_index("section")
    micro_count, tok_rows, width = latents.shape
    slot_count = qkv_weight.shape[0]
    own_layers = segment_layers[0]
    tick_count = micro_count + segment_count - 1

    def slot_layer(slot_index, current, length):
        return body_layer(
            current,
            length,
            lax.dynamic_index_in_dim(norm_gain, slot_index, 0, False),
            lax.dynamic_index_in_dim(qkv_weight, slot_index, 0, False),
            lax.dynamic_index_in_dim(qk_gain, slot_index, 0, False),
            lax.dynamic_index_in_dim(out_weight, slot_index, 0, False),
        )

    def advance(tick_index, loop_state):
        received, finished = loop_state
        micro_index = tick_index - segment_pos
        is_valid = (micro_index >= 0) & (micro_index < micro_count)
        clipped = jnp.clip(micro_index, 0, micro_count - 1)
        entering = lax.dynamic_index_in_dim(latents, clipped, 0, False)
        current = jnp.where(segment_pos == 0, entering, received)
        length = lax.dynamic_index_in_dim(lengths, clipped, 0, False)
        for slot_index in range(slot_count):
            updated = slot_layer(slot_index, current, length)
            current = jnp.where(slot_index < own_layers, updated, current)
        previous = lax.dynamic_index_in_dim(finished, clipped, 0, True)
        keep_it = is_valid & (segment_pos == segment_count - 1)
        finished = lax.dynamic_update_index_in_dim(
            finished, jnp.where(keep_it, current[None], previous), clipped, 0
        )
        received = shifted(current, "section", 1)
        return (received, finished)

    start_state = (
        jnp.zeros((tok_rows, width), jnp.bfloat16),
        jnp.zeros((micro_count, tok_rows, width), jnp.bfloat16),
    )
    final_state = lax.fori_loop(0, tick_count, advance, start_state)
    finished = final_state[1]
    terms = jnp.where(segment_pos == segment_count - 1, finished.astype(jnp.float32), 0.0)
    return lax.psum_scatter(terms.astype(jnp.bfloat16), "section", scatter_dimension=2, tiled=True)


LOG2E = 1.4426950408889634


def row_of(ref, slot, first=0, slots=2):
    row = ref[first : first + 1, :]
    for n in range(1, slots):
        row = jnp.where(slot == n, ref[first + n : first + n + 1, :], row)
    return row


def norm_rows(dst, src, start, gain):
    for row in range(0, dst.shape[0], 16):
        values = src[pl.ds(start + row, 16), :].astype(F32)
        mean = jnp.mean(values * values, axis=-1, keepdims=True)
        dst[row : row + 16, :] = (values * lax.rsqrt(mean + eps_norm) * gain).astype(BF16)


def head_norm(acc, gain, head_ones):
    mean = jnp.dot((acc * acc).astype(BF16), head_ones[...], preferred_element_type=F32)
    return (acc * lax.rsqrt(mean + eps_norm) * gain).astype(BF16)


def spread_heads(dst, tile, block, start, head_dim):
    per_tile = TILE // head_dim
    rows = dst.shape[1] // per_tile
    lane = lax.broadcasted_iota(jnp.int32, (1, TILE), 1) // head_dim
    for h in range(per_tile):
        dst[tile, pl.ds(h * rows + start, block.shape[0]), :] = jnp.where(lane == h, block, jnp.zeros_like(block))


def head_totals(weights, rows, head_dim):
    half = lax.broadcasted_iota(jnp.int32, (1, 128), 1) < 64
    totals = []
    for h in range(TILE // head_dim):
        low, high = h * rows, (h + 1) * rows
        total = None
        for at in range(low // 128 * 128, high, 128):
            piece = weights[:, at : at + 128]
            if at < low:
                piece = jnp.where(half, 0.0, piece)
            elif at + 128 > high:
                piece = jnp.where(half, piece, 0.0)
            total = piece if total is None else total + piece
        totals.append(1.0 / jnp.sum(total, axis=-1, keepdims=True))
    return totals


def keep_kernel(head_dim, lengths, qkv_hbm, norm_gain, qk_gain, qkv_w, norm_g, gains, bias, head_ones, token, sem):
    copy = pltpu.make_async_copy(qkv_hbm, qkv_w, sem)
    copy.start()
    slots = norm_gain.shape[0]
    per_tile = TILE // head_dim
    norm_g[...] = norm_gain[...].astype(F32)
    rows_gain = qk_gain[...].astype(F32)
    both = [jnp.concatenate([rows_gain[:, n * head_dim : (n + 1) * head_dim]] * per_tile, axis=1) for n in range(2)]
    gains[...] = jnp.concatenate(both, axis=0)
    lane_head = lax.broadcasted_iota(jnp.int32, (TILE, TILE), 1) // head_dim
    row_head = lax.broadcasted_iota(jnp.int32, (TILE, TILE), 0) // head_dim
    head_ones[...] = jnp.where(lane_head == row_head, 1.0 / head_dim, 0.0).astype(BF16)
    chips = lax.axis_size("seq") // 2
    seq = lax.axis_index("seq")
    chip, core = seq // 2, seq % 2
    rows = bias.shape[1] // per_tile
    piece = rows // chips // 2
    row = lax.broadcasted_iota(jnp.int32, (1, bias.shape[1]), 1) % rows
    number, half = row // piece % chips, row // (piece * chips)
    owner = half ^ core
    order = row // piece % chips
    later = 2 * owner + order // 2, owner ^ ((order + order // 2) % 2)
    length = lengths[chip // (chips // lengths.shape[0])]
    biases = []
    for block, from_core in ((number, owner), later):
        live = piece * (2 * (block ^ chip) + from_core) + row % piece < length
        for slot in range(slots):
            most = jnp.max(jnp.abs(both[0][slot : slot + 1])) * jnp.max(jnp.abs(both[1][slot : slot + 1]))
            biases.append(jnp.where(live, -1.01 * head_dim**0.5 * LOG2E * most, neg_large))
    bias[...] = jnp.concatenate(biases, axis=0)
    token[...] = jnp.zeros_like(token)
    copy.wait()


def keep_out_kernel(after, out_hbm, out_w, sem):
    copy = pltpu.make_async_copy(out_hbm, out_w, sem)
    copy.start()
    copy.wait()


def keep_out(after, out_w):
    far = pl.BlockSpec(memory_space=pltpu.HBM)
    whole = pl.BlockSpec(memory_space=pltpu.VMEM)
    return pl.pallas_call(
        keep_out_kernel,
        out_shape=pltpu.VMEM(out_w.shape, BF16),
        in_specs=[whole, far],
        out_specs=whole,
        scratch_shapes=[pltpu.SemaphoreType.DMA],
        compiler_params=pltpu.CompilerParams(vmem_limit_bytes=28 * 2**20),
        cost_estimate=pl.CostEstimate(flops=0, bytes_accessed=4 * out_w.size, transcendentals=0),
        name="keep_out",
    )(after, out_w)


def keep_weights(lengths, qkv_w, norm_gain, qk_gain, rows):
    far = pl.BlockSpec(memory_space=pltpu.HBM)
    whole = pl.BlockSpec(memory_space=pltpu.VMEM)
    small = pl.BlockSpec(memory_space=pltpu.SMEM)
    head_dim, slots = qk_gain.shape[1] // 2, qk_gain.shape[0]
    return pl.pallas_call(
        functools.partial(keep_kernel, head_dim),
        out_shape=[
            pltpu.VMEM(qkv_w.shape, BF16),
            pltpu.VMEM(norm_gain.shape, F32),
            pltpu.VMEM((2 * slots, TILE), F32),
            pltpu.VMEM((2 * slots, TILE // head_dim * rows), F32),
            pltpu.VMEM((TILE, TILE), BF16),
            pltpu.VMEM((8, 128), F32),
        ],
        in_specs=[small, far, whole, whole],
        out_specs=[whole] * 6,
        scratch_shapes=[pltpu.SemaphoreType.DMA],
        compiler_params=pltpu.CompilerParams(vmem_limit_bytes=40 * 2**20),
        cost_estimate=pl.CostEstimate(flops=0, bytes_accessed=4 * qkv_w.size, transcendentals=0),
        name="keep_weights",
    )(lengths, qkv_w, norm_gain, qk_gain)


def join_kernel(token, *refs):
    pieces, out = refs[:-1], refs[-1]
    out[...] = jnp.concatenate([piece[...].astype(F32) for piece in pieces], axis=0).astype(BF16)


def join_pieces(token, pieces):
    token = pltpu.with_memory_space_constraint(token, pltpu.VMEM)
    whole = pl.BlockSpec(memory_space=pltpu.VMEM)
    return pl.pallas_call(
        join_kernel,
        out_shape=jax.ShapeDtypeStruct((sum(piece.shape[0] for piece in pieces), pieces[0].shape[1]), BF16),
        in_specs=[whole] * (1 + len(pieces)),
        out_specs=whole,
        compiler_params=pltpu.CompilerParams(vmem_limit_bytes=8 * 2**20),
        name="join_pieces",
    )(token, *pieces)


def project_half(src, src_start, start, slot, head_dim, xn, k_s, v_s, q_s, qkv_w, norm_g, gains, head_ones):
    slots, inner = qkv_w.shape[0], qkv_w.shape[2] // 3
    tiles = inner // TILE
    q_gain, k_gain = row_of(gains, slot, 0, slots), row_of(gains, slot, slots, slots)
    norm_rows(xn, src, src_start, row_of(norm_g, slot, 0, slots))

    def keep(kind, t, acc):
        if kind == 0:
            q_s[pl.ds(start, acc.shape[0]), t * TILE : (t + 1) * TILE] = head_norm(acc, q_gain, head_ones)
        elif kind == 1:
            spread_heads(k_s, t, head_norm(acc, k_gain, head_ones), start, head_dim)
        else:
            spread_heads(v_s, t, acc.astype(BF16), start, head_dim)

    waiting = None
    for kind, t in [(kind, t) for kind in (1, 0, 2) for t in range(tiles)]:
        at = kind * inner + t * TILE
        acc = jnp.dot(xn[...], qkv_w[slot, :, at : at + TILE], preferred_element_type=F32)
        if waiting is not None:
            keep(*waiting)
        waiting = (kind, t, acc)
    keep(*waiting)


def attend_rows(starts, part, key_bias, slot, head_dim, x_s, att, k_s, v_s, q_s, out_w):
    rows = x_s.shape[0]
    inner, width = out_w.shape[1:]
    parts = [pl.ds(pl.multiple_of(start, 16), part) for start in starts]
    half = lax.broadcasted_iota(jnp.int32, (1, 128), 1) < 64
    for t in range(inner // TILE):
        queries = jnp.concatenate([q_s[rows_of, t * TILE : (t + 1) * TILE] for rows_of in parts], axis=0)
        scores = lax.dot_general(queries, k_s[t], (((1,), (1,)), ((), ())), preferred_element_type=F32)
        weights = jnp.exp2(scores * (head_dim ** (-0.5) * LOG2E) + key_bias)
        inverse = head_totals(weights, rows, head_dim)
        mixed = jnp.dot(weights.astype(BF16), v_s[t], preferred_element_type=F32)
        for g in range(2):
            scale = jnp.where(half, inverse[2 * g], inverse[2 * g + 1])
            at = t * TILE + g * 128
            att[:, at : at + 128] = (mixed[:, g * 128 : (g + 1) * 128] * scale).astype(BF16)
    for at in range(0, width, TILE):
        acc = jnp.dot(att[...], out_w[slot, :, at : at + TILE], preferred_element_type=F32)
        for n, rows_of in enumerate(parts):
            before = x_s[rows_of, at : at + TILE].astype(F32)
            x_s[rows_of, at : at + TILE] = (before + acc[n * part : (n + 1) * part]).astype(BF16)


def own_kernel(head_dim, stage, own, qkv_w, norm_g, gains, head_ones, k_s, v_s, q_s, xn):
    @pl.when(lax.axis_index("section") == stage)
    def run():
        project_half(own, 0, 0, 0, head_dim, xn, k_s, v_s, q_s, qkv_w, norm_g, gains, head_ones)


def stage_kernel(head_dim, stage, last_stage, layers, own, other, qkv_w, out_w, norm_g, gains, bias, head_ones, k_in, v_in, q_in, *refs):
    outs, (k_s, v_s, q_s, x_s, xn, att) = refs[:-6], refs[-6:]
    half_rows = own.shape[0]
    rows, part = 2 * half_rows, half_rows // 2
    slots = out_w.shape[0]

    @pl.when(lax.axis_index("section") == stage)
    def run():
        count = layers[0]
        core = lax.axis_index("seq") % 2
        x_s[0:half_rows, :] = own[...]
        x_s[half_rows:rows, :] = other[...]

        def one_slot(slot, carry):
            def one_half(n, carry):
                start = pl.multiple_of(n * half_rows, 16)
                project_half(x_s, start, start, slot, head_dim, xn, k_s, v_s, q_s, qkv_w, norm_g, gains, head_ones)
                return carry

            lax.fori_loop(jnp.where(slot == 0, 1, 0), 2, one_half, 0)
            key_bias = row_of(bias, slot, slots * min(stage, 1), slots)
            last = slot == count - 1

            def one_chunk(n, carry):
                if stage == 0:
                    starts = [jnp.where(last, half_rows * k + part * core, half_rows * n + part * k) for k in range(2)]
                else:
                    starts = [half_rows * n + part * k for k in range(2)]
                attend_rows(starts, part, key_bias, slot, head_dim, x_s, att, k_s, v_s, q_s, out_w)
                return carry

            lax.fori_loop(0, jnp.where(last, 1, 2), one_chunk, 0)
            return carry

        lax.fori_loop(0, count, one_slot, 0)
        piece = part // 2

        def some_rows(start, skip, size):
            whole = (skip + size + 15) // 16 * 16
            return x_s[pl.ds(start, whole), :].astype(F32)[skip : skip + size].astype(BF16)

        if last_stage:
            outs[0][...] = x_s[0:part, :]
        elif stage == 0:
            outs[0][...] = some_rows(pl.multiple_of(part * core, 16), 0, piece)
            outs[1][...] = x_s[pl.ds(pl.multiple_of(half_rows + part * core, 16), part), :]
        else:
            outs[0][...] = some_rows(0, 0, piece)
            outs[1][...] = some_rows(piece // 16 * 16, piece % 16, part)


def run_stage(stage, last_stage, layers, own, other, kept, head_dim):
    qkv_w, out_w, norm_g, gains, bias, head_ones = (pltpu.with_memory_space_constraint(array, pltpu.VMEM) for array in kept)
    half_rows, width = own.shape
    rows, inner = 2 * half_rows, out_w.shape[1]
    whole = pl.BlockSpec(memory_space=pltpu.VMEM)
    small = pl.BlockSpec(memory_space=pltpu.SMEM)
    heads = (inner // TILE, TILE // head_dim * rows, TILE)
    made_shapes = [pltpu.VMEM(heads, BF16), pltpu.VMEM(heads, BF16), pltpu.VMEM((rows, inner), BF16)]
    made = pl.pallas_call(
        functools.partial(own_kernel, head_dim, stage),
        out_shape=made_shapes,
        in_specs=[whole] * 5,
        out_specs=[whole] * 3,
        scratch_shapes=[pltpu.VMEM((half_rows, width), BF16)],
        compiler_params=pltpu.CompilerParams(vmem_limit_bytes=8 * 2**20),
        cost_estimate=pl.CostEstimate(flops=6 * half_rows * width * inner, bytes_accessed=0, transcendentals=0),
        name="own_half",
    )(own, qkv_w, norm_g, gains, head_ones)
    made = [pltpu.with_memory_space_constraint(array, pltpu.VMEM) for array in made]
    outs = [half_rows // 2] if last_stage else [half_rows // 4, half_rows // 2]
    results = pl.pallas_call(
        functools.partial(stage_kernel, head_dim, stage, last_stage),
        out_shape=[jax.ShapeDtypeStruct((size, width), BF16) for size in outs] + made_shapes,
        in_specs=[small] + [whole] * 11,
        out_specs=[whole] * (len(outs) + 3),
        scratch_shapes=[
            pltpu.VMEM((rows, width), BF16),
            pltpu.VMEM((half_rows, width), BF16),
            pltpu.VMEM((half_rows, inner), BF16),
        ],
        input_output_aliases={9 + n: len(outs) + n for n in range(3)},
        compiler_params=pltpu.CompilerParams(vmem_limit_bytes=12 * 2**20),
        name="stage",
    )(layers, own, other, qkv_w, out_w, norm_g, gains, bias, head_ones, *made)
    return results[: len(outs)]


def sent(value, seq_count, pairs):
    flat = [(a * seq_count + b, c * seq_count + d) for (a, b), (c, d) in pairs]
    return lax.ppermute(value, ("section", "seq"), flat)


def pair_local(latents, lengths, segment_layers, norm_gain, qkv_weight, qk_gain, out_weight):
    sections = lax.axis_size("section")
    seq_count = lax.axis_size("seq")
    chips = seq_count // 2
    micro_count, tok_rows, width = latents.shape
    section = lax.axis_index("section")
    seq = lax.axis_index("seq")
    core = seq % 2
    micro = seq // 2 // (chips // micro_count)
    seqs = range(seq_count)

    pieces = [lax.dynamic_index_in_dim(latents, micro, 0, False)]
    away = lax.dynamic_index_in_dim(latents, 1 - micro, 0, False)
    for k in range(1, chips):
        pairs = [(((0, 2, 3, 1)[k], s), (0, s ^ (2 * k))) for s in seqs]
        pieces.append(sent(pieces[0] if k < 2 else away, seq_count, pairs))
    qkv_kept, *kept, token = keep_weights(lengths, qkv_weight, norm_gain, qk_gain, seq_count * tok_rows)
    own = join_pieces(token, pieces)
    kept = [qkv_kept, keep_out(own, out_weight), *kept]

    for stage in range(sections):
        last = stage == sections - 1
        other = sent(own, seq_count, [((t, s), (t, s ^ 1)) for t in range(sections) for s in seqs])
        outs = run_stage(stage, last, segment_layers, own, other, kept, qk_gain.shape[1] // 2)
        if not last:
            onward = [((stage, s), (stage + 1, s)) for s in seqs]
            first, middle = (sent(part, seq_count, onward) for part in outs)
            fourth = sent(first, seq_count, [((t, s), (t, s ^ 2)) for t in range(sections) for s in seqs])
            own = join_pieces(token, [first, middle, fourth])
    own = outs[0]

    final = sections - 1
    cols = width // sections
    mine = None
    for t in range(sections):
        pairs = [((final, s), (t, 2 * ((s // 2) ^ (chips // 2 * (s % 2))) + s // 2 // (chips // 2))) for s in seqs]
        here = sent(own[:, t * cols : (t + 1) * cols], seq_count, pairs)
        mine = here if mine is None else jnp.where(section == t, here, mine)
    turned = micro != core
    front = jnp.where(turned, mine[tok_rows:], mine[:tok_rows])
    back = jnp.where(turned, mine[:tok_rows], mine[tok_rows:])
    pairs = [((t, s), (t, s ^ 1)) for t in range(sections) for s in seqs]
    got = sent(jnp.where(core == 0, back, front), seq_count, pairs)
    return jnp.where(core == 0, jnp.stack([front, got]), jnp.stack([got, back]))


def local(latents, lengths, segment_layers, norm_gain, qkv_weight, qk_gain, out_weight):
    args = (latents, lengths, segment_layers, norm_gain, qkv_weight, qk_gain, out_weight)
    pairwise = lax.axis_size("seq") == 8 and latents.shape[0] == 2
    return pair_local(*args) if pairwise else relay_local(*args)


def solution(mesh):
    return jax.shard_map(
        local,
        mesh=mesh,
        in_specs=(
            P(None, "seq", None),
            P(),
            P("section"),
            P("section", None),
            P("section", None, None),
            P("section", None),
            P("section", None, None),
        ),
        out_specs=P(None, "seq", "section"),
        check_vma=False,
    )
```

```python
import functools

import jax
import jax.numpy as jnp
from jax import lax
from jax.experimental import pallas as pl
from jax.experimental.pallas import tpu as pltpu
from jax.sharding import PartitionSpec as P

eps_norm = 1e-06
neg_large = -1e30
F32, BF16 = jnp.float32, jnp.bfloat16
TILE = 256


def shifted(value, axis, steps):
    count = lax.axis_size(axis)
    leading, last = (max(0, -steps), min(count, count - steps))
    return lax.ppermute(value, axis, [(source, source + steps) for source in range(leading, last)])


def rms_scale(values, gain_vec):
    return (
        values * lax.rsqrt(jnp.mean(values * values, axis=-1, keepdims=True) + eps_norm) * gain_vec
    )


def body_layer(current, length, norm_w, qkv_w, qk_w, out_w):
    tok_rows, width = current.shape
    inner = qkv_w.shape[1] // 3
    head_dim = qk_w.shape[0] // 2
    head_count = inner // head_dim
    resid = current.astype(jnp.float32)
    normed = rms_scale(resid, norm_w.astype(jnp.float32)).astype(jnp.bfloat16)
    projected = jnp.dot(normed, qkv_w, preferred_element_type=jnp.float32)
    queries = rms_scale(
        projected[:, :inner].reshape(tok_rows, head_count, head_dim),
        qk_w[:head_dim].astype(jnp.float32),
    ).astype(jnp.bfloat16)
    keys = (
        rms_scale(
            projected[:, inner : 2 * inner].reshape(tok_rows, head_count, head_dim),
            qk_w[head_dim:].astype(jnp.float32),
        )
        .astype(jnp.bfloat16)
        .reshape(tok_rows, inner)
    )
    values = projected[:, 2 * inner :].astype(jnp.bfloat16)
    score_scale = head_dim ** (-0.5)
    run_max = jnp.full((head_count, tok_rows), neg_large, jnp.float32)
    key_block = lax.all_gather(keys, "seq", axis=0, tiled=True)
    value_block = lax.all_gather(values, "seq", axis=0, tiled=True)
    block_rows = key_block.shape[0]
    key_heads = key_block.reshape(block_rows, head_count, head_dim)
    value_heads = value_block.reshape(block_rows, head_count, head_dim)
    scores = (
        jnp.einsum("qhd,khd->hqk", queries, key_heads, preferred_element_type=jnp.float32)
        * score_scale
    )
    positions = jnp.arange(block_rows, dtype=jnp.int32)
    scores = jnp.where((positions < length)[None, None, :], scores, neg_large)
    new_max = jnp.maximum(run_max, jnp.max(scores, axis=-1))
    weights = jnp.exp(scores - new_max[..., None])
    run_total = jnp.sum(weights, axis=-1)
    run_acc = jnp.einsum(
        "hqk,khd->hqd",
        weights.astype(jnp.bfloat16),
        value_heads,
        preferred_element_type=jnp.float32,
    )
    run_max, run_total, run_acc = (new_max, run_total, run_acc)
    attended = (run_acc / run_total[..., None]).astype(jnp.bfloat16)
    update = jnp.einsum(
        "hqd,hde->qe",
        attended,
        out_w.reshape(head_count, head_dim, width),
        preferred_element_type=jnp.float32,
    )
    return (resid + update).astype(jnp.bfloat16)


def relay_local(latents, lengths, segment_layers, norm_gain, qkv_weight, qk_gain, out_weight):
    segment_count = lax.axis_size("section")
    segment_pos = lax.axis_index("section")
    micro_count, tok_rows, width = latents.shape
    slot_count = qkv_weight.shape[0]
    own_layers = segment_layers[0]
    tick_count = micro_count + segment_count - 1

    def slot_layer(slot_index, current, length):
        return body_layer(
            current,
            length,
            lax.dynamic_index_in_dim(norm_gain, slot_index, 0, False),
            lax.dynamic_index_in_dim(qkv_weight, slot_index, 0, False),
            lax.dynamic_index_in_dim(qk_gain, slot_index, 0, False),
            lax.dynamic_index_in_dim(out_weight, slot_index, 0, False),
        )

    def advance(tick_index, loop_state):
        received, finished = loop_state
        micro_index = tick_index - segment_pos
        is_valid = (micro_index >= 0) & (micro_index < micro_count)
        clipped = jnp.clip(micro_index, 0, micro_count - 1)
        entering = lax.dynamic_index_in_dim(latents, clipped, 0, False)
        current = jnp.where(segment_pos == 0, entering, received)
        length = lax.dynamic_index_in_dim(lengths, clipped, 0, False)
        for slot_index in range(slot_count):
            updated = slot_layer(slot_index, current, length)
            current = jnp.where(slot_index < own_layers, updated, current)
        previous = lax.dynamic_index_in_dim(finished, clipped, 0, True)
        keep_it = is_valid & (segment_pos == segment_count - 1)
        finished = lax.dynamic_update_index_in_dim(
            finished, jnp.where(keep_it, current[None], previous), clipped, 0
        )
        received = shifted(current, "section", 1)
        return (received, finished)

    start_state = (
        jnp.zeros((tok_rows, width), jnp.bfloat16),
        jnp.zeros((micro_count, tok_rows, width), jnp.bfloat16),
    )
    final_state = lax.fori_loop(0, tick_count, advance, start_state)
    finished = final_state[1]
    terms = jnp.where(segment_pos == segment_count - 1, finished.astype(jnp.float32), 0.0)
    return lax.psum_scatter(terms.astype(jnp.bfloat16), "section", scatter_dimension=2, tiled=True)


LOG2E = 1.4426950408889634


def row_of(ref, slot, first=0, slots=2):
    row = ref[first : first + 1, :]
    for n in range(1, slots):
        row = jnp.where(slot == n, ref[first + n : first + n + 1, :], row)
    return row


def norm_rows(dst, src, start, gain):
    for row in range(0, dst.shape[0], 16):
        values = src[pl.ds(start + row, 16), :].astype(F32)
        mean = jnp.mean(values * values, axis=-1, keepdims=True)
        dst[row : row + 16, :] = (values * lax.rsqrt(mean + eps_norm) * gain).astype(BF16)


def head_norm(acc, gain, head_ones):
    mean = jnp.dot((acc * acc).astype(BF16), head_ones[...], preferred_element_type=F32)
    return (acc * lax.rsqrt(mean + eps_norm) * gain).astype(BF16)


def spread_heads(dst, tile, block, start, head_dim):
    per_tile = TILE // head_dim
    rows = dst.shape[1] // per_tile
    lane = lax.broadcasted_iota(jnp.int32, (1, TILE), 1) // head_dim
    for h in range(per_tile):
        dst[tile, pl.ds(h * rows + start, block.shape[0]), :] = jnp.where(lane == h, block, jnp.zeros_like(block))


def head_totals(weights, rows, head_dim):
    half = lax.broadcasted_iota(jnp.int32, (1, 128), 1) < 64
    totals = []
    for h in range(TILE // head_dim):
        low, high = h * rows, (h + 1) * rows
        total = None
        for at in range(low // 128 * 128, high, 128):
            piece = weights[:, at : at + 128]
            if at < low:
                piece = jnp.where(half, 0.0, piece)
            elif at + 128 > high:
                piece = jnp.where(half, piece, 0.0)
            total = piece if total is None else total + piece
        totals.append(1.0 / jnp.sum(total, axis=-1, keepdims=True))
    return totals


def keep_kernel(head_dim, lengths, qkv_hbm, norm_gain, qk_gain, qkv_w, norm_g, gains, bias, head_ones, token, sem):
    copy = pltpu.make_async_copy(qkv_hbm, qkv_w, sem)
    copy.start()
    slots = norm_gain.shape[0]
    per_tile = TILE // head_dim
    norm_g[...] = norm_gain[...].astype(F32)
    rows_gain = qk_gain[...].astype(F32)
    both = [jnp.concatenate([rows_gain[:, n * head_dim : (n + 1) * head_dim]] * per_tile, axis=1) for n in range(2)]
    gains[...] = jnp.concatenate(both, axis=0)
    lane_head = lax.broadcasted_iota(jnp.int32, (TILE, TILE), 1) // head_dim
    row_head = lax.broadcasted_iota(jnp.int32, (TILE, TILE), 0) // head_dim
    head_ones[...] = jnp.where(lane_head == row_head, 1.0 / head_dim, 0.0).astype(BF16)
    chips = lax.axis_size("seq") // 2
    seq = lax.axis_index("seq")
    chip, core = seq // 2, seq % 2
    rows = bias.shape[1] // per_tile
    piece = rows // chips // 2
    row = lax.broadcasted_iota(jnp.int32, (1, bias.shape[1]), 1) % rows
    number, half = row // piece % chips, row // (piece * chips)
    owner = half ^ core
    order = row // piece % chips
    micro = chip // (chips // lengths.shape[0])
    later = 2 * (owner ^ micro) + order // 2, owner ^ ((order + order // 2) % 2)
    length = lengths[micro]
    biases = []
    for block, from_core in ((number, owner), later):
        live = piece * (2 * (block ^ chip) + from_core) + row % piece < length
        for slot in range(slots):
            most = jnp.max(jnp.abs(both[0][slot : slot + 1])) * jnp.max(jnp.abs(both[1][slot : slot + 1]))
            biases.append(jnp.where(live, -1.01 * head_dim**0.5 * LOG2E * most, neg_large))
    bias[...] = jnp.concatenate(biases, axis=0)
    token[...] = jnp.zeros_like(token)
    copy.wait()


def keep_out_kernel(after, out_hbm, out_w, sem):
    copy = pltpu.make_async_copy(out_hbm, out_w, sem)
    copy.start()
    copy.wait()


def keep_out(after, out_w):
    far = pl.BlockSpec(memory_space=pltpu.HBM)
    whole = pl.BlockSpec(memory_space=pltpu.VMEM)
    return pl.pallas_call(
        keep_out_kernel,
        out_shape=pltpu.VMEM(out_w.shape, BF16),
        in_specs=[whole, far],
        out_specs=whole,
        scratch_shapes=[pltpu.SemaphoreType.DMA],
        compiler_params=pltpu.CompilerParams(vmem_limit_bytes=28 * 2**20),
        cost_estimate=pl.CostEstimate(flops=0, bytes_accessed=4 * out_w.size, transcendentals=0),
        name="keep_out",
    )(after, out_w)


def keep_weights(lengths, qkv_w, norm_gain, qk_gain, rows):
    far = pl.BlockSpec(memory_space=pltpu.HBM)
    whole = pl.BlockSpec(memory_space=pltpu.VMEM)
    small = pl.BlockSpec(memory_space=pltpu.SMEM)
    head_dim, slots = qk_gain.shape[1] // 2, qk_gain.shape[0]
    return pl.pallas_call(
        functools.partial(keep_kernel, head_dim),
        out_shape=[
            pltpu.VMEM(qkv_w.shape, BF16),
            pltpu.VMEM(norm_gain.shape, F32),
            pltpu.VMEM((2 * slots, TILE), F32),
            pltpu.VMEM((2 * slots, TILE // head_dim * rows), F32),
            pltpu.VMEM((TILE, TILE), BF16),
            pltpu.VMEM((8, 128), F32),
        ],
        in_specs=[small, far, whole, whole],
        out_specs=[whole] * 6,
        scratch_shapes=[pltpu.SemaphoreType.DMA],
        compiler_params=pltpu.CompilerParams(vmem_limit_bytes=40 * 2**20),
        cost_estimate=pl.CostEstimate(flops=0, bytes_accessed=4 * qkv_w.size, transcendentals=0),
        name="keep_weights",
    )(lengths, qkv_w, norm_gain, qk_gain)


def join_kernel(token, *refs):
    pieces, out = refs[:-1], refs[-1]
    out[...] = jnp.concatenate([piece[...].astype(F32) for piece in pieces], axis=0).astype(BF16)


def join_pieces(token, pieces):
    token = pltpu.with_memory_space_constraint(token, pltpu.VMEM)
    whole = pl.BlockSpec(memory_space=pltpu.VMEM)
    return pl.pallas_call(
        join_kernel,
        out_shape=jax.ShapeDtypeStruct((sum(piece.shape[0] for piece in pieces), pieces[0].shape[1]), BF16),
        in_specs=[whole] * (1 + len(pieces)),
        out_specs=whole,
        compiler_params=pltpu.CompilerParams(vmem_limit_bytes=8 * 2**20),
        name="join_pieces",
    )(token, *pieces)


def project_half(src, src_start, start, slot, head_dim, xn, k_s, v_s, q_s, qkv_w, norm_g, gains, head_ones):
    slots, inner = qkv_w.shape[0], qkv_w.shape[2] // 3
    tiles = inner // TILE
    q_gain, k_gain = row_of(gains, slot, 0, slots), row_of(gains, slot, slots, slots)
    norm_rows(xn, src, src_start, row_of(norm_g, slot, 0, slots))

    def keep(kind, t, acc):
        if kind == 0:
            q_s[pl.ds(start, acc.shape[0]), t * TILE : (t + 1) * TILE] = head_norm(acc, q_gain, head_ones)
        elif kind == 1:
            spread_heads(k_s, t, head_norm(acc, k_gain, head_ones), start, head_dim)
        else:
            spread_heads(v_s, t, acc.astype(BF16), start, head_dim)

    waiting = None
    for kind, t in [(kind, t) for kind in (1, 0, 2) for t in range(tiles)]:
        at = kind * inner + t * TILE
        acc = jnp.dot(xn[...], qkv_w[slot, :, at : at + TILE], preferred_element_type=F32)
        if waiting is not None:
            keep(*waiting)
        waiting = (kind, t, acc)
    keep(*waiting)


def attend_rows(starts, part, key_bias, slot, head_dim, x_s, att, k_s, v_s, q_s, out_w):
    rows = x_s.shape[0]
    inner, width = out_w.shape[1:]
    parts = [pl.ds(pl.multiple_of(start, 16), part) for start in starts]
    half = lax.broadcasted_iota(jnp.int32, (1, 128), 1) < 64
    for t in range(inner // TILE):
        queries = jnp.concatenate([q_s[rows_of, t * TILE : (t + 1) * TILE] for rows_of in parts], axis=0)
        scores = lax.dot_general(queries, k_s[t], (((1,), (1,)), ((), ())), preferred_element_type=F32)
        weights = jnp.exp2(scores * (head_dim ** (-0.5) * LOG2E) + key_bias)
        inverse = head_totals(weights, rows, head_dim)
        mixed = jnp.dot(weights.astype(BF16), v_s[t], preferred_element_type=F32)
        for g in range(2):
            scale = jnp.where(half, inverse[2 * g], inverse[2 * g + 1])
            at = t * TILE + g * 128
            att[:, at : at + 128] = (mixed[:, g * 128 : (g + 1) * 128] * scale).astype(BF16)
    for at in range(0, width, TILE):
        acc = jnp.dot(att[...], out_w[slot, :, at : at + TILE], preferred_element_type=F32)
        for n, rows_of in enumerate(parts):
            before = x_s[rows_of, at : at + TILE].astype(F32)
            x_s[rows_of, at : at + TILE] = (before + acc[n * part : (n + 1) * part]).astype(BF16)


def own_kernel(head_dim, stage, own, qkv_w, norm_g, gains, head_ones, k_s, v_s, q_s, xn):
    @pl.when(lax.axis_index("section") == stage)
    def run():
        project_half(own, 0, 0, 0, head_dim, xn, k_s, v_s, q_s, qkv_w, norm_g, gains, head_ones)


def stage_kernel(head_dim, micro_count, stage, last_stage, layers, own, other, qkv_w, out_w, norm_g, gains, bias, head_ones, k_in, v_in, q_in, *refs):
    outs, (k_s, v_s, q_s, x_s, xn, att) = refs[:-6], refs[-6:]
    half_rows = own.shape[0]
    rows, part = 2 * half_rows, half_rows // 2
    slots = out_w.shape[0]

    @pl.when(lax.axis_index("section") == stage)
    def run():
        count = layers[0]
        seq, seq_count = lax.axis_index("seq"), lax.axis_size("seq")
        away = seq % 2 ^ seq // (seq_count // micro_count)
        x_s[0:half_rows, :] = own[...]
        x_s[half_rows:rows, :] = other[...]

        def one_slot(slot, carry):
            def one_half(n, carry):
                start = pl.multiple_of(n * half_rows, 16)
                project_half(x_s, start, start, slot, head_dim, xn, k_s, v_s, q_s, qkv_w, norm_g, gains, head_ones)
                return carry

            lax.fori_loop(jnp.where(slot == 0, 1, 0), 2, one_half, 0)
            key_bias = row_of(bias, slot, slots * min(stage, 1), slots)
            last = slot == count - 1

            def one_chunk(n, carry):
                if stage == 0:
                    starts = [jnp.where(last, half_rows * k + part * away, half_rows * n + part * k) for k in range(2)]
                else:
                    starts = [half_rows * n + part * k for k in range(2)]
                attend_rows(starts, part, key_bias, slot, head_dim, x_s, att, k_s, v_s, q_s, out_w)
                return carry

            lax.fori_loop(0, jnp.where(last, 1, 2), one_chunk, 0)
            return carry

        lax.fori_loop(0, count, one_slot, 0)
        piece = part // 2

        def some_rows(start, skip, size):
            whole = (skip + size + 15) // 16 * 16
            return x_s[pl.ds(start, whole), :].astype(F32)[skip : skip + size].astype(BF16)

        if last_stage:
            outs[0][...] = x_s[0:part, :]
        elif stage == 0:
            outs[0][...] = some_rows(pl.multiple_of(part * away, 16), 0, piece)
            outs[1][...] = x_s[pl.ds(pl.multiple_of(half_rows + part * away, 16), part), :]
        else:
            outs[0][...] = some_rows(0, 0, piece)
            outs[1][...] = some_rows(piece // 16 * 16, piece % 16, part)


def run_stage(stage, last_stage, layers, own, other, kept, head_dim, micro_count):
    qkv_w, out_w, norm_g, gains, bias, head_ones = (pltpu.with_memory_space_constraint(array, pltpu.VMEM) for array in kept)
    half_rows, width = own.shape
    rows, inner = 2 * half_rows, out_w.shape[1]
    whole = pl.BlockSpec(memory_space=pltpu.VMEM)
    small = pl.BlockSpec(memory_space=pltpu.SMEM)
    heads = (inner // TILE, TILE // head_dim * rows, TILE)
    made_shapes = [pltpu.VMEM(heads, BF16), pltpu.VMEM(heads, BF16), pltpu.VMEM((rows, inner), BF16)]
    made = pl.pallas_call(
        functools.partial(own_kernel, head_dim, stage),
        out_shape=made_shapes,
        in_specs=[whole] * 5,
        out_specs=[whole] * 3,
        scratch_shapes=[pltpu.VMEM((half_rows, width), BF16)],
        compiler_params=pltpu.CompilerParams(vmem_limit_bytes=8 * 2**20),
        cost_estimate=pl.CostEstimate(flops=6 * half_rows * width * inner, bytes_accessed=0, transcendentals=0),
        name="own_half",
    )(own, qkv_w, norm_g, gains, head_ones)
    made = [pltpu.with_memory_space_constraint(array, pltpu.VMEM) for array in made]
    outs = [half_rows // 2] if last_stage else [half_rows // 4, half_rows // 2]
    results = pl.pallas_call(
        functools.partial(stage_kernel, head_dim, micro_count, stage, last_stage),
        out_shape=[jax.ShapeDtypeStruct((size, width), BF16) for size in outs] + made_shapes,
        in_specs=[small] + [whole] * 11,
        out_specs=[whole] * (len(outs) + 3),
        scratch_shapes=[
            pltpu.VMEM((rows, width), BF16),
            pltpu.VMEM((half_rows, width), BF16),
            pltpu.VMEM((half_rows, inner), BF16),
        ],
        input_output_aliases={9 + n: len(outs) + n for n in range(3)},
        compiler_params=pltpu.CompilerParams(vmem_limit_bytes=12 * 2**20),
        name="stage",
    )(layers, own, other, qkv_w, out_w, norm_g, gains, bias, head_ones, *made)
    return results[: len(outs)]


def sent(value, seq_count, pairs):
    flat = [(a * seq_count + b, c * seq_count + d) for (a, b), (c, d) in pairs]
    return lax.ppermute(value, ("section", "seq"), flat)


def pair_local(latents, lengths, segment_layers, norm_gain, qkv_weight, qk_gain, out_weight):
    sections = lax.axis_size("section")
    seq_count = lax.axis_size("seq")
    chips = seq_count // 2
    micro_count, tok_rows, width = latents.shape
    section = lax.axis_index("section")
    seq = lax.axis_index("seq")
    core = seq % 2
    micro = seq // 2 // (chips // micro_count)
    seqs = range(seq_count)

    pieces = [lax.dynamic_index_in_dim(latents, micro, 0, False)]
    away = lax.dynamic_index_in_dim(latents, 1 - micro, 0, False)
    for k in range(1, chips):
        pairs = [(((0, 2, 3, 1)[k], s), (0, s ^ (2 * k))) for s in seqs]
        pieces.append(sent(pieces[0] if k < 2 else away, seq_count, pairs))
    qkv_kept, *kept, token = keep_weights(lengths, qkv_weight, norm_gain, qk_gain, seq_count * tok_rows)
    own = join_pieces(token, pieces)
    kept = [qkv_kept, keep_out(own, out_weight), *kept]

    for stage in range(sections):
        last = stage == sections - 1
        other = sent(own, seq_count, [((t, s), (t, s ^ 1)) for t in range(sections) for s in seqs])
        outs = run_stage(stage, last, segment_layers, own, other, kept, qk_gain.shape[1] // 2, micro_count)
        if not last:
            onward = [((stage, s), (stage + 1, s)) for s in seqs]
            around = [((t, s), ((t + 1) % sections, s)) for t in range(sections) for s in seqs]
            first, middle = sent(outs[0], seq_count, around), sent(outs[1], seq_count, onward)
            fourth = sent(first, seq_count, [((t, s), (t, s ^ 2)) for t in range(sections) for s in seqs])
            own = join_pieces(token, [first, middle, fourth])
    own = outs[0]

    final = sections - 1
    cols = width // sections

    def crosses(s):
        return s % 2 != s // (seq_count // micro_count)

    def target(s):
        return 2 * (s // 2 ^ (chips // 2 if crosses(s) else 0)) + s // (seq_count // micro_count)

    crossed = own[:, final * cols :]
    crossing = [s for s in seqs if crosses(s)]
    mine = None
    for t in range(final):
        here = sent(own[:, t * cols : (t + 1) * cols], seq_count, [((final, s), (t, target(s))) for s in seqs])
        mine = here if mine is None else jnp.where(section == t, here, mine)
    crossed = sent(crossed, seq_count, [((final, s), (final, target(s))) for s in crossing])
    stays = jnp.where(core == micro, own[:, final * cols :], crossed)
    mine = jnp.where(section == final, stays, mine)
    turned = micro == 1
    front = jnp.where(turned, mine[tok_rows:], mine[:tok_rows])
    back = jnp.where(turned, mine[:tok_rows], mine[tok_rows:])
    pairs = [((t, s), (t, s ^ 1)) for t in range(sections) for s in seqs]
    got = sent(jnp.where(core == 0, back, front), seq_count, pairs)
    return jnp.where(core == 0, jnp.stack([front, got]), jnp.stack([got, back]))


def local(latents, lengths, segment_layers, norm_gain, qkv_weight, qk_gain, out_weight):
    args = (latents, lengths, segment_layers, norm_gain, qkv_weight, qk_gain, out_weight)
    pairwise = lax.axis_size("seq") == 8 and latents.shape[0] == 2
    return pair_local(*args) if pairwise else relay_local(*args)


def solution(mesh):
    return jax.shard_map(
        local,
        mesh=mesh,
        in_specs=(
            P(None, "seq", None),
            P(),
            P("section"),
            P("section", None),
            P("section", None, None),
            P("section", None),
            P("section", None, None),
        ),
        out_specs=P(None, "seq", "section"),
        check_vma=False,
    )
```

```python
import functools

import jax
import jax.numpy as jnp
from jax import lax
from jax.experimental import pallas as pl
from jax.experimental.pallas import tpu as pltpu
from jax.sharding import PartitionSpec as P

eps_norm = 1e-06
neg_large = -1e30
F32, BF16 = jnp.float32, jnp.bfloat16
TILE = 256


def shifted(value, axis, steps):
    count = lax.axis_size(axis)
    leading, last = (max(0, -steps), min(count, count - steps))
    return lax.ppermute(value, axis, [(source, source + steps) for source in range(leading, last)])


def rms_scale(values, gain_vec):
    return (
        values * lax.rsqrt(jnp.mean(values * values, axis=-1, keepdims=True) + eps_norm) * gain_vec
    )


def body_layer(current, length, norm_w, qkv_w, qk_w, out_w):
    tok_rows, width = current.shape
    inner = qkv_w.shape[1] // 3
    head_dim = qk_w.shape[0] // 2
    head_count = inner // head_dim
    resid = current.astype(jnp.float32)
    normed = rms_scale(resid, norm_w.astype(jnp.float32)).astype(jnp.bfloat16)
    projected = jnp.dot(normed, qkv_w, preferred_element_type=jnp.float32)
    queries = rms_scale(
        projected[:, :inner].reshape(tok_rows, head_count, head_dim),
        qk_w[:head_dim].astype(jnp.float32),
    ).astype(jnp.bfloat16)
    keys = (
        rms_scale(
            projected[:, inner : 2 * inner].reshape(tok_rows, head_count, head_dim),
            qk_w[head_dim:].astype(jnp.float32),
        )
        .astype(jnp.bfloat16)
        .reshape(tok_rows, inner)
    )
    values = projected[:, 2 * inner :].astype(jnp.bfloat16)
    score_scale = head_dim ** (-0.5)
    run_max = jnp.full((head_count, tok_rows), neg_large, jnp.float32)
    key_block = lax.all_gather(keys, "seq", axis=0, tiled=True)
    value_block = lax.all_gather(values, "seq", axis=0, tiled=True)
    block_rows = key_block.shape[0]
    key_heads = key_block.reshape(block_rows, head_count, head_dim)
    value_heads = value_block.reshape(block_rows, head_count, head_dim)
    scores = (
        jnp.einsum("qhd,khd->hqk", queries, key_heads, preferred_element_type=jnp.float32)
        * score_scale
    )
    positions = jnp.arange(block_rows, dtype=jnp.int32)
    scores = jnp.where((positions < length)[None, None, :], scores, neg_large)
    new_max = jnp.maximum(run_max, jnp.max(scores, axis=-1))
    weights = jnp.exp(scores - new_max[..., None])
    run_total = jnp.sum(weights, axis=-1)
    run_acc = jnp.einsum(
        "hqk,khd->hqd",
        weights.astype(jnp.bfloat16),
        value_heads,
        preferred_element_type=jnp.float32,
    )
    run_max, run_total, run_acc = (new_max, run_total, run_acc)
    attended = (run_acc / run_total[..., None]).astype(jnp.bfloat16)
    update = jnp.einsum(
        "hqd,hde->qe",
        attended,
        out_w.reshape(head_count, head_dim, width),
        preferred_element_type=jnp.float32,
    )
    return (resid + update).astype(jnp.bfloat16)


def relay_local(latents, lengths, segment_layers, norm_gain, qkv_weight, qk_gain, out_weight):
    segment_count = lax.axis_size("section")
    segment_pos = lax.axis_index("section")
    micro_count, tok_rows, width = latents.shape
    slot_count = qkv_weight.shape[0]
    own_layers = segment_layers[0]
    tick_count = micro_count + segment_count - 1

    def slot_layer(slot_index, current, length):
        return body_layer(
            current,
            length,
            lax.dynamic_index_in_dim(norm_gain, slot_index, 0, False),
            lax.dynamic_index_in_dim(qkv_weight, slot_index, 0, False),
            lax.dynamic_index_in_dim(qk_gain, slot_index, 0, False),
            lax.dynamic_index_in_dim(out_weight, slot_index, 0, False),
        )

    def advance(tick_index, loop_state):
        received, finished = loop_state
        micro_index = tick_index - segment_pos
        is_valid = (micro_index >= 0) & (micro_index < micro_count)
        clipped = jnp.clip(micro_index, 0, micro_count - 1)
        entering = lax.dynamic_index_in_dim(latents, clipped, 0, False)
        current = jnp.where(segment_pos == 0, entering, received)
        length = lax.dynamic_index_in_dim(lengths, clipped, 0, False)
        for slot_index in range(slot_count):
            updated = slot_layer(slot_index, current, length)
            current = jnp.where(slot_index < own_layers, updated, current)
        previous = lax.dynamic_index_in_dim(finished, clipped, 0, True)
        keep_it = is_valid & (segment_pos == segment_count - 1)
        finished = lax.dynamic_update_index_in_dim(
            finished, jnp.where(keep_it, current[None], previous), clipped, 0
        )
        received = shifted(current, "section", 1)
        return (received, finished)

    start_state = (
        jnp.zeros((tok_rows, width), jnp.bfloat16),
        jnp.zeros((micro_count, tok_rows, width), jnp.bfloat16),
    )
    final_state = lax.fori_loop(0, tick_count, advance, start_state)
    finished = final_state[1]
    terms = jnp.where(segment_pos == segment_count - 1, finished.astype(jnp.float32), 0.0)
    return lax.psum_scatter(terms.astype(jnp.bfloat16), "section", scatter_dimension=2, tiled=True)


LOG2E = 1.4426950408889634


def row_of(ref, slot, first=0, slots=2):
    row = ref[first : first + 1, :]
    for n in range(1, slots):
        row = jnp.where(slot == n, ref[first + n : first + n + 1, :], row)
    return row


def norm_rows(dst, src, start, gain):
    for row in range(0, dst.shape[0], 16):
        values = src[pl.ds(start + row, 16), :].astype(F32)
        mean = jnp.mean(values * values, axis=-1, keepdims=True)
        dst[row : row + 16, :] = (values * lax.rsqrt(mean + eps_norm) * gain).astype(BF16)


def head_norm(acc, gain, head_ones):
    mean = jnp.dot((acc * acc).astype(BF16), head_ones[...], preferred_element_type=F32)
    return (acc * lax.rsqrt(mean + eps_norm) * gain).astype(BF16)


def spread_heads(dst, tile, block, start, head_dim):
    per_tile = TILE // head_dim
    rows = dst.shape[1] // per_tile
    lane = lax.broadcasted_iota(jnp.int32, (1, TILE), 1) // head_dim
    for h in range(per_tile):
        dst[tile, pl.ds(h * rows + start, block.shape[0]), :] = jnp.where(lane == h, block, jnp.zeros_like(block))


def head_totals(weights, rows, head_dim):
    half = lax.broadcasted_iota(jnp.int32, (1, 128), 1) < 64
    totals = []
    for h in range(TILE // head_dim):
        low, high = h * rows, (h + 1) * rows
        total = None
        for at in range(low // 128 * 128, high, 128):
            piece = weights[:, at : at + 128]
            if at < low:
                piece = jnp.where(half, 0.0, piece)
            elif at + 128 > high:
                piece = jnp.where(half, piece, 0.0)
            total = piece if total is None else total + piece
        totals.append(1.0 / jnp.sum(total, axis=-1, keepdims=True))
    return totals


def keep_kernel(head_dim, lengths, layers, qkv_hbm, norm_gain, qk_gain, qkv_w, norm_g, gains, bias, head_ones, token, sem):
    copy = pltpu.make_async_copy(qkv_hbm, qkv_w, sem)
    copy.start()
    slots = norm_gain.shape[0]
    per_tile = TILE // head_dim
    norm_g[...] = norm_gain[...].astype(F32)
    rows_gain = qk_gain[...].astype(F32)
    both = [jnp.concatenate([rows_gain[:, n * head_dim : (n + 1) * head_dim]] * per_tile, axis=1) for n in range(2)]
    gains[...] = jnp.concatenate(both, axis=0)
    lane_head = lax.broadcasted_iota(jnp.int32, (TILE, TILE), 1) // head_dim
    row_head = lax.broadcasted_iota(jnp.int32, (TILE, TILE), 0) // head_dim
    head_ones[...] = jnp.where(lane_head == row_head, 1.0 / head_dim, 0.0).astype(BF16)
    chips = lax.axis_size("seq") // 2
    seq = lax.axis_index("seq")
    chip, core = seq // 2, seq % 2
    rows = bias.shape[1] // per_tile
    piece = rows // chips // 2
    row = lax.broadcasted_iota(jnp.int32, (1, bias.shape[1]), 1) % rows
    number, half = row // piece % chips, row // (piece * chips)
    owner = half ^ core
    order = row // piece % chips
    micro = chip // (chips // lengths.shape[0])
    later = 2 * (owner ^ micro) + order // 2, owner ^ ((order + order // 2) % 2)
    length = lengths[micro]
    biases = []
    for block, from_core in ((number, owner), later):
        live = piece * (2 * (block ^ chip) + from_core) + row % piece < length
        for slot in range(slots):
            most = jnp.max(jnp.abs(both[0][slot : slot + 1])) * jnp.max(jnp.abs(both[1][slot : slot + 1]))
            biases.append(jnp.where(live, -1.01 * head_dim**0.5 * LOG2E * most, neg_large))
    bias[...] = jnp.concatenate(biases, axis=0)
    token[...] = jnp.zeros_like(token)
    copy.wait()


def keep_out_kernel(after, out_hbm, out_w, sem):
    copy = pltpu.make_async_copy(out_hbm, out_w, sem)
    copy.start()
    copy.wait()


def keep_out(after, out_w):
    far = pl.BlockSpec(memory_space=pltpu.HBM)
    whole = pl.BlockSpec(memory_space=pltpu.VMEM)
    return pl.pallas_call(
        keep_out_kernel,
        out_shape=pltpu.VMEM(out_w.shape, BF16),
        in_specs=[whole, far],
        out_specs=whole,
        scratch_shapes=[pltpu.SemaphoreType.DMA],
        compiler_params=pltpu.CompilerParams(vmem_limit_bytes=28 * 2**20),
        cost_estimate=pl.CostEstimate(flops=0, bytes_accessed=4 * out_w.size, transcendentals=0),
        name="keep_out",
    )(after, out_w)


def keep_weights(lengths, layers, qkv_w, norm_gain, qk_gain, rows):
    far = pl.BlockSpec(memory_space=pltpu.HBM)
    whole = pl.BlockSpec(memory_space=pltpu.VMEM)
    small = pl.BlockSpec(memory_space=pltpu.SMEM)
    head_dim, slots = qk_gain.shape[1] // 2, qk_gain.shape[0]
    return pl.pallas_call(
        functools.partial(keep_kernel, head_dim),
        out_shape=[
            pltpu.VMEM(qkv_w.shape, BF16),
            pltpu.VMEM(norm_gain.shape, F32),
            pltpu.VMEM((2 * slots, TILE), F32),
            pltpu.VMEM((2 * slots, TILE // head_dim * rows), F32),
            pltpu.VMEM((TILE, TILE), BF16),
            pltpu.VMEM((8, 128), F32),
        ],
        in_specs=[small, small, far, whole, whole],
        out_specs=[whole] * 6,
        scratch_shapes=[pltpu.SemaphoreType.DMA],
        compiler_params=pltpu.CompilerParams(vmem_limit_bytes=40 * 2**20),
        cost_estimate=pl.CostEstimate(flops=0, bytes_accessed=4 * qkv_w.size, transcendentals=0),
        name="keep_weights",
    )(lengths, layers, qkv_w, norm_gain, qk_gain)


def join_kernel(token, *refs):
    pieces, out = refs[:-1], refs[-1]
    out[...] = jnp.concatenate([piece[...].astype(F32) for piece in pieces], axis=0).astype(BF16)


def join_pieces(token, pieces):
    token = pltpu.with_memory_space_constraint(token, pltpu.VMEM)
    whole = pl.BlockSpec(memory_space=pltpu.VMEM)
    return pl.pallas_call(
        join_kernel,
        out_shape=jax.ShapeDtypeStruct((sum(piece.shape[0] for piece in pieces), pieces[0].shape[1]), BF16),
        in_specs=[whole] * (1 + len(pieces)),
        out_specs=whole,
        compiler_params=pltpu.CompilerParams(vmem_limit_bytes=8 * 2**20),
        name="join_pieces",
    )(token, *pieces)


def project_half(src, src_start, start, slot, head_dim, xn, k_s, v_s, q_s, qkv_w, norm_g, gains, head_ones):
    slots, inner = qkv_w.shape[0], qkv_w.shape[2] // 3
    tiles = inner // TILE
    q_gain, k_gain = row_of(gains, slot, 0, slots), row_of(gains, slot, slots, slots)
    norm_rows(xn, src, src_start, row_of(norm_g, slot, 0, slots))

    def keep(kind, t, acc):
        if kind == 0:
            q_s[pl.ds(start, acc.shape[0]), t * TILE : (t + 1) * TILE] = head_norm(acc, q_gain, head_ones)
        elif kind == 1:
            spread_heads(k_s, t, head_norm(acc, k_gain, head_ones), start, head_dim)
        else:
            spread_heads(v_s, t, acc.astype(BF16), start, head_dim)

    waiting = None
    for kind, t in [(kind, t) for kind in (1, 0, 2) for t in range(tiles)]:
        at = kind * inner + t * TILE
        acc = jnp.dot(xn[...], qkv_w[slot, :, at : at + TILE], preferred_element_type=F32)
        if waiting is not None:
            keep(*waiting)
        waiting = (kind, t, acc)
    keep(*waiting)


def attend_rows(starts, part, key_bias, slot, head_dim, x_s, att, k_s, v_s, q_s, out_w):
    rows = x_s.shape[0]
    inner, width = out_w.shape[1:]
    parts = [pl.ds(pl.multiple_of(start, 16), part) for start in starts]
    half = lax.broadcasted_iota(jnp.int32, (1, 128), 1) < 64
    for t in range(inner // TILE):
        queries = jnp.concatenate([q_s[rows_of, t * TILE : (t + 1) * TILE] for rows_of in parts], axis=0)
        scores = lax.dot_general(queries, k_s[t], (((1,), (1,)), ((), ())), preferred_element_type=F32)
        weights = jnp.exp2(scores * (head_dim ** (-0.5) * LOG2E) + key_bias)
        inverse = head_totals(weights, rows, head_dim)
        mixed = jnp.dot(weights.astype(BF16), v_s[t], preferred_element_type=F32)
        for g in range(2):
            scale = jnp.where(half, inverse[2 * g], inverse[2 * g + 1])
            at = t * TILE + g * 128
            att[:, at : at + 128] = (mixed[:, g * 128 : (g + 1) * 128] * scale).astype(BF16)
    for at in range(0, width, TILE):
        acc = jnp.dot(att[...], out_w[slot, :, at : at + TILE], preferred_element_type=F32)
        for n, rows_of in enumerate(parts):
            before = x_s[rows_of, at : at + TILE].astype(F32)
            x_s[rows_of, at : at + TILE] = (before + acc[n * part : (n + 1) * part]).astype(BF16)


def own_kernel(head_dim, stage, own, qkv_w, norm_g, gains, head_ones, k_s, v_s, q_s, xn):
    @pl.when(lax.axis_index("section") == stage)
    def run():
        project_half(own, 0, 0, 0, head_dim, xn, k_s, v_s, q_s, qkv_w, norm_g, gains, head_ones)


def stage_kernel(head_dim, micro_count, stage, last_stage, layers, own, other, qkv_w, out_w, norm_g, gains, bias, head_ones, k_in, v_in, q_in, *refs):
    outs, (k_s, v_s, q_s, x_s, xn, att) = refs[:-6], refs[-6:]
    half_rows = own.shape[0]
    rows, part = 2 * half_rows, half_rows // 2
    slots = out_w.shape[0]

    @pl.when(lax.axis_index("section") == stage)
    def run():
        count = layers[0]
        seq, seq_count = lax.axis_index("seq"), lax.axis_size("seq")
        away = seq % 2 ^ seq // (seq_count // micro_count)
        x_s[0:half_rows, :] = own[...]
        x_s[half_rows:rows, :] = other[...]

        def one_slot(slot, carry):
            def one_half(n, carry):
                start = pl.multiple_of(n * half_rows, 16)
                project_half(x_s, start, start, slot, head_dim, xn, k_s, v_s, q_s, qkv_w, norm_g, gains, head_ones)
                return carry

            lax.fori_loop(jnp.where(slot == 0, 1, 0), 2, one_half, 0)
            key_bias = row_of(bias, slot, slots * min(stage, 1), slots)
            last = slot == count - 1

            def one_chunk(n, carry):
                if stage == 0:
                    starts = [jnp.where(last, half_rows * k + part * away, half_rows * n + part * k) for k in range(2)]
                else:
                    starts = [half_rows * n + part * k for k in range(2)]
                attend_rows(starts, part, key_bias, slot, head_dim, x_s, att, k_s, v_s, q_s, out_w)
                return carry

            lax.fori_loop(0, jnp.where(last, 1, 2), one_chunk, 0)
            return carry

        lax.fori_loop(0, count, one_slot, 0)
        piece = part // 2

        def some_rows(start, skip, size):
            whole = (skip + size + 15) // 16 * 16
            return x_s[pl.ds(start, whole), :].astype(F32)[skip : skip + size].astype(BF16)

        if last_stage:
            outs[0][...] = x_s[0:part, :]
        elif stage == 0:
            outs[0][...] = some_rows(pl.multiple_of(part * away, 16), 0, piece)
            outs[1][...] = x_s[pl.ds(pl.multiple_of(half_rows + part * away, 16), part), :]
        else:
            outs[0][...] = some_rows(0, 0, piece)
            outs[1][...] = some_rows(piece // 16 * 16, piece % 16, part)


def run_stage(stage, last_stage, layers, own, other, kept, head_dim, micro_count):
    qkv_w, out_w, norm_g, gains, bias, head_ones = (pltpu.with_memory_space_constraint(array, pltpu.VMEM) for array in kept)
    half_rows, width = own.shape
    rows, inner = 2 * half_rows, out_w.shape[1]
    whole = pl.BlockSpec(memory_space=pltpu.VMEM)
    small = pl.BlockSpec(memory_space=pltpu.SMEM)
    heads = (inner // TILE, TILE // head_dim * rows, TILE)
    made_shapes = [pltpu.VMEM(heads, BF16), pltpu.VMEM(heads, BF16), pltpu.VMEM((rows, inner), BF16)]
    made = pl.pallas_call(
        functools.partial(own_kernel, head_dim, stage),
        out_shape=made_shapes,
        in_specs=[whole] * 5,
        out_specs=[whole] * 3,
        scratch_shapes=[pltpu.VMEM((half_rows, width), BF16)],
        compiler_params=pltpu.CompilerParams(vmem_limit_bytes=8 * 2**20),
        cost_estimate=pl.CostEstimate(flops=6 * half_rows * width * inner, bytes_accessed=0, transcendentals=0),
        name="own_half",
    )(own, qkv_w, norm_g, gains, head_ones)
    made = [pltpu.with_memory_space_constraint(array, pltpu.VMEM) for array in made]
    outs = [half_rows // 2] if last_stage else [half_rows // 4, half_rows // 2]
    results = pl.pallas_call(
        functools.partial(stage_kernel, head_dim, micro_count, stage, last_stage),
        out_shape=[jax.ShapeDtypeStruct((size, width), BF16) for size in outs] + made_shapes,
        in_specs=[small] + [whole] * 11,
        out_specs=[whole] * (len(outs) + 3),
        scratch_shapes=[
            pltpu.VMEM((rows, width), BF16),
            pltpu.VMEM((half_rows, width), BF16),
            pltpu.VMEM((half_rows, inner), BF16),
        ],
        input_output_aliases={9 + n: len(outs) + n for n in range(3)},
        compiler_params=pltpu.CompilerParams(vmem_limit_bytes=12 * 2**20),
        name="stage",
    )(layers, own, other, qkv_w, out_w, norm_g, gains, bias, head_ones, *made)
    return results[: len(outs)]


def sent(value, seq_count, pairs):
    flat = [(a * seq_count + b, c * seq_count + d) for (a, b), (c, d) in pairs]
    return lax.ppermute(value, ("section", "seq"), flat)


def pair_local(latents, lengths, segment_layers, norm_gain, qkv_weight, qk_gain, out_weight):
    sections = lax.axis_size("section")
    seq_count = lax.axis_size("seq")
    chips = seq_count // 2
    micro_count, tok_rows, width = latents.shape
    section = lax.axis_index("section")
    seq = lax.axis_index("seq")
    core = seq % 2
    micro = seq // 2 // (chips // micro_count)
    seqs = range(seq_count)

    pieces = [lax.dynamic_index_in_dim(latents, micro, 0, False)]
    away = lax.dynamic_index_in_dim(latents, 1 - micro, 0, False)
    for k in range(1, chips):
        pairs = [(((0, 2, 3, 1)[k], s), (0, s ^ (2 * k))) for s in seqs]
        pieces.append(sent(pieces[0] if k < 2 else away, seq_count, pairs))
    qkv_kept, *kept, token = keep_weights(lengths, segment_layers, qkv_weight, norm_gain, qk_gain, seq_count * tok_rows)
    kept = [qkv_kept, keep_out(token, out_weight), *kept]
    own = join_pieces(token, pieces)

    for stage in range(sections):
        last = stage == sections - 1
        other = sent(own, seq_count, [((t, s), (t, s ^ 1)) for t in range(sections) for s in seqs])
        outs = run_stage(stage, last, segment_layers, own, other, kept, qk_gain.shape[1] // 2, micro_count)
        if not last:
            onward = [((stage, s), (stage + 1, s)) for s in seqs]
            around = [((t, s), ((t + 1) % sections, s)) for t in range(sections) for s in seqs]
            first, middle = sent(outs[0], seq_count, around), sent(outs[1], seq_count, onward)
            fourth = sent(first, seq_count, [((t, s), (t, s ^ 2)) for t in range(sections) for s in seqs])
            own = join_pieces(token, [first, middle, fourth])
    own = outs[0]

    final = sections - 1
    cols = width // sections

    def crosses(s):
        return s % 2 != s // (seq_count // micro_count)

    def target(s):
        return 2 * (s // 2 ^ (chips // 2 if crosses(s) else 0)) + s // (seq_count // micro_count)

    crossed = own[:, final * cols :]
    crossing = [s for s in seqs if crosses(s)]
    mine = None
    for t in range(final):
        here = sent(own[:, t * cols : (t + 1) * cols], seq_count, [((final, s), (t, target(s))) for s in seqs])
        mine = here if mine is None else jnp.where(section == t, here, mine)
    crossed = sent(crossed, seq_count, [((final, s), (final, target(s))) for s in crossing])
    stays = jnp.where(core == micro, own[:, final * cols :], crossed)
    mine = jnp.where(section == final, stays, mine)
    turned = micro == 1
    front = jnp.where(turned, mine[tok_rows:], mine[:tok_rows])
    back = jnp.where(turned, mine[:tok_rows], mine[tok_rows:])
    pairs = [((t, s), (t, s ^ 1)) for t in range(sections) for s in seqs]
    got = sent(jnp.where(core == 0, back, front), seq_count, pairs)
    return jnp.where(core == 0, jnp.stack([front, got]), jnp.stack([got, back]))


def local(latents, lengths, segment_layers, norm_gain, qkv_weight, qk_gain, out_weight):
    args = (latents, lengths, segment_layers, norm_gain, qkv_weight, qk_gain, out_weight)
    pairwise = lax.axis_size("seq") == 8 and latents.shape[0] == 2
    return pair_local(*args) if pairwise else relay_local(*args)


def solution(mesh):
    return jax.shard_map(
        local,
        mesh=mesh,
        in_specs=(
            P(None, "seq", None),
            P(),
            P("section"),
            P("section", None),
            P("section", None, None),
            P("section", None),
            P("section", None, None),
        ),
        out_specs=P(None, "seq", "section"),
        check_vma=False,
    )
```

```python
import functools

import jax
import jax.numpy as jnp
from jax import lax
from jax.experimental import pallas as pl
from jax.experimental.pallas import tpu as pltpu
from jax.sharding import PartitionSpec as P

eps_norm = 1e-06
neg_large = -1e30
F32, BF16 = jnp.float32, jnp.bfloat16
TILE = 256


def shifted(value, axis, steps):
    count = lax.axis_size(axis)
    leading, last = (max(0, -steps), min(count, count - steps))
    return lax.ppermute(value, axis, [(source, source + steps) for source in range(leading, last)])


def rms_scale(values, gain_vec):
    return (
        values * lax.rsqrt(jnp.mean(values * values, axis=-1, keepdims=True) + eps_norm) * gain_vec
    )


def body_layer(current, length, norm_w, qkv_w, qk_w, out_w):
    tok_rows, width = current.shape
    inner = qkv_w.shape[1] // 3
    head_dim = qk_w.shape[0] // 2
    head_count = inner // head_dim
    resid = current.astype(jnp.float32)
    normed = rms_scale(resid, norm_w.astype(jnp.float32)).astype(jnp.bfloat16)
    projected = jnp.dot(normed, qkv_w, preferred_element_type=jnp.float32)
    queries = rms_scale(
        projected[:, :inner].reshape(tok_rows, head_count, head_dim),
        qk_w[:head_dim].astype(jnp.float32),
    ).astype(jnp.bfloat16)
    keys = (
        rms_scale(
            projected[:, inner : 2 * inner].reshape(tok_rows, head_count, head_dim),
            qk_w[head_dim:].astype(jnp.float32),
        )
        .astype(jnp.bfloat16)
        .reshape(tok_rows, inner)
    )
    values = projected[:, 2 * inner :].astype(jnp.bfloat16)
    score_scale = head_dim ** (-0.5)
    run_max = jnp.full((head_count, tok_rows), neg_large, jnp.float32)
    key_block = lax.all_gather(keys, "seq", axis=0, tiled=True)
    value_block = lax.all_gather(values, "seq", axis=0, tiled=True)
    block_rows = key_block.shape[0]
    key_heads = key_block.reshape(block_rows, head_count, head_dim)
    value_heads = value_block.reshape(block_rows, head_count, head_dim)
    scores = (
        jnp.einsum("qhd,khd->hqk", queries, key_heads, preferred_element_type=jnp.float32)
        * score_scale
    )
    positions = jnp.arange(block_rows, dtype=jnp.int32)
    scores = jnp.where((positions < length)[None, None, :], scores, neg_large)
    new_max = jnp.maximum(run_max, jnp.max(scores, axis=-1))
    weights = jnp.exp(scores - new_max[..., None])
    run_total = jnp.sum(weights, axis=-1)
    run_acc = jnp.einsum(
        "hqk,khd->hqd",
        weights.astype(jnp.bfloat16),
        value_heads,
        preferred_element_type=jnp.float32,
    )
    run_max, run_total, run_acc = (new_max, run_total, run_acc)
    attended = (run_acc / run_total[..., None]).astype(jnp.bfloat16)
    update = jnp.einsum(
        "hqd,hde->qe",
        attended,
        out_w.reshape(head_count, head_dim, width),
        preferred_element_type=jnp.float32,
    )
    return (resid + update).astype(jnp.bfloat16)


def relay_local(latents, lengths, segment_layers, norm_gain, qkv_weight, qk_gain, out_weight):
    segment_count = lax.axis_size("section")
    segment_pos = lax.axis_index("section")
    micro_count, tok_rows, width = latents.shape
    slot_count = qkv_weight.shape[0]
    own_layers = segment_layers[0]
    tick_count = micro_count + segment_count - 1

    def slot_layer(slot_index, current, length):
        return body_layer(
            current,
            length,
            lax.dynamic_index_in_dim(norm_gain, slot_index, 0, False),
            lax.dynamic_index_in_dim(qkv_weight, slot_index, 0, False),
            lax.dynamic_index_in_dim(qk_gain, slot_index, 0, False),
            lax.dynamic_index_in_dim(out_weight, slot_index, 0, False),
        )

    def advance(tick_index, loop_state):
        received, finished = loop_state
        micro_index = tick_index - segment_pos
        is_valid = (micro_index >= 0) & (micro_index < micro_count)
        clipped = jnp.clip(micro_index, 0, micro_count - 1)
        entering = lax.dynamic_index_in_dim(latents, clipped, 0, False)
        current = jnp.where(segment_pos == 0, entering, received)
        length = lax.dynamic_index_in_dim(lengths, clipped, 0, False)
        for slot_index in range(slot_count):
            updated = slot_layer(slot_index, current, length)
            current = jnp.where(slot_index < own_layers, updated, current)
        previous = lax.dynamic_index_in_dim(finished, clipped, 0, True)
        keep_it = is_valid & (segment_pos == segment_count - 1)
        finished = lax.dynamic_update_index_in_dim(
            finished, jnp.where(keep_it, current[None], previous), clipped, 0
        )
        received = shifted(current, "section", 1)
        return (received, finished)

    start_state = (
        jnp.zeros((tok_rows, width), jnp.bfloat16),
        jnp.zeros((micro_count, tok_rows, width), jnp.bfloat16),
    )
    final_state = lax.fori_loop(0, tick_count, advance, start_state)
    finished = final_state[1]
    terms = jnp.where(segment_pos == segment_count - 1, finished.astype(jnp.float32), 0.0)
    return lax.psum_scatter(terms.astype(jnp.bfloat16), "section", scatter_dimension=2, tiled=True)


LOG2E = 1.4426950408889634


def row_of(ref, slot, first=0, slots=2):
    row = ref[first : first + 1, :]
    for n in range(1, slots):
        row = jnp.where(slot == n, ref[first + n : first + n + 1, :], row)
    return row


def norm_rows(dst, src, start, gain):
    for row in range(0, dst.shape[0], 16):
        values = src[pl.ds(start + row, 16), :].astype(F32)
        mean = jnp.mean(values * values, axis=-1, keepdims=True)
        dst[row : row + 16, :] = (values * lax.rsqrt(mean + eps_norm) * gain).astype(BF16)


def head_norm(acc, gain, head_ones):
    mean = jnp.dot((acc * acc).astype(BF16), head_ones[...], preferred_element_type=F32)
    return (acc * lax.rsqrt(mean + eps_norm) * gain).astype(BF16)


def spread_heads(dst, tile, block, start, head_dim):
    per_tile = TILE // head_dim
    rows = dst.shape[1] // per_tile
    lane = lax.broadcasted_iota(jnp.int32, (1, TILE), 1) // head_dim
    for h in range(per_tile):
        dst[tile, pl.ds(h * rows + start, block.shape[0]), :] = jnp.where(lane == h, block, jnp.zeros_like(block))


def head_totals(weights, rows, head_dim):
    half = lax.broadcasted_iota(jnp.int32, (1, 128), 1) < 64
    totals = []
    for h in range(TILE // head_dim):
        low, high = h * rows, (h + 1) * rows
        total = None
        for at in range(low // 128 * 128, high, 128):
            piece = weights[:, at : at + 128]
            if at < low:
                piece = jnp.where(half, 0.0, piece)
            elif at + 128 > high:
                piece = jnp.where(half, piece, 0.0)
            total = piece if total is None else total + piece
        totals.append(1.0 / jnp.sum(total, axis=-1, keepdims=True))
    return totals


def keep_kernel(head_dim, lengths, layers, qkv_hbm, norm_gain, qk_gain, qkv_w, norm_g, gains, bias, head_ones, token, sem):
    copy = pltpu.make_async_copy(qkv_hbm, qkv_w, sem)
    copy.start()
    slots = norm_gain.shape[0]
    per_tile = TILE // head_dim
    norm_g[...] = norm_gain[...].astype(F32)
    rows_gain = qk_gain[...].astype(F32)
    both = [jnp.concatenate([rows_gain[:, n * head_dim : (n + 1) * head_dim]] * per_tile, axis=1) for n in range(2)]
    gains[...] = jnp.concatenate(both, axis=0)
    lane_head = lax.broadcasted_iota(jnp.int32, (TILE, TILE), 1) // head_dim
    row_head = lax.broadcasted_iota(jnp.int32, (TILE, TILE), 0) // head_dim
    head_ones[...] = jnp.where(lane_head == row_head, 1.0 / head_dim, 0.0).astype(BF16)
    chips = lax.axis_size("seq") // 2
    seq = lax.axis_index("seq")
    chip, core = seq // 2, seq % 2
    rows = bias.shape[1] // per_tile
    piece = rows // chips // 2
    row = lax.broadcasted_iota(jnp.int32, (1, bias.shape[1]), 1) % rows
    number, half = row // piece % chips, row // (piece * chips)
    owner = half ^ core
    order = row // piece % chips
    micro = chip // (chips // lengths.shape[0])
    later = 2 * (owner ^ micro) + order // 2, owner ^ ((order + order // 2) % 2)
    length = lengths[micro]
    biases = []
    for block, from_core in ((number, owner), later):
        live = piece * (2 * (block ^ chip) + from_core) + row % piece < length
        for slot in range(slots):
            most = jnp.max(jnp.abs(both[0][slot : slot + 1])) * jnp.max(jnp.abs(both[1][slot : slot + 1]))
            biases.append(jnp.where(live, -1.01 * head_dim**0.5 * LOG2E * most, neg_large))
    bias[...] = jnp.concatenate(biases, axis=0)
    token[...] = jnp.zeros_like(token)
    copy.wait()


def keep_out_kernel(after, out_hbm, out_w, sem):
    copy = pltpu.make_async_copy(out_hbm, out_w, sem)
    copy.start()
    copy.wait()


def keep_out(after, out_w):
    far = pl.BlockSpec(memory_space=pltpu.HBM)
    whole = pl.BlockSpec(memory_space=pltpu.VMEM)
    return pl.pallas_call(
        keep_out_kernel,
        out_shape=pltpu.VMEM(out_w.shape, BF16),
        in_specs=[whole, far],
        out_specs=whole,
        scratch_shapes=[pltpu.SemaphoreType.DMA],
        compiler_params=pltpu.CompilerParams(vmem_limit_bytes=28 * 2**20),
        cost_estimate=pl.CostEstimate(flops=0, bytes_accessed=4 * out_w.size, transcendentals=0),
        name="keep_out",
    )(after, out_w)


def keep_weights(lengths, layers, qkv_w, norm_gain, qk_gain, rows):
    far = pl.BlockSpec(memory_space=pltpu.HBM)
    whole = pl.BlockSpec(memory_space=pltpu.VMEM)
    small = pl.BlockSpec(memory_space=pltpu.SMEM)
    head_dim, slots = qk_gain.shape[1] // 2, qk_gain.shape[0]
    return pl.pallas_call(
        functools.partial(keep_kernel, head_dim),
        out_shape=[
            pltpu.VMEM(qkv_w.shape, BF16),
            pltpu.VMEM(norm_gain.shape, F32),
            pltpu.VMEM((2 * slots, TILE), F32),
            pltpu.VMEM((2 * slots, TILE // head_dim * rows), F32),
            pltpu.VMEM((TILE, TILE), BF16),
            pltpu.VMEM((8, 128), F32),
        ],
        in_specs=[small, small, far, whole, whole],
        out_specs=[whole] * 6,
        scratch_shapes=[pltpu.SemaphoreType.DMA],
        compiler_params=pltpu.CompilerParams(vmem_limit_bytes=40 * 2**20),
        cost_estimate=pl.CostEstimate(flops=0, bytes_accessed=4 * qkv_w.size, transcendentals=0),
        name="keep_weights",
    )(lengths, layers, qkv_w, norm_gain, qk_gain)


def join_kernel(token, *refs):
    pieces, out = refs[:-1], refs[-1]
    out[...] = jnp.concatenate([piece[...].astype(F32) for piece in pieces], axis=0).astype(BF16)


def join_pieces(token, pieces):
    token = pltpu.with_memory_space_constraint(token, pltpu.VMEM)
    whole = pl.BlockSpec(memory_space=pltpu.VMEM)
    return pl.pallas_call(
        join_kernel,
        out_shape=jax.ShapeDtypeStruct((sum(piece.shape[0] for piece in pieces), pieces[0].shape[1]), BF16),
        in_specs=[whole] * (1 + len(pieces)),
        out_specs=whole,
        compiler_params=pltpu.CompilerParams(vmem_limit_bytes=8 * 2**20),
        name="join_pieces",
    )(token, *pieces)


def project_half(src, src_start, start, slot, head_dim, xn, k_s, v_s, q_s, qkv_w, norm_g, gains, head_ones):
    slots, inner = qkv_w.shape[0], qkv_w.shape[2] // 3
    tiles = inner // TILE
    q_gain, k_gain = row_of(gains, slot, 0, slots), row_of(gains, slot, slots, slots)
    norm_rows(xn, src, src_start, row_of(norm_g, slot, 0, slots))

    def keep(kind, t, acc):
        if kind == 0:
            q_s[pl.ds(start, acc.shape[0]), t * TILE : (t + 1) * TILE] = head_norm(acc, q_gain, head_ones)
        elif kind == 1:
            spread_heads(k_s, t, head_norm(acc, k_gain, head_ones), start, head_dim)
        else:
            spread_heads(v_s, t, acc.astype(BF16), start, head_dim)

    waiting = None
    for kind, t in [(kind, t) for kind in (1, 0, 2) for t in range(tiles)]:
        at = kind * inner + t * TILE
        acc = jnp.dot(xn[...], qkv_w[slot, :, at : at + TILE], preferred_element_type=F32)
        if waiting is not None:
            keep(*waiting)
        waiting = (kind, t, acc)
    keep(*waiting)


def attend_rows(starts, part, key_bias, slot, head_dim, x_s, att, k_s, v_s, q_s, out_w):
    rows = x_s.shape[0]
    inner, width = out_w.shape[1:]
    parts = [pl.ds(pl.multiple_of(start, 16), part) for start in starts]
    half = lax.broadcasted_iota(jnp.int32, (1, 128), 1) < 64
    for t in range(inner // TILE):
        queries = jnp.concatenate([q_s[rows_of, t * TILE : (t + 1) * TILE] for rows_of in parts], axis=0)
        scores = lax.dot_general(queries, k_s[t], (((1,), (1,)), ((), ())), preferred_element_type=F32)
        weights = jnp.exp2(scores * (head_dim ** (-0.5) * LOG2E) + key_bias)
        inverse = head_totals(weights, rows, head_dim)
        mixed = jnp.dot(weights.astype(BF16), v_s[t], preferred_element_type=F32)
        for g in range(2):
            scale = jnp.where(half, inverse[2 * g], inverse[2 * g + 1])
            at = t * TILE + g * 128
            att[:, at : at + 128] = (mixed[:, g * 128 : (g + 1) * 128] * scale).astype(BF16)
    for at in range(0, width, TILE):
        acc = jnp.dot(att[...], out_w[slot, :, at : at + TILE], preferred_element_type=F32)
        for n, rows_of in enumerate(parts):
            before = x_s[rows_of, at : at + TILE].astype(F32)
            x_s[rows_of, at : at + TILE] = (before + acc[n * part : (n + 1) * part]).astype(BF16)


def own_kernel(head_dim, stage, own, qkv_w, norm_g, gains, head_ones, k_s, v_s, q_s, xn):
    @pl.when(lax.axis_index("section") == stage)
    def run():
        project_half(own, 0, 0, 0, head_dim, xn, k_s, v_s, q_s, qkv_w, norm_g, gains, head_ones)


def stage_kernel(head_dim, micro_count, stage, last_stage, layers, own, other, qkv_w, out_w, norm_g, gains, bias, head_ones, k_in, v_in, q_in, *refs):
    outs, (k_s, v_s, q_s, x_s, xn, att) = refs[:-6], refs[-6:]
    half_rows = own.shape[0]
    rows, part = 2 * half_rows, half_rows // 2
    slots = out_w.shape[0]

    @pl.when(lax.axis_index("section") == stage)
    def run():
        count = layers[0]
        seq, seq_count = lax.axis_index("seq"), lax.axis_size("seq")
        away = seq % 2 ^ seq // (seq_count // micro_count)
        x_s[0:half_rows, :] = own[...]
        x_s[half_rows:rows, :] = other[...]

        def one_slot(slot, carry):
            def one_half(n, carry):
                start = pl.multiple_of(n * half_rows, 16)
                project_half(x_s, start, start, slot, head_dim, xn, k_s, v_s, q_s, qkv_w, norm_g, gains, head_ones)
                return carry

            lax.fori_loop(jnp.where(slot == 0, 1, 0), 2, one_half, 0)
            key_bias = row_of(bias, slot, slots * min(stage, 1), slots)
            last = slot == count - 1

            def one_chunk(n, carry):
                if stage == 0:
                    starts = [jnp.where(last, half_rows * k + part * away, half_rows * n + part * k) for k in range(2)]
                else:
                    starts = [half_rows * n + part * k for k in range(2)]
                attend_rows(starts, part, key_bias, slot, head_dim, x_s, att, k_s, v_s, q_s, out_w)
                return carry

            lax.fori_loop(0, jnp.where(last, 1, 2), one_chunk, 0)
            return carry

        lax.fori_loop(0, count, one_slot, 0)
        piece = part // 2

        def some_rows(start, skip, size):
            whole = (skip + size + 15) // 16 * 16
            return x_s[pl.ds(start, whole), :].astype(F32)[skip : skip + size].astype(BF16)

        if last_stage:
            outs[0][...] = x_s[0:part, :]
        elif stage == 0:
            outs[0][...] = some_rows(pl.multiple_of(part * away, 16), 0, piece)
            outs[1][...] = x_s[pl.ds(pl.multiple_of(half_rows + part * away, 16), part), :]
        else:
            outs[0][...] = some_rows(0, 0, piece)
            outs[1][...] = some_rows(piece // 16 * 16, piece % 16, part)


def run_stage(stage, last_stage, layers, own, other, kept, head_dim, micro_count):
    qkv_w, out_w, norm_g, gains, bias, head_ones = (pltpu.with_memory_space_constraint(array, pltpu.VMEM) for array in kept)
    half_rows, width = own.shape
    rows, inner = 2 * half_rows, out_w.shape[1]
    whole = pl.BlockSpec(memory_space=pltpu.VMEM)
    small = pl.BlockSpec(memory_space=pltpu.SMEM)
    heads = (inner // TILE, TILE // head_dim * rows, TILE)
    made_shapes = [pltpu.VMEM(heads, BF16), pltpu.VMEM(heads, BF16), pltpu.VMEM((rows, inner), BF16)]
    made = pl.pallas_call(
        functools.partial(own_kernel, head_dim, stage),
        out_shape=made_shapes,
        in_specs=[whole] * 5,
        out_specs=[whole] * 3,
        scratch_shapes=[pltpu.VMEM((half_rows, width), BF16)],
        compiler_params=pltpu.CompilerParams(vmem_limit_bytes=8 * 2**20),
        cost_estimate=pl.CostEstimate(flops=6 * half_rows * width * inner, bytes_accessed=0, transcendentals=0),
        name="own_half",
    )(own, qkv_w, norm_g, gains, head_ones)
    made = [pltpu.with_memory_space_constraint(array, pltpu.VMEM) for array in made]
    outs = [half_rows // 2] if last_stage else [half_rows // 4, half_rows // 2]
    results = pl.pallas_call(
        functools.partial(stage_kernel, head_dim, micro_count, stage, last_stage),
        out_shape=[jax.ShapeDtypeStruct((size, width), BF16) for size in outs] + made_shapes,
        in_specs=[small] + [whole] * 11,
        out_specs=[whole] * (len(outs) + 3),
        scratch_shapes=[
            pltpu.VMEM((rows, width), BF16),
            pltpu.VMEM((half_rows, width), BF16),
            pltpu.VMEM((half_rows, inner), BF16),
        ],
        input_output_aliases={9 + n: len(outs) + n for n in range(3)},
        compiler_params=pltpu.CompilerParams(vmem_limit_bytes=12 * 2**20),
        name="stage",
    )(layers, own, other, qkv_w, out_w, norm_g, gains, bias, head_ones, *made)
    return results[: len(outs)]


def sent(value, seq_count, pairs):
    flat = [(a * seq_count + b, c * seq_count + d) for (a, b), (c, d) in pairs]
    return lax.ppermute(value, ("section", "seq"), flat)


def pair_local(latents, lengths, segment_layers, norm_gain, qkv_weight, qk_gain, out_weight):
    sections = lax.axis_size("section")
    seq_count = lax.axis_size("seq")
    chips = seq_count // 2
    micro_count, tok_rows, width = latents.shape
    section = lax.axis_index("section")
    seq = lax.axis_index("seq")
    core = seq % 2
    micro = seq // 2 // (chips // micro_count)
    seqs = range(seq_count)

    pieces = [lax.dynamic_index_in_dim(latents, micro, 0, False)]
    away = lax.dynamic_index_in_dim(latents, 1 - micro, 0, False)
    for k in range(1, chips):
        pairs = [(((0, 2, 3, 1)[k], s), (0, s ^ (2 * k))) for s in seqs]
        pieces.append(sent(pieces[0] if k < 2 else away, seq_count, pairs))
    qkv_kept, *kept, token = keep_weights(lengths, segment_layers, qkv_weight, norm_gain, qk_gain, seq_count * tok_rows)
    kept = [qkv_kept, keep_out(token, out_weight), *kept]
    own = join_pieces(token, pieces)

    for stage in range(sections):
        last = stage == sections - 1
        other = sent(own, seq_count, [((t, s), (t, s ^ 1)) for t in range(sections) for s in seqs])
        outs = run_stage(stage, last, segment_layers, own, other, kept, qk_gain.shape[1] // 2, micro_count)
        if not last:
            onward = [((stage, s), (stage + 1, s)) for s in seqs]
            around = [((t, s), ((t + 1) % sections, s)) for t in range(sections) for s in seqs]
            first, middle = sent(outs[0], seq_count, around), sent(outs[1], seq_count, onward)
            fourth = sent(first, seq_count, [((t, s), (t, s ^ 2)) for t in range(sections) for s in seqs])
            own = join_pieces(token, [first, middle, fourth])
    own = outs[0]

    final = sections - 1
    cols = width // sections

    def crosses(s):
        return s % 2 != s // (seq_count // micro_count)

    def target(s):
        return 2 * (s // 2 ^ (chips // 2 if crosses(s) else 0)) + s // (seq_count // micro_count)

    crossed = own[:, final * cols :]
    crossing = [s for s in seqs if crosses(s)]
    mine = None
    for t in reversed(range(final)):
        here = sent(own[:, t * cols : (t + 1) * cols], seq_count, [((final, s), (t, target(s))) for s in seqs])
        mine = here if mine is None else jnp.where(section == t, here, mine)
    crossed = sent(crossed, seq_count, [((final, s), (final, target(s))) for s in crossing])
    stays = jnp.where(core == micro, own[:, final * cols :], crossed)
    mine = jnp.where(section == final, stays, mine)
    turned = micro == 1
    front = jnp.where(turned, mine[tok_rows:], mine[:tok_rows])
    back = jnp.where(turned, mine[:tok_rows], mine[tok_rows:])
    pairs = [((t, s), (t, s ^ 1)) for t in range(sections) for s in seqs]
    got = sent(jnp.where(core == 0, back, front), seq_count, pairs)
    return jnp.where(core == 0, jnp.stack([front, got]), jnp.stack([got, back]))


def local(latents, lengths, segment_layers, norm_gain, qkv_weight, qk_gain, out_weight):
    args = (latents, lengths, segment_layers, norm_gain, qkv_weight, qk_gain, out_weight)
    pairwise = lax.axis_size("seq") == 8 and latents.shape[0] == 2
    return pair_local(*args) if pairwise else relay_local(*args)


def solution(mesh):
    return jax.shard_map(
        local,
        mesh=mesh,
        in_specs=(
            P(None, "seq", None),
            P(),
            P("section"),
            P("section", None),
            P("section", None, None),
            P("section", None),
            P("section", None, None),
        ),
        out_specs=P(None, "seq", "section"),
        check_vma=False,
    )
```
